32 devices in a mesh: dp: 8 (over z, x), ep: 4 (over y, core).
Axes of the slice: x: 2, y: 2, z: 4, core: 2. Of those that a mesh axis runs over, the one named last changes fastest.
Arguments:
- hidden: bfloat16 [2, 512, 3584], P(None, ('dp', 'ep')), may hold values from -6 to 6
- routes: int32 [2, 512, 8], P(None, ('dp', 'ep')), may hold values from 0 to 31, all different within a row; in each aligned block of 16 rows (0 to 15, 16 to 31, ..., all dimensions but the last counted through in order) at most 8 rows name the same one
- route_weights: float32 [2, 512, 8], P(None, ('dp', 'ep')), may hold values from 0.1 to 0.6
- expert_in: bfloat16 [32, 3584, 2048], P(('dp', 'ep')), may hold values from -0.09375 to 0.09375
- expert_out: bfloat16 [32, 1024, 3584], P(('dp', 'ep')), may hold values from -0.1875 to 0.1875
- queries: bfloat16 [512, 64, 576], P(('dp', 'ep')), may hold values from -6 to 6
- fresh_key: bfloat16 [512, 576], P(('dp', 'ep')), may hold values from -4 to 4
- latent_cache: bfloat16 [512, 128, 576], P(('dp', 'ep')), may hold values from -4 to 4
- lengths: int32 [512], replicated, may hold values from 2 to 128, as said below
- swapped: int32 [512], P(('dp', 'ep')), may hold values from 0 to 1, as said below
Outputs:
- mixed: bfloat16 [2, 512, 3584], P(None, ('dp', 'ep'))
- context: bfloat16 [512, 64, 512], P(('dp', 'ep'))
The draws below stay inside these ranges and needn't reach their ends.
Inputs may be any that keep to these rules, and one draw needn't show every extreme that they name: `routes`: in each step the 8 experts of a token differ; the 16 tokens of one device name one expert at most 8 times, a bound that some block reaches. `lengths`: some request holds exactly 128 positions. `swapped`: A marked slot trades with the slot at the same position on the device of the same ep index whose dp index differs by half the dp axis; both devices of such a pair carry the same marks; a device carries at most 4 marks, and some device exactly 4.
All inputs are finite; a program needn't handle non-finite values.
Results may differ from the reference program's by a relative error of at most 0.0058.
Values may be sent and summed in bfloat16 or wider, within the bound.
No kernel may reach another device: no remote copies, remote signals or barrier semaphores. Data moves between devices by JAX's collectives and lax.ppermute only.
A program may use at most 128 MiB of HBM per device.

```python
import math
import jax
import jax.numpy as jnp
import numpy as np
from jax import lax

D = 3584
FF = 1024
HEADS = 64
LATENT = 512
ROPE = 64
TOPK = 8
STEPS = 2
MOVE = 4
TOK_DEV = 16
LMAX = 128
EXPERTS = 32
CAP = 8
TOKENS = 512
N_DP = 8
N_EP = 4


def pair_mask(key):
    base = jax.random.fold_in(key, 101)
    pair_count = TOKENS // (2 * TOK_DEV)
    moving = jax.random.randint(jax.random.fold_in(base, 1), (pair_count,), 1, MOVE + 1)
    moving = moving.at[0].set(MOVE)
    ranking = jax.random.randint(jax.random.fold_in(base, 2), (pair_count, TOK_DEV), 0, 1 << 20) * TOK_DEV + jnp.arange(TOK_DEV, dtype=jnp.int32)[None, :]
    ranked = jnp.argsort(jnp.argsort(ranking, axis=1), axis=1)
    lower = (ranked < moving[:, None]).astype(jnp.int32)
    return jnp.concatenate([lower, lower], axis=0).reshape(-1)


def draw_swapped(key, part):
    return pair_mask(key).astype(jnp.int32)


def draw_lengths(key, part):
    base = jax.random.fold_in(key, 202)
    pair_count = TOKENS // (2 * TOK_DEV)
    side = jax.random.randint(jax.random.fold_in(base, 1), (pair_count,), 0, 2)
    heavy = jnp.concatenate([side, 1 - side])
    longer = jax.random.randint(jax.random.fold_in(base, 2), (2 * pair_count, TOK_DEV), LMAX // 2, LMAX + 1)
    shorter = jax.random.randint(jax.random.fold_in(base, 3), (2 * pair_count, TOK_DEV), 2, LMAX // 2 + 1)
    chosen = jnp.where(heavy[:, None] == 1, longer, shorter).reshape(-1)
    return chosen.at[0].set(LMAX).astype(jnp.int32)


def draw_latent_cache(key, part):
    full_width = LATENT + ROPE
    drawn = jax.random.normal(jax.random.fold_in(key, 405), (TOKENS, LMAX, full_width), jnp.float32)
    return jnp.clip(drawn, -4.0, 4.0).astype(jnp.bfloat16)


def draw_queries(key, part):
    full_width = LATENT + ROPE
    drawn = jax.random.normal(jax.random.fold_in(key, 508), (TOKENS, HEADS, full_width), jnp.float32)
    return jnp.clip(drawn, -4.0, 4.0).astype(jnp.bfloat16)


def block_levels(stream_key, dims, shards, low, largest):
    gain = 1.0
    for position, parts in shards:
        steps = jax.random.uniform(jax.random.fold_in(jax.random.fold_in(stream_key, 6), position), (parts,), jnp.float32, low / len(shards), largest / len(shards))
        gain = gain * jnp.repeat(jnp.exp(steps), dims[position] // parts).reshape((-1,) + (1,) * (len(dims) - 1 - position))
    return gain


def shared_out(stream_key, own, number, rows, count, top, reach, skew):
    sequence = jax.random.permutation(stream_key, count)
    crowded, common = shares(count, rows * top, reach, skew, True), shares(count, rows * top, reach, skew, False)
    places = jnp.arange(count)

    def named(sizes, rotation):
        used = int((sizes > 0).sum())
        fixed = max(1, used // 4)
        shifted = fixed + (places - fixed + rotation * (used - fixed)) % max(1, count - fixed)
        return jnp.zeros((count,), jnp.int32).at[sequence[jnp.where(places < fixed, places, shifted)]].set(jnp.asarray(sizes, jnp.int32))

    sizes = jnp.where(number % 4 == 0, named(crowded, number // 4), named(common, number - number // 4 - 1))
    mixed = jax.random.permutation(jax.random.fold_in(own, 3), count)
    source_of, taker = mixed[0:count // 2 * 2:2], mixed[1:count // 2 * 2:2]
    margin = jnp.minimum(sizes[source_of] - 1, reach - sizes[taker]) // 2
    margin = jnp.where((source_of == sequence[0]) | (taker == sequence[0]) | (sizes[taker] == 0), 0, jnp.maximum(margin, 0))
    shifted = jax.random.randint(jax.random.fold_in(own, 4), (count // 2,), 0, 1 << 20) % (margin + 1)
    sizes = sizes.at[source_of].add(-shifted).at[taker].add(shifted)
    labels = jnp.searchsorted(jnp.cumsum(sizes), jnp.arange(rows * top), side="right").astype(jnp.int32)
    listing = labels.reshape(top, rows).T
    listing = listing[jax.random.permutation(jax.random.fold_in(own, 1), rows)]
    rotation = jax.random.randint(jax.random.fold_in(own, 2), (rows, 1), 0, top)
    return jnp.take_along_axis(listing, (jnp.arange(top)[None, :] + rotation) % top, axis=1)


def shares(count, total, limit, lean, full):
    loads = [(1 << 20) // math.isqrt(standing ** lean) + 1 for standing in range(1, count + 1)]
    largest = limit if full else min(limit, max(-(-total // count), total * loads[0] // sum(loads)))
    least = 1 if total - largest >= count - 1 else 0
    counts, spare = [largest] + [least] * (count - 1), total - largest - least * (count - 1)
    while spare > 0:
        movable = [i for i in range(1, count) if counts[i] < largest] or [i for i in range(1, count) if counts[i] < limit]
        whole, budget = sum([loads[i] for i in movable]), spare
        for i in movable:
            extra = min(limit - counts[i], max(1, budget * loads[i] // whole), spare)
            counts[i] = counts[i] + extra
            spare = spare - extra
    return np.array(counts)


def centred(rng, shape, spread, reach, shards=(), kind=jnp.bfloat16):
    values = spread * jax.random.normal(rng, shape, jnp.float32)
    if shards:
        values = values * block_levels(rng, shape, shards, -0.22, 0.18)
    return jnp.clip(values, -reach, reach).astype(kind)


def setup_inputs(seed: int = 0) -> dict:
    streams_of = jax.random.split(jax.random.key(seed), 11)
    hidden = centred(streams_of[0], (STEPS, TOKENS, D), 1.0, 6.0, ((1, 32),))
    routes_keys = jax.random.split(jax.random.fold_in(streams_of[1], 1), STEPS * TOKENS // TOK_DEV)
    routes_turns = jax.random.permutation(jax.random.fold_in(streams_of[1], 3), STEPS * TOKENS // TOK_DEV)
    routes = jax.vmap(lambda own, number: shared_out(jax.random.fold_in(streams_of[1], 2), own, number, TOK_DEV, N_DP * N_EP, TOPK, CAP, 1))(routes_keys, routes_turns).reshape((STEPS, TOKENS, TOPK))
    route_weights = jnp.clip(0.1 + 0.5 * jax.random.uniform(streams_of[2], (STEPS, TOKENS, TOPK), jnp.float32) ** block_levels(streams_of[2], (STEPS, TOKENS, TOPK), ((1, 32),), -0.2, 0.2), 0.1, 0.6)
    expert_in = centred(streams_of[3], (EXPERTS, D, 2 * FF), D ** -0.5, 0.09375, ((0, 32),))
    expert_out = centred(streams_of[4], (EXPERTS, FF, D), FF ** -0.5, 0.1875, ((0, 32),))
    queries = draw_queries(jax.random.fold_in(streams_of[10], 71), 0)
    fresh_key = centred(streams_of[6], (TOKENS, LATENT + ROPE), 1.0, 4.0, ((0, 32),))
    latent_cache = draw_latent_cache(jax.random.fold_in(streams_of[10], 71), 0)
    lengths = draw_lengths(jax.random.fold_in(streams_of[10], 71), 0)
    swapped = draw_swapped(jax.random.fold_in(streams_of[10], 71), 0)
    return dict(hidden=hidden, routes=routes, route_weights=route_weights, expert_in=expert_in, expert_out=expert_out, queries=queries, fresh_key=fresh_key, latent_cache=latent_cache, lengths=lengths, swapped=swapped)


SOFTMAX_SCALE = 192.0 ** -0.5


def expert_rows(picked, expert_in, expert_out):
    projected = jnp.dot(picked, expert_in, preferred_element_type=jnp.float32)
    half_width = projected.shape[1] // 2
    activated = (jax.nn.silu(projected[:, :half_width]) * projected[:, half_width:]).astype(jnp.bfloat16)
    return jnp.dot(activated, expert_out, preferred_element_type=jnp.float32).astype(jnp.bfloat16)


def routed_step(hidden, routes, route_weights, expert_in, expert_out):
    flat_ids = routes.reshape(-1)
    gate_values = route_weights.reshape(-1)
    capacity = N_DP * N_EP * CAP

    def add_expert(summed, expert):
        matches = flat_ids == expert
        located = jnp.nonzero(matches, size=capacity, fill_value=0)[0].astype(jnp.int32)
        is_valid = jnp.arange(capacity, dtype=jnp.int32) < jnp.sum(matches.astype(jnp.int32))
        token_rows = located // TOPK
        result = expert_rows(hidden[token_rows], expert_in[expert], expert_out[expert]).astype(jnp.float32)
        gate_scale = jnp.where(is_valid, gate_values[located], 0.0)
        return summed.at[token_rows].add(result * gate_scale[:, None]), None

    initial = jnp.zeros((hidden.shape[0], hidden.shape[1]), jnp.float32)
    summed, _ = lax.scan(add_expert, initial, jnp.arange(EXPERTS, dtype=jnp.int32))
    return summed.astype(jnp.bfloat16)


def attend_request(query_rows, cache_rows, length, fresh_row):
    scores = jnp.dot(query_rows, cache_rows.T, preferred_element_type=jnp.float32) * SOFTMAX_SCALE
    own_score = jnp.dot(query_rows, fresh_row, preferred_element_type=jnp.float32) * SOFTMAX_SCALE
    live_mask = jnp.arange(cache_rows.shape[0], dtype=jnp.int32) < length
    scores = jnp.where(live_mask[None, :], scores, -jnp.inf)
    row_top = jnp.maximum(jnp.max(scores, axis=1), own_score)
    weights = jnp.exp(scores - row_top[:, None])
    own_weight = jnp.exp(own_score - row_top)
    summed = jnp.sum(weights, axis=1) + own_weight
    blended = jnp.dot(weights.astype(jnp.bfloat16), cache_rows[:, :LATENT], preferred_element_type=jnp.float32)
    own_rounded = lax.optimization_barrier(own_weight.astype(jnp.bfloat16))
    blended = blended + own_rounded.astype(jnp.float32)[:, None] * fresh_row[None, :LATENT].astype(jnp.float32)
    return (blended / summed[:, None]).astype(jnp.bfloat16)


def reference(hidden, routes, route_weights, expert_in, expert_out, queries, fresh_key, latent_cache, lengths, swapped):
    mixed = jnp.stack([routed_step(hidden[step], routes[step], route_weights[step], expert_in, expert_out) for step in range(STEPS)])
    request_ids = jnp.arange(TOKENS, dtype=jnp.int32)
    anchor = jnp.where(swapped == 1, (request_ids + TOKENS // 2) % TOKENS, request_ids).astype(jnp.int32)

    def single_request(request):
        source = anchor[request]
        return attend_request(queries[request], latent_cache[source], lengths[source], fresh_key[request])

    context = lax.map(single_request, request_ids)
    return mixed, context
```

```python
import functools

import jax
import jax.numpy as jnp
from jax import lax
from jax.experimental import pallas as pl
from jax.experimental.pallas import tpu as pltpu
from jax.sharding import PartitionSpec as P

AXES = ("dp", "ep")
LATENT = 512
STEPS = 2
MOVE = 4
Z_BITS = 2

SOFTMAX_SCALE = 192.0 ** (-0.5)
VMEM_BYTES = 56 * 1024 * 1024


def exchange(value, masks):
    count = lax.axis_size(AXES)
    pairs = [(source, source ^ masks[source % 2]) for source in range(count)]
    return lax.ppermute(value, AXES, pairs)


def swap_halves(index, bits):
    low = index & ((1 << bits) - 1)
    return (low << bits) | (index >> bits)


def ffn_body(line_count, up_steps, down_steps, *refs):
    refs = list(refs)
    core_ref = refs.pop(0)
    del core_ref
    pieces = [refs.pop(0) for _ in range(2 * line_count)]
    gate_own, gate_sib, up_own, up_sib, down_ref, scale_ref = [refs.pop(0) for _ in range(6)]
    theirs = [refs.pop(0) for _ in range(line_count)]
    mine = [refs.pop(0) for _ in range(line_count)]
    rows_ref, act_ref, sems = refs
    step = pl.program_id(0)
    line_rows, half = pieces[0].shape
    block = gate_own.shape[2]
    half_bits = (line_count.bit_length() - 1) // 2

    def copies():
        made = []
        for index in range(line_count):
            made.append(
                pltpu.make_async_copy(
                    pieces[index],
                    rows_ref.at[pl.ds(index * line_rows, line_rows), pl.ds(0, half)],
                    sems.at[index],
                )
            )
            place = swap_halves(index, half_bits)
            made.append(
                pltpu.make_async_copy(
                    pieces[line_count + index],
                    rows_ref.at[pl.ds(place * line_rows, line_rows), pl.ds(half, half)],
                    sems.at[line_count + index],
                )
            )
        return made

    @pl.when(step == 0)
    def _():
        made = copies()
        for copy in made:
            copy.start()
        for copy in made:
            copy.wait()

    @pl.when(step < up_steps)
    def _():
        own = rows_ref[:, :half]
        sib = rows_ref[:, half:]
        gate = jnp.dot(own, gate_own[0], preferred_element_type=jnp.float32)
        gate += jnp.dot(sib, gate_sib[0], preferred_element_type=jnp.float32)
        up = jnp.dot(own, up_own[0], preferred_element_type=jnp.float32)
        up += jnp.dot(sib, up_sib[0], preferred_element_type=jnp.float32)
        value = (gate / (1.0 + jnp.exp(-gate)) * up).astype(jnp.bfloat16)
        act_ref[:, pl.ds(pl.multiple_of(step * block, block), block)] = value

    def down(outs, places):
        answer = jnp.dot(act_ref[...], down_ref[...], preferred_element_type=jnp.float32)
        weighed = answer.astype(jnp.bfloat16).astype(jnp.float32) * scale_ref[...]
        weighed = weighed.astype(jnp.bfloat16)
        for index, out in enumerate(outs):
            place = places(index)
            out[...] = weighed[place * line_rows : (place + 1) * line_rows]

    @pl.when((step >= up_steps) & (step < up_steps + down_steps))
    def _():
        down(theirs, lambda index: swap_halves(index, half_bits))

    @pl.when(step >= up_steps + down_steps)
    def _():
        down(mine, lambda index: index)


def expert_ffn(core, own_pieces, sib_pieces, expert_in, expert_out, scales):
    line_count = len(own_pieces)
    line_rows, half = own_pieces[0].shape
    width = 2 * half
    hidden_units = expert_out.shape[0]
    rows = line_count * line_rows
    block = 256
    up_steps = hidden_units // block
    down_steps = half // block
    halves = expert_in.reshape(2, half, 2 * hidden_units)
    clip = lambda value, low, high: jnp.minimum(jnp.maximum(value, low), high)
    up_at = lambda i: jnp.minimum(i, up_steps - 1)
    they_at = lambda i: clip(i - up_steps, 0, down_steps - 1)
    mine_at = lambda i: clip(i - up_steps - down_steps, 0, down_steps - 1)

    def out_at(i, core_ref):
        is_mine = (i >= up_steps + down_steps).astype(jnp.int32)
        side = jnp.where(is_mine == 1, core_ref[0], 1 - core_ref[0])
        return (0, side * down_steps + jnp.where(is_mine == 1, mine_at(i), they_at(i)))

    line = lambda place: pl.BlockSpec((line_rows, block), lambda i, c: (0, place(i)))
    return pl.pallas_call(
        functools.partial(ffn_body, line_count, up_steps, down_steps),
        grid_spec=pltpu.PrefetchScalarGridSpec(
            num_scalar_prefetch=1,
            grid=(up_steps + 2 * down_steps,),
            in_specs=[pl.BlockSpec(memory_space=pl.ANY)] * (2 * line_count)
            + [
                pl.BlockSpec((1, half, block), lambda i, c: (c[0], 0, up_at(i))),
                pl.BlockSpec((1, half, block), lambda i, c: (1 - c[0], 0, up_at(i))),
                pl.BlockSpec((1, half, block), lambda i, c: (c[0], 0, up_steps + up_at(i))),
                pl.BlockSpec((1, half, block), lambda i, c: (1 - c[0], 0, up_steps + up_at(i))),
                pl.BlockSpec((hidden_units, block), out_at),
                pl.BlockSpec((rows, 1), lambda i, c: (0, 0)),
            ],
            out_specs=[line(they_at)] * line_count + [line(mine_at)] * line_count,
            scratch_shapes=[
                pltpu.VMEM((rows, width), jnp.bfloat16),
                pltpu.VMEM((rows, hidden_units), jnp.bfloat16),
                pltpu.SemaphoreType.DMA((2 * line_count,)),
            ],
        ),
        out_shape=[jax.ShapeDtypeStruct((line_rows, half), jnp.bfloat16)] * (2 * line_count),
        compiler_params=pltpu.CompilerParams(
            dimension_semantics=("arbitrary",), vmem_limit_bytes=VMEM_BYTES
        ),
        cost_estimate=pl.CostEstimate(
            flops=6 * rows * width * hidden_units,
            bytes_accessed=6 * width * hidden_units + 4 * rows * width,
            transcendentals=rows * hidden_units,
        ),
        name="expert_ffn",
    )(
        core.reshape(1),
        *own_pieces,
        *sib_pieces,
        halves,
        halves,
        halves,
        halves,
        expert_out,
        scales,
    )


def pick_body(index_ref, cache_ref, out_ref):
    out_ref[...] = cache_ref[...]


def pick_caches(outgoing, cache):
    count = outgoing.shape[0]
    shape = (1,) + cache.shape[1:]
    return pl.pallas_call(
        pick_body,
        grid_spec=pltpu.PrefetchScalarGridSpec(
            num_scalar_prefetch=1,
            grid=(count,),
            in_specs=[pl.BlockSpec(shape, lambda i, index: (index[i], 0, 0))],
            out_specs=pl.BlockSpec(shape, lambda i, index: (i, 0, 0)),
        ),
        out_shape=jax.ShapeDtypeStruct((count,) + cache.shape[1:], cache.dtype),
        name="pick_caches",
    )(outgoing, cache)


def attend_body(group, moved_ref, arrival_ref, length_ref, query_ref, cache_ref, came_ref, fresh_ref, out_ref):
    first = pl.program_id(0) * group
    for slot in range(group):
        request = first + slot
        query = query_ref[slot]
        cache = jnp.where(moved_ref[request] == 1, came_ref[arrival_ref[request]], cache_ref[slot])
        fresh = fresh_ref[slot].astype(jnp.float32)
        scores = jnp.dot(query, cache, preferred_element_type=jnp.float32) * SOFTMAX_SCALE
        own = jnp.sum(query.astype(jnp.float32) * fresh, axis=1, keepdims=True) * SOFTMAX_SCALE
        positions = lax.broadcasted_iota(jnp.int32, scores.shape, 1)
        scores = jnp.where(positions < length_ref[request], scores, -jnp.inf)
        top = jnp.maximum(jnp.max(scores, axis=1, keepdims=True), own)
        weights = jnp.exp(scores - top)
        own_weight = jnp.exp(own - top)
        summed = jnp.sum(weights, axis=1, keepdims=True) + own_weight
        blended = lax.dot_general(
            weights.astype(jnp.bfloat16),
            cache[:LATENT],
            (((1,), (1,)), ((), ())),
            preferred_element_type=jnp.float32,
        )
        own_rounded = own_weight.astype(jnp.bfloat16).astype(jnp.float32)
        blended = blended + own_rounded * fresh[:, :LATENT]
        out_ref[slot] = (blended / summed).astype(jnp.bfloat16)


def attend(moved, arrival, live, queries, cache, came, fresh):
    count, heads, full = queries.shape
    positions = cache.shape[2]
    group = 4
    return pl.pallas_call(
        functools.partial(attend_body, group),
        grid_spec=pltpu.PrefetchScalarGridSpec(
            num_scalar_prefetch=3,
            grid=(count // group,),
            in_specs=[
                pl.BlockSpec((group, heads, full), lambda i, *_: (i, 0, 0)),
                pl.BlockSpec((group, full, positions), lambda i, *_: (i, 0, 0)),
                pl.BlockSpec(came.shape, lambda i, *_: (0, 0, 0)),
                pl.BlockSpec((group, 1, full), lambda i, *_: (i, 0, 0)),
            ],
            out_specs=pl.BlockSpec((group, heads, LATENT), lambda i, *_: (i, 0, 0)),
        ),
        out_shape=jax.ShapeDtypeStruct((count, heads, LATENT), jnp.bfloat16),
        compiler_params=pltpu.CompilerParams(
            dimension_semantics=("arbitrary",), vmem_limit_bytes=32 * 1024 * 1024
        ),
        cost_estimate=pl.CostEstimate(
            flops=4 * count * heads * full * positions,
            bytes_accessed=2 * count * (heads * (full + LATENT) + full * positions),
            transcendentals=count * heads * positions,
        ),
        name="attend",
    )(moved, arrival, live, queries, cache, came, fresh[:, None, :])


def per_device(
    hidden,
    routes,
    route_weights,
    expert_in,
    expert_out,
    queries,
    fresh_key,
    latent_cache,
    lengths,
    swapped,
):
    dp_count, ep_count = lax.axis_size("dp"), lax.axis_size("ep")
    device_count = dp_count * ep_count
    token_count, width = hidden.shape[1], hidden.shape[2]
    half = width // 2
    me = lax.axis_index(AXES)
    core = me % 2
    dp_bits, ep_bits = dp_count.bit_length() - 1, ep_count.bit_length() - 1
    x_masks = [ep_count << bit for bit in range(dp_bits - Z_BITS)]
    z_unit = ep_count << (dp_bits - Z_BITS)
    y_masks = [1 << bit for bit in range(1, ep_bits)]
    z_masks = [z_unit * step for step in range(1 << Z_BITS)]
    orders = (x_masks + y_masks, y_masks + x_masks)
    level_masks = list(zip(*orders))
    line_count = 1 << len(level_masks)
    sibling = (1, 1)

    meta = jnp.concatenate([routes.astype(jnp.float32), route_weights], axis=2)
    all_meta = lax.all_gather(meta, AXES, axis=0, tiled=False)
    pick_count = routes.shape[2]
    chosen = all_meta[..., :pick_count] == me.astype(jnp.float32)
    gates = jnp.sum(jnp.where(chosen, all_meta[..., pick_count:], 0.0), axis=3)
    line_masks = []
    for order in orders:
        line_masks.append(
            [
                sum(mask for bit, mask in enumerate(order) if index >> bit & 1)
                for index in range(line_count)
            ]
        )
    by_core = jnp.where(
        core == 0, jnp.array(line_masks[0], jnp.int32), jnp.array(line_masks[1], jnp.int32)
    )
    sources = (
        (me - core)
        ^ by_core[:, None, None]
        ^ jnp.array(z_masks, jnp.int32)[None, :, None]
        ^ jnp.arange(2, dtype=jnp.int32)[None, None, :]
    ).reshape(-1)
    scales = jnp.take(gates, sources, axis=0).transpose(1, 0, 2).reshape(STEPS, -1, 1)

    row_count = swapped.shape[0]
    is_moved = swapped == 1
    rank = jnp.cumsum(swapped) - 1
    arrival = jnp.clip(rank, 0, MOVE - 1)
    slots = jnp.arange(row_count, dtype=jnp.int32)
    outgoing = jnp.sum(
        jnp.where(
            is_moved[None, :] & (rank[None, :] == jnp.arange(MOVE, dtype=jnp.int32)[:, None]),
            slots[None, :],
            0,
        ),
        axis=1,
    )
    device_rows = me * row_count + slots
    total_rows = device_count * row_count
    anchor = jnp.where(is_moved, (device_rows + total_rows // 2) % total_rows, device_rows)
    live = lengths[anchor]
    stored = jnp.swapaxes(latent_cache, 1, 2)
    leaving = pick_caches(outgoing, stored)

    own_half = lax.dynamic_slice_in_dim(hidden, core * half, half, axis=2)
    other_half = lax.dynamic_slice_in_dim(hidden, (1 - core) * half, half, axis=2)
    came_half = exchange(other_half, sibling)
    pair = jnp.where(
        core == 0,
        jnp.concatenate([own_half, came_half], axis=1),
        jnp.concatenate([came_half, own_half], axis=1),
    )

    mixed = []
    z_done = None
    for step in range(STEPS):
        block = pair[step]
        if z_done is not None:
            block, z_done = lax.optimization_barrier((block, z_done))
        parts = [block] + [exchange(block, (mask, mask)) for mask in z_masks[1:]]
        z_done = parts[-1]
        pieces = [jnp.concatenate(parts, axis=0)]
        for masks in level_masks:
            pieces = pieces + [exchange(piece, masks) for piece in pieces]
        sib_pieces = [exchange(piece, sibling) for piece in pieces]
        outs = expert_ffn(core, pieces, sib_pieces, expert_in[0], expert_out[0], scales[step])
        theirs, mine = outs[:line_count], outs[line_count:]
        sums = [None] * line_count
        for index in reversed(range(line_count)):
            sums[index] = mine[index].astype(jnp.float32) + exchange(theirs[index], sibling).astype(
                jnp.float32
            )
        for masks in reversed(level_masks):
            kept = len(sums) // 2
            for index in reversed(range(kept)):
                came = exchange(sums[kept + index].astype(jnp.bfloat16), masks)
                sums[index] = sums[index] + came.astype(jnp.float32)
            sums = sums[:kept]
        parts = sums[0].reshape(len(z_masks), 2 * token_count, half)
        total = parts[0]
        for place in range(1, len(z_masks)):
            mask = z_masks[place]
            came = exchange(parts[place].astype(jnp.bfloat16), (mask, mask))
            total = total + came.astype(jnp.float32)
        total = total.astype(jnp.bfloat16).reshape(2, token_count, half)
        kept = lax.dynamic_index_in_dim(total, core, 0, keepdims=False)
        sent = lax.dynamic_index_in_dim(total, 1 - core, 0, keepdims=False)
        came = exchange(sent, sibling)
        mixed.append(
            jnp.where(
                core == 0,
                jnp.concatenate([kept, came], axis=1),
                jnp.concatenate([came, kept], axis=1),
            )
        )

    leaving, z_done = lax.optimization_barrier((leaving, z_done))
    far = device_count // 2
    came_cache = exchange(leaving, (far, far))
    context = attend(
        swapped, arrival, live, queries, stored, came_cache, fresh_key
    )
    return (jnp.stack(mixed), context)


def solution(mesh):
    in_specs = (
        P(None, ("dp", "ep"), None),
        P(None, ("dp", "ep"), None),
        P(None, ("dp", "ep"), None),
        P(("dp", "ep"), None, None),
        P(("dp", "ep"), None, None),
        P(("dp", "ep"), None, None),
        P(("dp", "ep"), None),
        P(("dp", "ep"), None, None),
        P(),
        P(("dp", "ep")),
    )
    out_specs = (P(None, ("dp", "ep"), None), P(("dp", "ep"), None, None))
    return jax.shard_map(
        per_device, mesh=mesh, in_specs=in_specs, out_specs=out_specs, check_vma=False
    )
```

```python
import functools

import jax
import jax.numpy as jnp
from jax import lax
from jax.experimental import pallas as pl
from jax.experimental.pallas import tpu as pltpu
from jax.sharding import PartitionSpec as P

AXES = ("dp", "ep")
LATENT = 512
STEPS = 2
MOVE = 4
LANES = 128
META_PICKS = 8
Z_BITS = 2

SOFTMAX_SCALE = 192.0 ** (-0.5)


def exchange(value, masks):
    count = lax.axis_size(AXES)
    pairs = [(source, source ^ masks[source % 2]) for source in range(count)]
    return lax.ppermute(value, AXES, pairs)


def swap_halves(index, bits):
    low = index & ((1 << bits) - 1)
    return (low << bits) | (index >> bits)


def up_body(line_rows, piece_counts, with_meta, block, spot_ref, *refs):
    refs = list(refs)
    own = [refs.pop(0) for _ in piece_counts]
    sib = [refs.pop(0) for _ in piece_counts]
    weight_ref, act_ref = refs.pop(0), refs.pop(0)
    scale_refs = [refs.pop(0) for _ in range(STEPS if with_meta else 0)]
    own_rows, sib_rows, weights, act, row_sems, weight_sems, act_sems = refs
    line_count = sum(piece_counts)
    half_bits = (line_count.bit_length() - 1) // 2
    half = weight_ref.shape[0] // 2
    hidden_units = weight_ref.shape[1] // 2
    steps = hidden_units // block
    core = spot_ref[0]

    def row_copies(side):
        made = []
        line = 0
        for piece, count in zip(sib if side else own, piece_counts):
            for index in range(count):
                place = swap_halves(line, half_bits) if side else line
                made.append(
                    pltpu.make_async_copy(
                        piece.at[pl.ds(index * line_rows, line_rows)],
                        (sib_rows if side else own_rows).at[pl.ds(place * line_rows, line_rows)],
                        row_sems.at[side, line],
                    )
                )
                line += 1
        return made

    def weight_copies(step, side):
        first = pl.multiple_of((1 - core if side else core) * half, half)
        return [
            pltpu.make_async_copy(
                weight_ref.at[
                    pl.ds(first, half),
                    pl.ds(pl.multiple_of(part * hidden_units + step * block, block), block),
                ],
                weights.at[step % 2, 2 * side + part],
                weight_sems.at[step % 2, 2 * side + part],
            )
            for part in range(2)
        ]

    def act_copy(step):
        columns = pl.ds(pl.multiple_of(step * block, block), block)
        return pltpu.make_async_copy(act.at[:, columns], act_ref.at[:, columns], act_sems.at[step])

    def start(copies):
        for copy in copies:
            copy.start()

    def wait(copies):
        for copy in copies:
            copy.wait()

    for side in range(2):
        start(row_copies(side) + weight_copies(0, side))

    @pl.loop(0, steps)
    def _(step):
        slot = step % 2

        @pl.when(step == 0)
        def _():
            wait(row_copies(0))

        wait(weight_copies(step, 0))

        @pl.when(step + 1 < steps)
        def _():
            start(weight_copies(step + 1, 0) + weight_copies(step + 1, 1))

        own_value = own_rows[:, :half]
        gate = jnp.dot(own_value, weights[slot, 0], preferred_element_type=jnp.float32)
        up = jnp.dot(own_value, weights[slot, 1], preferred_element_type=jnp.float32)

        @pl.when(step == 0)
        def _():
            wait(row_copies(1))

        wait(weight_copies(step, 1))
        sib_value = sib_rows[:, :half]
        gate += jnp.dot(sib_value, weights[slot, 2], preferred_element_type=jnp.float32)
        up += jnp.dot(sib_value, weights[slot, 3], preferred_element_type=jnp.float32)
        value = (gate / (1.0 + jnp.exp(-gate)) * up).astype(jnp.bfloat16)
        act[:, pl.ds(pl.multiple_of(step * block, block), block)] = value
        act_copy(step).start()

    if with_meta:
        meta = own_rows[:, half:].astype(jnp.float32) + sib_rows[:, half:].astype(jnp.float32)
        me = spot_ref[1].astype(jnp.float32)
        lanes = lax.broadcasted_iota(jnp.int32, meta.shape, 1)
        for step, scale_ref in enumerate(scale_refs):
            base = step * 4 * META_PICKS
            value = jnp.zeros_like(meta)
            for part in range(1, 4):
                low = base + part * META_PICKS
                named = pltpu.roll(meta, part * META_PICKS, 1) == me
                inside = (lanes >= low) & (lanes < low + META_PICKS)
                value = value + jnp.where(named & inside, meta, 0.0)
            total = jnp.sum(value, axis=1, keepdims=True)
            scale_ref[...] = jnp.broadcast_to(total, scale_ref.shape)
    for step in range(steps):
        act_copy(step).wait()


def expert_up(spot, own_pieces, sib_pieces, expert_in, line_rows, with_meta):
    piece_counts = [piece.shape[0] // line_rows for piece in own_pieces]
    wide = own_pieces[0].shape[1]
    half = expert_in.shape[0] // 2
    hidden_units = expert_in.shape[1] // 2
    rows = sum(piece_counts) * line_rows
    block = 256
    out_specs = [pl.BlockSpec(memory_space=pl.ANY)]
    out_shape = [jax.ShapeDtypeStruct((rows, hidden_units), jnp.bfloat16)]
    if with_meta:
        out_specs += [pl.BlockSpec((rows, LANES), lambda i, c: (0, 0))] * STEPS
        out_shape += [jax.ShapeDtypeStruct((rows, LANES), jnp.float32)] * STEPS
    held = 2 * rows * (2 * wide + hidden_units) + 16 * half * block
    return pl.pallas_call(
        functools.partial(up_body, line_rows, piece_counts, with_meta, block),
        grid_spec=pltpu.PrefetchScalarGridSpec(
            num_scalar_prefetch=1,
            grid=(1,),
            in_specs=[pl.BlockSpec(memory_space=pl.ANY)] * (2 * len(own_pieces) + 1),
            out_specs=out_specs,
            scratch_shapes=[
                pltpu.VMEM((rows, wide), jnp.bfloat16),
                pltpu.VMEM((rows, wide), jnp.bfloat16),
                pltpu.VMEM((2, 4, half, block), jnp.bfloat16),
                pltpu.VMEM((rows, hidden_units), jnp.bfloat16),
                pltpu.SemaphoreType.DMA((2, sum(piece_counts))),
                pltpu.SemaphoreType.DMA((2, 4)),
                pltpu.SemaphoreType.DMA((hidden_units // block,)),
            ],
        ),
        out_shape=out_shape,
        compiler_params=pltpu.CompilerParams(
            dimension_semantics=("arbitrary",), vmem_limit_bytes=max(50 << 20, held + 24 * rows * block + (4 << 20))
        ),
        cost_estimate=pl.CostEstimate(
            flops=8 * rows * half * hidden_units,
            bytes_accessed=8 * half * hidden_units + 4 * rows * wide + 2 * rows * hidden_units,
            transcendentals=rows * hidden_units,
        ),
        name="expert_up",
    )(spot, *own_pieces, *sib_pieces, expert_in)


def down_body(line_rows, places, spot_ref, act_ref, down_ref, scale_ref, low_ref, high_ref):
    del spot_ref
    answer = jnp.dot(act_ref[...], down_ref[...], preferred_element_type=jnp.float32)
    scale = scale_ref[...]
    half_lines = len(places) // 2
    for column in range(0, answer.shape[1], LANES):
        value = answer[:, column : column + LANES].astype(jnp.bfloat16).astype(jnp.float32)
        value = (value * scale).astype(jnp.bfloat16)
        for index, place in enumerate(places):
            out = low_ref if index < half_lines else high_ref
            at = index % half_lines * line_rows
            out[at : at + line_rows, column : column + LANES] = value[
                place * line_rows : (place + 1) * line_rows
            ]


def expert_down(spot, act, expert_out, scale, line_rows, side):
    rows, hidden_units = act.shape
    half = expert_out.shape[1] // 2
    line_count = rows // line_rows
    half_bits = (line_count.bit_length() - 1) // 2
    places = [swap_halves(index, half_bits) if side else index for index in range(line_count)]
    block = 896
    steps = half // block
    out = pl.BlockSpec((rows // 2, block), lambda i, c: (0, i))
    return pl.pallas_call(
        functools.partial(down_body, line_rows, places),
        grid_spec=pltpu.PrefetchScalarGridSpec(
            num_scalar_prefetch=1,
            grid=(steps,),
            in_specs=[
                pl.BlockSpec((rows, hidden_units), lambda i, c: (0, 0)),
                pl.BlockSpec(
                    (hidden_units, block),
                    lambda i, c: (0, (1 - c[0] if side else c[0]) * steps + i),
                ),
                pl.BlockSpec((rows, LANES), lambda i, c: (0, 0)),
            ],
            out_specs=[out, out],
        ),
        out_shape=[jax.ShapeDtypeStruct((rows // 2, half), jnp.bfloat16)] * 2,
        compiler_params=pltpu.CompilerParams(
            dimension_semantics=("arbitrary",),
            vmem_limit_bytes=4 * (rows + block) * hidden_units + 24 * rows * block + (2 << 20),
        ),
        cost_estimate=pl.CostEstimate(
            flops=2 * rows * half * hidden_units,
            bytes_accessed=2 * half * hidden_units + 2 * rows * (half + hidden_units),
            transcendentals=0,
        ),
        name="expert_down",
    )(spot, act, expert_out, scale)


def meta_body(route_ref, weight_ref, meta_ref):
    token_count, wide = meta_ref.shape
    total = jnp.zeros((token_count, wide), jnp.float32)
    lanes = lax.broadcasted_iota(jnp.int32, (META_PICKS, wide), 1)
    picks = lax.broadcasted_iota(jnp.int32, (META_PICKS, wide), 0)
    for step in range(STEPS):
        weight = weight_ref[step]
        top = weight.astype(jnp.bfloat16)
        rest = weight - top.astype(jnp.float32)
        middle = rest.astype(jnp.bfloat16)
        last = (rest - middle.astype(jnp.float32)).astype(jnp.bfloat16)
        ids = route_ref[step].astype(jnp.float32).astype(jnp.bfloat16)
        for part, value in enumerate((ids, top, middle, last)):
            place = (step * 4 + part) * META_PICKS
            spots = (lanes == picks + place).astype(jnp.bfloat16)
            total += lax.dot_general(
                value, spots, (((0,), (0,)), ((), ())), preferred_element_type=jnp.float32
            )
    meta_ref[...] = total.astype(jnp.bfloat16)


def meta_columns(routes, weights):
    return pl.pallas_call(
        meta_body,
        out_shape=jax.ShapeDtypeStruct((routes.shape[2], LANES), jnp.bfloat16),
        name="meta_columns",
    )(routes, weights)


def pick_body(index_ref, cache_ref, out_ref):
    out_ref[...] = cache_ref[...]


def pick_caches(outgoing, cache):
    count = outgoing.shape[0]
    shape = (1,) + cache.shape[1:]
    return pl.pallas_call(
        pick_body,
        grid_spec=pltpu.PrefetchScalarGridSpec(
            num_scalar_prefetch=1,
            grid=(count,),
            in_specs=[pl.BlockSpec(shape, lambda i, index: (index[i], 0, 0))],
            out_specs=pl.BlockSpec(shape, lambda i, index: (i, 0, 0)),
        ),
        out_shape=jax.ShapeDtypeStruct((count,) + cache.shape[1:], cache.dtype),
        name="pick_caches",
    )(outgoing, cache)


def attend_body(group, moved_ref, arrival_ref, length_ref, query_ref, cache_ref, came_ref, fresh_ref, out_ref):
    first = pl.program_id(0) * group
    for slot in range(group):
        request = first + slot
        query = query_ref[slot]
        cache = jnp.where(moved_ref[request] == 1, came_ref[arrival_ref[request]], cache_ref[slot])
        fresh = fresh_ref[slot].astype(jnp.float32)
        scores = jnp.dot(query, cache, preferred_element_type=jnp.float32) * SOFTMAX_SCALE
        own = jnp.sum(query.astype(jnp.float32) * fresh, axis=1, keepdims=True) * SOFTMAX_SCALE
        positions = lax.broadcasted_iota(jnp.int32, scores.shape, 1)
        scores = jnp.where(positions < length_ref[request], scores, -jnp.inf)
        top = jnp.maximum(jnp.max(scores, axis=1, keepdims=True), own)
        weights = jnp.exp(scores - top)
        own_weight = jnp.exp(own - top)
        summed = jnp.sum(weights, axis=1, keepdims=True) + own_weight
        blended = lax.dot_general(
            weights.astype(jnp.bfloat16),
            cache[:LATENT],
            (((1,), (1,)), ((), ())),
            preferred_element_type=jnp.float32,
        )
        own_rounded = own_weight.astype(jnp.bfloat16).astype(jnp.float32)
        blended = blended + own_rounded * fresh[:, :LATENT]
        out_ref[slot] = (blended / summed).astype(jnp.bfloat16)


def attend(moved, arrival, live, queries, cache, came, fresh):
    count, heads, full = queries.shape
    positions = cache.shape[2]
    group = 4
    return pl.pallas_call(
        functools.partial(attend_body, group),
        grid_spec=pltpu.PrefetchScalarGridSpec(
            num_scalar_prefetch=3,
            grid=(count // group,),
            in_specs=[
                pl.BlockSpec((group, heads, full), lambda i, *_: (i, 0, 0)),
                pl.BlockSpec((group, full, positions), lambda i, *_: (i, 0, 0)),
                pl.BlockSpec(came.shape, lambda i, *_: (0, 0, 0)),
                pl.BlockSpec((group, 1, full), lambda i, *_: (i, 0, 0)),
            ],
            out_specs=pl.BlockSpec((group, heads, LATENT), lambda i, *_: (i, 0, 0)),
        ),
        out_shape=jax.ShapeDtypeStruct((count, heads, LATENT), jnp.bfloat16),
        compiler_params=pltpu.CompilerParams(
            dimension_semantics=("arbitrary",), vmem_limit_bytes=12 << 20
        ),
        cost_estimate=pl.CostEstimate(
            flops=4 * count * heads * full * positions,
            bytes_accessed=2 * count * (heads * (full + LATENT) + full * positions),
            transcendentals=count * heads * positions,
        ),
        name="attend",
    )(moved, arrival, live, queries, cache, came, fresh[:, None, :])


def per_device(
    hidden,
    routes,
    route_weights,
    expert_in,
    expert_out,
    queries,
    fresh_key,
    latent_cache,
    lengths,
    swapped,
):
    dp_count, ep_count = lax.axis_size("dp"), lax.axis_size("ep")
    device_count = dp_count * ep_count
    token_count, width = hidden.shape[1], hidden.shape[2]
    half = width // 2
    me = lax.axis_index(AXES)
    core = me % 2
    dp_bits, ep_bits = dp_count.bit_length() - 1, ep_count.bit_length() - 1
    x_masks = [ep_count << bit for bit in range(dp_bits - Z_BITS)]
    z_unit = ep_count << (dp_bits - Z_BITS)
    y_masks = [1 << bit for bit in range(1, ep_bits)]
    z_masks = [z_unit * step for step in range(1 << Z_BITS)]
    orders = (x_masks + y_masks, y_masks + x_masks)
    level_masks = list(zip(*orders))
    line_count = 1 << len(level_masks)
    sibling = (1, 1)
    spot = jnp.stack([core, me]).astype(jnp.int32)

    meta = meta_columns(jnp.swapaxes(routes, 1, 2), jnp.swapaxes(route_weights, 1, 2))

    own_half = lax.dynamic_slice_in_dim(hidden, core * half, half, axis=2)
    other_half = lax.dynamic_slice_in_dim(hidden, (1 - core) * half, half, axis=2)
    came_half = exchange(other_half, sibling)
    by_core = lambda mine, theirs, axis: jnp.where(
        core == 0,
        jnp.concatenate([mine, theirs], axis=axis),
        jnp.concatenate([theirs, mine], axis=axis),
    )
    pair = by_core(own_half, came_half, 1)
    pair_meta = by_core(meta, jnp.zeros_like(meta), 0)
    line_rows = len(z_masks) * 2 * token_count

    window = lambda *values: lax.optimization_barrier(values)
    far = device_count // 2
    bottom, top_masks = level_masks[:-1], level_masks[-1]

    def send_line(block):
        return [exchange(block, (mask, mask)) for mask in z_masks[1:]]

    def spread(line):
        for masks in bottom:
            line = jnp.concatenate([line, exchange(line, masks)], axis=0)
        return line

    add = lambda terms: functools.reduce(
        lambda total, term: total + term, [term.astype(jnp.float32) for term in terms]
    )
    rounded_sum = lambda terms: add(terms).astype(jnp.bfloat16)
    up = lambda own, sib, with_meta: expert_up(
        spot, own, sib, expert_in[0], line_rows, with_meta
    )
    down = lambda act, scale, side: expert_down(
        spot, act, expert_out[0], scale, line_rows, side
    )
    halves_of = lambda terms: (
        [term[: term.shape[0] // 2] for term in terms],
        [term[term.shape[0] // 2 :] for term in terms],
    )

    def fold(terms):
        for masks in reversed(bottom):
            terms, high = halves_of(terms)
            terms = terms + [exchange(rounded_sum(high), masks)]
        return terms

    def finish_sends(terms):
        block = 2 * token_count
        at = lambda place: [term[place * block : (place + 1) * block] for term in terms]
        return at(0), [rounded_sum(at(place)) for place in range(1, len(z_masks))]

    def finish_line(sends):
        return [exchange(value, (mask, mask)) for value, mask in zip(sends, z_masks[1:])]

    def finish(terms):
        total = rounded_sum(terms).reshape(2, token_count, half)
        kept = lax.dynamic_index_in_dim(total, core, 0, keepdims=False)
        sent = lax.dynamic_index_in_dim(total, 1 - core, 0, keepdims=False)
        return by_core(kept, exchange(sent, sibling), 1)

    block0 = jnp.concatenate([pair[0], pair_meta], axis=1)
    block0, swapped = window(block0, swapped)

    row_count = swapped.shape[0]
    is_moved = swapped == 1
    rank = jnp.cumsum(swapped) - 1
    arrival = jnp.clip(rank, 0, MOVE - 1)
    slots = jnp.arange(row_count, dtype=jnp.int32)
    outgoing = jnp.sum(
        jnp.where(
            is_moved[None, :] & (rank[None, :] == jnp.arange(MOVE, dtype=jnp.int32)[:, None]),
            slots[None, :],
            0,
        ),
        axis=1,
    )
    device_rows = me * row_count + slots
    total_rows = device_count * row_count
    anchor = jnp.where(is_moved, (device_rows + total_rows // 2) % total_rows, device_rows)
    live = lengths[anchor]
    stored = jnp.swapaxes(latent_cache, 1, 2)

    came0 = send_line(block0)
    leaving = pick_caches(outgoing, stored)
    *came0, leaving = window(*came0, leaving)

    low0 = spread(jnp.concatenate([block0] + came0, axis=0))
    low0, block1 = window(low0, pair[1])

    high0 = exchange(low0, top_masks)
    sib_low0 = exchange(low0, sibling)
    came1 = send_line(block1)
    high0, sib_low0, *came1 = window(high0, sib_low0, *came1)

    line1 = jnp.concatenate([block1] + came1, axis=0)
    sib_high0 = exchange(high0, sibling)
    low0, high0, sib_low0, sib_high0, line1, leaving = window(
        low0, high0, sib_low0, sib_high0, line1, leaving
    )

    low1 = spread(line1)
    cache_a = exchange(leaving[: MOVE // 2], (far, far))
    act0, scale0, scale1 = up([low0, high0], [sib_low0, sib_high0], True)
    low1, cache_a, act0, scale0, scale1 = window(low1, cache_a, act0, scale0, scale1)

    part = low1.shape[0] // 2
    high1a = exchange(low1[:part], top_masks)
    sib_low1 = exchange(low1, sibling)
    they_low0, they_high0 = down(act0, scale0, 1)
    low1, high1a, sib_low1, they_low0, they_high0, act0 = window(
        low1, high1a, sib_low1, they_low0, they_high0, act0
    )

    high1b = exchange(low1[part:], top_masks)
    sib_high1a = exchange(high1a, sibling)
    they_low0, they_high0 = exchange(they_low0, sibling), exchange(they_high0, sibling)
    my_low0, my_high0 = down(act0, scale0, 0)
    high1b, sib_high1a, they_low0, they_high0, my_low0, my_high0 = window(
        high1b, sib_high1a, they_low0, they_high0, my_low0, my_high0
    )

    send0 = rounded_sum([my_high0, they_high0])
    sib_high1b = exchange(high1b, sibling)
    send0, sib_high1b, leaving = window(send0, sib_high1b, leaving)

    came = exchange(send0, top_masks)
    cache_b = exchange(leaving[MOVE // 2 :], (far, far))
    (act1,) = up([low1, high1a, high1b], [sib_low1, sib_high1a, sib_high1b], False)
    came, act1, cache_b = window(came, act1, cache_b)

    terms0 = fold([my_low0, they_low0, came])
    they_low1, they_high1 = down(act1, scale1, 1)
    *terms0, they_low1, they_high1 = window(*terms0, they_low1, they_high1)

    kept0, sends0 = finish_sends(terms0)
    *sends0, act1, scale1 = window(*sends0, act1, scale1)
    last0 = finish_line(sends0)
    they_low1, they_high1 = exchange(they_low1, sibling), exchange(they_high1, sibling)
    my_low1, my_high1 = down(act1, scale1, 0)
    they_low1, they_high1, my_low1, my_high1 = window(
        they_low1, they_high1, my_low1, my_high1
    )

    send1 = rounded_sum([my_high1, they_high1])
    send1, queries = window(send1, queries)
    came = exchange(send1, top_masks)
    came_cache = jnp.concatenate([cache_a, cache_b], axis=0)
    context = attend(swapped, arrival, live, queries, stored, came_cache, fresh_key)
    came, context, *last0 = window(came, context, *last0)

    terms1 = fold([my_low1, they_low1, came])
    mixed0 = finish(kept0 + last0)
    kept1, sends1 = finish_sends(terms1)
    mixed1 = finish(kept1 + finish_line(sends1))
    return (jnp.stack([mixed0, mixed1]), context)


def solution(mesh):
    in_specs = (
        P(None, ("dp", "ep"), None),
        P(None, ("dp", "ep"), None),
        P(None, ("dp", "ep"), None),
        P(("dp", "ep"), None, None),
        P(("dp", "ep"), None, None),
        P(("dp", "ep"), None, None),
        P(("dp", "ep"), None),
        P(("dp", "ep"), None, None),
        P(),
        P(("dp", "ep")),
    )
    out_specs = (P(None, ("dp", "ep"), None), P(("dp", "ep"), None, None))
    return jax.shard_map(
        per_device, mesh=mesh, in_specs=in_specs, out_specs=out_specs, check_vma=False
    )
```

```python
import functools

import jax
import jax.numpy as jnp
from jax import lax
from jax.experimental import pallas as pl
from jax.experimental.pallas import tpu as pltpu
from jax.sharding import PartitionSpec as P

AXES = ("dp", "ep")
LATENT = 512
STEPS = 2
MOVE = 4
LANES = 128
META_PICKS = 8
Z_BITS = 2

SOFTMAX_SCALE = 192.0 ** (-0.5)


def exchange(value, masks):
    count = lax.axis_size(AXES)
    pairs = [(source, source ^ masks[source % 2]) for source in range(count)]
    return lax.ppermute(value, AXES, pairs)


def swap_halves(index, bits):
    low = index & ((1 << bits) - 1)
    return (low << bits) | (index >> bits)


def up_body(line_rows, piece_counts, with_meta, block, spot_ref, *refs):
    refs = list(refs)
    own = [refs.pop(0) for _ in piece_counts]
    sib = [refs.pop(0) for _ in piece_counts]
    weight_ref, act_ref = refs.pop(0), refs.pop(0)
    scale_refs = [refs.pop(0) for _ in range(STEPS if with_meta else 0)]
    own_rows, sib_rows, weights, act, row_sems, weight_sems, act_sems = refs
    line_count = sum(piece_counts)
    half_bits = (line_count.bit_length() - 1) // 2
    half = weight_ref.shape[0] // 2
    hidden_units = weight_ref.shape[1] // 2
    steps = hidden_units // block
    core = spot_ref[0]

    def row_copies(side):
        made = []
        line = 0
        for piece, count in zip(sib if side else own, piece_counts):
            for index in range(count):
                place = swap_halves(line, half_bits) if side else line
                made.append(
                    pltpu.make_async_copy(
                        piece.at[pl.ds(index * line_rows, line_rows)],
                        (sib_rows if side else own_rows).at[pl.ds(place * line_rows, line_rows)],
                        row_sems.at[side, line],
                    )
                )
                line += 1
        return made

    def weight_copies(step, side):
        first = pl.multiple_of((1 - core if side else core) * half, half)
        return [
            pltpu.make_async_copy(
                weight_ref.at[
                    pl.ds(first, half),
                    pl.ds(pl.multiple_of(part * hidden_units + step * block, block), block),
                ],
                weights.at[step % 2, 2 * side + part],
                weight_sems.at[step % 2, 2 * side + part],
            )
            for part in range(2)
        ]

    def act_copy(step):
        columns = pl.ds(pl.multiple_of(step * block, block), block)
        return pltpu.make_async_copy(act.at[:, columns], act_ref.at[:, columns], act_sems.at[step])

    def start(copies):
        for copy in copies:
            copy.start()

    def wait(copies):
        for copy in copies:
            copy.wait()

    for side in range(2):
        start(row_copies(side) + weight_copies(0, side))

    @pl.loop(0, steps)
    def _(step):
        slot = step % 2

        @pl.when(step == 0)
        def _():
            wait(row_copies(0))

        wait(weight_copies(step, 0))

        @pl.when(step + 1 < steps)
        def _():
            start(weight_copies(step + 1, 0) + weight_copies(step + 1, 1))

        own_value = own_rows[:, :half]
        gate = jnp.dot(own_value, weights[slot, 0], preferred_element_type=jnp.float32)
        up = jnp.dot(own_value, weights[slot, 1], preferred_element_type=jnp.float32)

        @pl.when(step == 0)
        def _():
            wait(row_copies(1))

        wait(weight_copies(step, 1))
        sib_value = sib_rows[:, :half]
        gate += jnp.dot(sib_value, weights[slot, 2], preferred_element_type=jnp.float32)
        up += jnp.dot(sib_value, weights[slot, 3], preferred_element_type=jnp.float32)
        value = (gate / (1.0 + jnp.exp(-gate)) * up).astype(jnp.bfloat16)
        act[:, pl.ds(pl.multiple_of(step * block, block), block)] = value
        act_copy(step).start()

    if with_meta:
        meta = own_rows[:, half:].astype(jnp.float32) + sib_rows[:, half:].astype(jnp.float32)
        me = spot_ref[1].astype(jnp.float32)
        lanes = lax.broadcasted_iota(jnp.int32, meta.shape, 1)
        for step, scale_ref in enumerate(scale_refs):
            base = step * 4 * META_PICKS
            value = jnp.zeros_like(meta)
            for part in range(1, 4):
                low = base + part * META_PICKS
                named = pltpu.roll(meta, part * META_PICKS, 1) == me
                inside = (lanes >= low) & (lanes < low + META_PICKS)
                value = value + jnp.where(named & inside, meta, 0.0)
            total = jnp.sum(value, axis=1, keepdims=True)
            scale_ref[...] = jnp.broadcast_to(total, scale_ref.shape)
    for step in range(steps):
        act_copy(step).wait()


def expert_up(spot, own_pieces, sib_pieces, expert_in, line_rows, with_meta):
    piece_counts = [piece.shape[0] // line_rows for piece in own_pieces]
    wide = own_pieces[0].shape[1]
    half = expert_in.shape[0] // 2
    hidden_units = expert_in.shape[1] // 2
    rows = sum(piece_counts) * line_rows
    block = 256
    out_specs = [pl.BlockSpec(memory_space=pl.ANY)]
    out_shape = [jax.ShapeDtypeStruct((rows, hidden_units), jnp.bfloat16)]
    if with_meta:
        out_specs += [pl.BlockSpec((rows, LANES), lambda i, c: (0, 0))] * STEPS
        out_shape += [jax.ShapeDtypeStruct((rows, LANES), jnp.float32)] * STEPS
    held = 2 * rows * (2 * wide + hidden_units) + 16 * half * block
    return pl.pallas_call(
        functools.partial(up_body, line_rows, piece_counts, with_meta, block),
        grid_spec=pltpu.PrefetchScalarGridSpec(
            num_scalar_prefetch=1,
            grid=(1,),
            in_specs=[pl.BlockSpec(memory_space=pl.ANY)] * (2 * len(own_pieces) + 1),
            out_specs=out_specs,
            scratch_shapes=[
                pltpu.VMEM((rows, wide), jnp.bfloat16),
                pltpu.VMEM((rows, wide), jnp.bfloat16),
                pltpu.VMEM((2, 4, half, block), jnp.bfloat16),
                pltpu.VMEM((rows, hidden_units), jnp.bfloat16),
                pltpu.SemaphoreType.DMA((2, sum(piece_counts))),
                pltpu.SemaphoreType.DMA((2, 4)),
                pltpu.SemaphoreType.DMA((hidden_units // block,)),
            ],
        ),
        out_shape=out_shape,
        compiler_params=pltpu.CompilerParams(
            dimension_semantics=("arbitrary",), vmem_limit_bytes=max(47 << 20, held + 24 * rows * block + (4 << 20))
        ),
        cost_estimate=pl.CostEstimate(
            flops=8 * rows * half * hidden_units,
            bytes_accessed=8 * half * hidden_units + 4 * rows * wide + 2 * rows * hidden_units,
            transcendentals=rows * hidden_units,
        ),
        name="expert_up",
    )(spot, *own_pieces, *sib_pieces, expert_in)


def down_body(line_rows, places, spot_ref, act_ref, down_ref, scale_ref, low_ref, high_ref):
    del spot_ref
    answer = jnp.dot(act_ref[...], down_ref[...], preferred_element_type=jnp.float32)
    scale = scale_ref[...]
    half_lines = len(places) // 2
    for column in range(0, answer.shape[1], LANES):
        value = answer[:, column : column + LANES].astype(jnp.bfloat16).astype(jnp.float32)
        value = (value * scale).astype(jnp.bfloat16)
        for index, place in enumerate(places):
            out = low_ref if index < half_lines else high_ref
            at = index % half_lines * line_rows
            out[at : at + line_rows, column : column + LANES] = value[
                place * line_rows : (place + 1) * line_rows
            ]


def expert_down(spot, act, expert_out, scale, line_rows, side):
    rows, hidden_units = act.shape
    half = expert_out.shape[1] // 2
    line_count = rows // line_rows
    half_bits = (line_count.bit_length() - 1) // 2
    places = [swap_halves(index, half_bits) if side else index for index in range(line_count)]
    block = 896
    steps = half // block
    out = pl.BlockSpec((rows // 2, block), lambda i, c: (0, i))
    return pl.pallas_call(
        functools.partial(down_body, line_rows, places),
        grid_spec=pltpu.PrefetchScalarGridSpec(
            num_scalar_prefetch=1,
            grid=(steps,),
            in_specs=[
                pl.BlockSpec((rows, hidden_units), lambda i, c: (0, 0)),
                pl.BlockSpec(
                    (hidden_units, block),
                    lambda i, c: (0, (1 - c[0] if side else c[0]) * steps + i),
                ),
                pl.BlockSpec((rows, LANES), lambda i, c: (0, 0)),
            ],
            out_specs=[out, out],
        ),
        out_shape=[jax.ShapeDtypeStruct((rows // 2, half), jnp.bfloat16)] * 2,
        compiler_params=pltpu.CompilerParams(
            dimension_semantics=("arbitrary",),
            vmem_limit_bytes=4 * (rows + block) * hidden_units + 24 * rows * block + (2 << 20),
        ),
        cost_estimate=pl.CostEstimate(
            flops=1 << 36,
            bytes_accessed=1 << 27,
            transcendentals=0,
        ),
        name="expert_down",
    )(spot, act, expert_out, scale)


def meta_body(route_ref, weight_ref, meta_ref):
    token_count, wide = meta_ref.shape
    total = jnp.zeros((token_count, wide), jnp.float32)
    lanes = lax.broadcasted_iota(jnp.int32, (META_PICKS, wide), 1)
    picks = lax.broadcasted_iota(jnp.int32, (META_PICKS, wide), 0)
    for step in range(STEPS):
        weight = weight_ref[step]
        top = weight.astype(jnp.bfloat16)
        rest = weight - top.astype(jnp.float32)
        middle = rest.astype(jnp.bfloat16)
        last = (rest - middle.astype(jnp.float32)).astype(jnp.bfloat16)
        ids = route_ref[step].astype(jnp.float32).astype(jnp.bfloat16)
        for part, value in enumerate((ids, top, middle, last)):
            place = (step * 4 + part) * META_PICKS
            spots = (lanes == picks + place).astype(jnp.bfloat16)
            total += lax.dot_general(
                value, spots, (((0,), (0,)), ((), ())), preferred_element_type=jnp.float32
            )
    meta_ref[...] = total.astype(jnp.bfloat16)


def meta_columns(routes, weights):
    return pl.pallas_call(
        meta_body,
        out_shape=jax.ShapeDtypeStruct((routes.shape[2], LANES), jnp.bfloat16),
        name="meta_columns",
    )(routes, weights)


def pick_body(index_ref, cache_ref, out_ref):
    out_ref[...] = cache_ref[...]


def pick_caches(outgoing, cache):
    count = outgoing.shape[0]
    shape = (1,) + cache.shape[1:]
    return pl.pallas_call(
        pick_body,
        grid_spec=pltpu.PrefetchScalarGridSpec(
            num_scalar_prefetch=1,
            grid=(count,),
            in_specs=[pl.BlockSpec(shape, lambda i, index: (index[i], 0, 0))],
            out_specs=pl.BlockSpec(shape, lambda i, index: (i, 0, 0)),
        ),
        out_shape=jax.ShapeDtypeStruct((count,) + cache.shape[1:], cache.dtype),
        name="pick_caches",
    )(outgoing, cache)


def attend_body(group, moved_ref, arrival_ref, length_ref, query_ref, cache_ref, came_ref, fresh_ref, out_ref):
    first = pl.program_id(0) * group
    for slot in range(group):
        request = first + slot
        query = query_ref[slot]
        cache = jnp.where(moved_ref[request] == 1, came_ref[arrival_ref[request]], cache_ref[slot])
        fresh = fresh_ref[slot].astype(jnp.float32)
        scores = jnp.dot(query, cache, preferred_element_type=jnp.float32) * SOFTMAX_SCALE
        own = jnp.sum(query.astype(jnp.float32) * fresh, axis=1, keepdims=True) * SOFTMAX_SCALE
        positions = lax.broadcasted_iota(jnp.int32, scores.shape, 1)
        scores = jnp.where(positions < length_ref[request], scores, -jnp.inf)
        top = jnp.maximum(jnp.max(scores, axis=1, keepdims=True), own)
        weights = jnp.exp(scores - top)
        own_weight = jnp.exp(own - top)
        summed = jnp.sum(weights, axis=1, keepdims=True) + own_weight
        blended = lax.dot_general(
            weights.astype(jnp.bfloat16),
            cache[:LATENT],
            (((1,), (1,)), ((), ())),
            preferred_element_type=jnp.float32,
        )
        own_rounded = own_weight.astype(jnp.bfloat16).astype(jnp.float32)
        blended = blended + own_rounded * fresh[:, :LATENT]
        out_ref[slot] = (blended / summed).astype(jnp.bfloat16)


def attend(moved, arrival, live, queries, cache, came, fresh):
    count, heads, full = queries.shape
    positions = cache.shape[2]
    group = 4
    return pl.pallas_call(
        functools.partial(attend_body, group),
        grid_spec=pltpu.PrefetchScalarGridSpec(
            num_scalar_prefetch=3,
            grid=(count // group,),
            in_specs=[
                pl.BlockSpec((group, heads, full), lambda i, *_: (i, 0, 0)),
                pl.BlockSpec((group, full, positions), lambda i, *_: (i, 0, 0)),
                pl.BlockSpec(came.shape, lambda i, *_: (0, 0, 0)),
                pl.BlockSpec((group, 1, full), lambda i, *_: (i, 0, 0)),
            ],
            out_specs=pl.BlockSpec((group, heads, LATENT), lambda i, *_: (i, 0, 0)),
        ),
        out_shape=jax.ShapeDtypeStruct((count, heads, LATENT), jnp.bfloat16),
        compiler_params=pltpu.CompilerParams(
            dimension_semantics=("arbitrary",), vmem_limit_bytes=12 << 20
        ),
        cost_estimate=pl.CostEstimate(
            flops=4 * count * heads * full * positions,
            bytes_accessed=2 * count * (heads * (full + LATENT) + full * positions),
            transcendentals=count * heads * positions,
        ),
        name="attend",
    )(moved, arrival, live, queries, cache, came, fresh[:, None, :])


def per_device(
    hidden,
    routes,
    route_weights,
    expert_in,
    expert_out,
    queries,
    fresh_key,
    latent_cache,
    lengths,
    swapped,
):
    dp_count, ep_count = lax.axis_size("dp"), lax.axis_size("ep")
    device_count = dp_count * ep_count
    token_count, width = hidden.shape[1], hidden.shape[2]
    half = width // 2
    me = lax.axis_index(AXES)
    core = me % 2
    dp_bits, ep_bits = dp_count.bit_length() - 1, ep_count.bit_length() - 1
    x_masks = [ep_count << bit for bit in range(dp_bits - Z_BITS)]
    z_unit = ep_count << (dp_bits - Z_BITS)
    y_masks = [1 << bit for bit in range(1, ep_bits)]
    z_masks = [z_unit * step for step in range(1 << Z_BITS)]
    orders = (x_masks + y_masks, y_masks + x_masks)
    level_masks = list(zip(*orders))
    line_count = 1 << len(level_masks)
    sibling = (1, 1)
    spot = jnp.stack([core, me]).astype(jnp.int32)

    meta = meta_columns(jnp.swapaxes(routes, 1, 2), jnp.swapaxes(route_weights, 1, 2))

    own_half = lax.dynamic_slice_in_dim(hidden, core * half, half, axis=2)
    other_half = lax.dynamic_slice_in_dim(hidden, (1 - core) * half, half, axis=2)
    came_half = exchange(other_half, sibling)
    by_core = lambda mine, theirs, axis: jnp.where(
        core == 0,
        jnp.concatenate([mine, theirs], axis=axis),
        jnp.concatenate([theirs, mine], axis=axis),
    )
    pair = by_core(own_half, came_half, 1)
    pair_meta = by_core(meta, jnp.zeros_like(meta), 0)
    line_rows = len(z_masks) * 2 * token_count

    window = lambda *values: lax.optimization_barrier(values)
    far = device_count // 2
    bottom, top_masks = level_masks[:-1], level_masks[-1]

    def send_line(block):
        return [exchange(block, (mask, mask)) for mask in z_masks[1:]]

    def spread(line):
        for masks in bottom:
            line = jnp.concatenate([line, exchange(line, masks)], axis=0)
        return line

    add = lambda terms: functools.reduce(
        lambda total, term: total + term, [term.astype(jnp.float32) for term in terms]
    )
    rounded_sum = lambda terms: add(terms).astype(jnp.bfloat16)
    up = lambda own, sib, with_meta: expert_up(
        spot, own, sib, expert_in[0], line_rows, with_meta
    )
    down = lambda act, scale, side: expert_down(
        spot, act, expert_out[0], scale, line_rows, side
    )
    halves_of = lambda terms: (
        [term[: term.shape[0] // 2] for term in terms],
        [term[term.shape[0] // 2 :] for term in terms],
    )

    def fold(terms):
        for masks in reversed(bottom):
            terms, high = halves_of(terms)
            terms = terms + [exchange(rounded_sum(high), masks)]
        return terms

    def finish_sends(terms):
        block = 2 * token_count
        at = lambda place: [term[place * block : (place + 1) * block] for term in terms]
        return at(0), [rounded_sum(at(place)) for place in range(1, len(z_masks))]

    def finish_line(sends):
        return [exchange(value, (mask, mask)) for value, mask in zip(sends, z_masks[1:])]

    def finish(terms):
        total = rounded_sum(terms).reshape(2, token_count, half)
        kept = lax.dynamic_index_in_dim(total, core, 0, keepdims=False)
        sent = lax.dynamic_index_in_dim(total, 1 - core, 0, keepdims=False)
        return by_core(kept, exchange(sent, sibling), 1)

    block0 = jnp.concatenate([pair[0], pair_meta], axis=1)
    block0, swapped = window(block0, swapped)

    row_count = swapped.shape[0]
    is_moved = swapped == 1
    rank = jnp.cumsum(swapped) - 1
    arrival = jnp.clip(rank, 0, MOVE - 1)
    slots = jnp.arange(row_count, dtype=jnp.int32)
    outgoing = jnp.sum(
        jnp.where(
            is_moved[None, :] & (rank[None, :] == jnp.arange(MOVE, dtype=jnp.int32)[:, None]),
            slots[None, :],
            0,
        ),
        axis=1,
    )
    device_rows = me * row_count + slots
    total_rows = device_count * row_count
    anchor = jnp.where(is_moved, (device_rows + total_rows // 2) % total_rows, device_rows)
    live = lengths[anchor]
    stored = jnp.swapaxes(latent_cache, 1, 2)

    came0 = send_line(block0)
    leaving = pick_caches(outgoing, stored)
    *came0, leaving = window(*came0, leaving)

    low0 = spread(jnp.concatenate([block0] + came0, axis=0))
    low0, block1 = window(low0, pair[1])

    high0 = exchange(low0, top_masks)
    sib_low0 = exchange(low0, sibling)
    came1 = send_line(block1)
    high0, sib_low0, *came1 = window(high0, sib_low0, *came1)

    line1 = jnp.concatenate([block1] + came1, axis=0)
    sib_high0 = exchange(high0, sibling)
    low0, high0, sib_low0, sib_high0, line1, leaving = window(
        low0, high0, sib_low0, sib_high0, line1, leaving
    )

    low1 = spread(line1)
    cache_a = exchange(leaving[: MOVE // 2], (far, far))
    act0, scale0, scale1 = up([low0, high0], [sib_low0, sib_high0], True)
    low1, cache_a, act0, scale0, scale1 = window(low1, cache_a, act0, scale0, scale1)

    part = low1.shape[0] // 2
    high1 = exchange(low1, top_masks)
    they_low0, they_high0 = down(act0, scale0, 1)
    sib_low1 = exchange(low1, sibling)
    they_low0, they_high0 = exchange(they_low0, sibling), exchange(they_high0, sibling)
    my_low0, my_high0 = down(act0, scale0, 0)
    high1, sib_low1, they_low0, they_high0, my_low0, my_high0 = window(
        high1, sib_low1, they_low0, they_high0, my_low0, my_high0
    )

    send0 = rounded_sum([my_high0, they_high0])
    sib_high1 = exchange(high1, sibling)
    send0, sib_high1, leaving = window(send0, sib_high1, leaving)

    came = exchange(send0, top_masks)
    cache_b = exchange(leaving[MOVE // 2 :], (far, far))
    (act1,) = up([low1, high1], [sib_low1, sib_high1], False)
    came, act1, cache_b = window(came, act1, cache_b)

    terms0 = fold([my_low0, they_low0, came])
    they_low1, they_high1 = down(act1, scale1, 1)
    *terms0, they_low1, they_high1 = window(*terms0, they_low1, they_high1)

    kept0, sends0 = finish_sends(terms0)
    *sends0, act1, scale1 = window(*sends0, act1, scale1)
    last0 = finish_line(sends0)
    they_low1, they_high1 = exchange(they_low1, sibling), exchange(they_high1, sibling)
    my_low1, my_high1 = down(act1, scale1, 0)
    they_low1, they_high1, my_low1, my_high1 = window(
        they_low1, they_high1, my_low1, my_high1
    )

    send1 = rounded_sum([my_high1, they_high1])
    send1, queries = window(send1, queries)
    came = exchange(send1, top_masks)
    came_cache = jnp.concatenate([cache_a, cache_b], axis=0)
    context = attend(swapped, arrival, live, queries, stored, came_cache, fresh_key)
    came, context, *last0 = window(came, context, *last0)

    terms1 = fold([my_low1, they_low1, came])
    mixed0 = finish(kept0 + last0)
    kept1, sends1 = finish_sends(terms1)
    mixed1 = finish(kept1 + finish_line(sends1))
    return (jnp.stack([mixed0, mixed1]), context)


def solution(mesh):
    in_specs = (
        P(None, ("dp", "ep"), None),
        P(None, ("dp", "ep"), None),
        P(None, ("dp", "ep"), None),
        P(("dp", "ep"), None, None),
        P(("dp", "ep"), None, None),
        P(("dp", "ep"), None, None),
        P(("dp", "ep"), None),
        P(("dp", "ep"), None, None),
        P(),
        P(("dp", "ep")),
    )
    out_specs = (P(None, ("dp", "ep"), None), P(("dp", "ep"), None, None))
    return jax.shard_map(
        per_device, mesh=mesh, in_specs=in_specs, out_specs=out_specs, check_vma=False
    )
```

```python
import functools

import jax
import jax.numpy as jnp
from jax import lax
from jax.experimental import pallas as pl
from jax.experimental.pallas import tpu as pltpu
from jax.sharding import PartitionSpec as P

AXES = ("dp", "ep")
LATENT = 512
STEPS = 2
MOVE = 4
LANES = 128
META_PICKS = 8
Z_BITS = 2

SOFTMAX_SCALE = 192.0 ** (-0.5)


def exchange(value, masks):
    count = lax.axis_size(AXES)
    pairs = [(source, source ^ masks[source % 2]) for source in range(count)]
    return lax.ppermute(value, AXES, pairs)


def swap_halves(index, bits):
    low = index & ((1 << bits) - 1)
    return (low << bits) | (index >> bits)


def up_body(line_rows, piece_counts, with_meta, block, spot_ref, *refs):
    refs = list(refs)
    own = [refs.pop(0) for _ in piece_counts]
    sib = [refs.pop(0) for _ in piece_counts]
    weight_ref, act_ref = refs.pop(0), refs.pop(0)
    scale_refs = [refs.pop(0) for _ in range(STEPS if with_meta else 0)]
    own_rows, sib_rows, weights, act, row_sems, weight_sems, act_sems = refs
    line_count = sum(piece_counts)
    half_bits = (line_count.bit_length() - 1) // 2
    half = weight_ref.shape[0] // 2
    hidden_units = weight_ref.shape[1] // 2
    steps = hidden_units // block
    core = spot_ref[0]

    def row_copies(side):
        made = []
        line = 0
        for piece, count in zip(sib if side else own, piece_counts):
            for index in range(count):
                place = swap_halves(line, half_bits) if side else line
                made.append(
                    pltpu.make_async_copy(
                        piece.at[pl.ds(index * line_rows, line_rows)],
                        (sib_rows if side else own_rows).at[pl.ds(place * line_rows, line_rows)],
                        row_sems.at[side, line],
                    )
                )
                line += 1
        return made

    def weight_copies(step, side):
        first = pl.multiple_of((1 - core if side else core) * half, half)
        return [
            pltpu.make_async_copy(
                weight_ref.at[
                    pl.ds(first, half),
                    pl.ds(pl.multiple_of(part * hidden_units + step * block, block), block),
                ],
                weights.at[step % 2, 2 * side + part],
                weight_sems.at[step % 2, 2 * side + part],
            )
            for part in range(2)
        ]

    def act_copy(step):
        columns = pl.ds(pl.multiple_of(step * block, block), block)
        return pltpu.make_async_copy(act.at[:, columns], act_ref.at[:, columns], act_sems.at[step])

    def start(copies):
        for copy in copies:
            copy.start()

    def wait(copies):
        for copy in copies:
            copy.wait()

    for side in range(2):
        start(row_copies(side) + weight_copies(0, side))

    @pl.loop(0, steps)
    def _(step):
        slot = step % 2

        @pl.when(step == 0)
        def _():
            wait(row_copies(0))

        wait(weight_copies(step, 0))

        @pl.when(step + 1 < steps)
        def _():
            start(weight_copies(step + 1, 0) + weight_copies(step + 1, 1))

        own_value = own_rows[:, :half]
        gate = jnp.dot(own_value, weights[slot, 0], preferred_element_type=jnp.float32)
        up = jnp.dot(own_value, weights[slot, 1], preferred_element_type=jnp.float32)

        @pl.when(step == 0)
        def _():
            wait(row_copies(1))

        wait(weight_copies(step, 1))
        sib_value = sib_rows[:, :half]
        gate += jnp.dot(sib_value, weights[slot, 2], preferred_element_type=jnp.float32)
        up += jnp.dot(sib_value, weights[slot, 3], preferred_element_type=jnp.float32)
        value = (gate / (1.0 + jnp.exp(-gate)) * up).astype(jnp.bfloat16)
        act[:, pl.ds(pl.multiple_of(step * block, block), block)] = value
        act_copy(step).start()

    if with_meta:
        meta = own_rows[:, half:].astype(jnp.float32) + sib_rows[:, half:].astype(jnp.float32)
        me = spot_ref[1].astype(jnp.float32)
        lanes = lax.broadcasted_iota(jnp.int32, meta.shape, 1)
        for step, scale_ref in enumerate(scale_refs):
            base = step * 4 * META_PICKS
            value = jnp.zeros_like(meta)
            for part in range(1, 4):
                low = base + part * META_PICKS
                named = pltpu.roll(meta, part * META_PICKS, 1) == me
                inside = (lanes >= low) & (lanes < low + META_PICKS)
                value = value + jnp.where(named & inside, meta, 0.0)
            total = jnp.sum(value, axis=1, keepdims=True)
            scale_ref[...] = jnp.broadcast_to(total, scale_ref.shape)
    for step in range(steps):
        act_copy(step).wait()


def expert_up(spot, own_pieces, sib_pieces, expert_in, line_rows, with_meta):
    piece_counts = [piece.shape[0] // line_rows for piece in own_pieces]
    wide = own_pieces[0].shape[1]
    half = expert_in.shape[0] // 2
    hidden_units = expert_in.shape[1] // 2
    rows = sum(piece_counts) * line_rows
    block = 256
    out_specs = [pl.BlockSpec(memory_space=pl.ANY)]
    out_shape = [jax.ShapeDtypeStruct((rows, hidden_units), jnp.bfloat16)]
    if with_meta:
        out_specs += [pl.BlockSpec((rows, LANES), lambda i, c: (0, 0))] * STEPS
        out_shape += [jax.ShapeDtypeStruct((rows, LANES), jnp.float32)] * STEPS
    held = 2 * rows * (2 * wide + hidden_units) + 16 * half * block
    return pl.pallas_call(
        functools.partial(up_body, line_rows, piece_counts, with_meta, block),
        grid_spec=pltpu.PrefetchScalarGridSpec(
            num_scalar_prefetch=1,
            grid=(1,),
            in_specs=[pl.BlockSpec(memory_space=pl.ANY)] * (2 * len(own_pieces) + 1),
            out_specs=out_specs,
            scratch_shapes=[
                pltpu.VMEM((rows, wide), jnp.bfloat16),
                pltpu.VMEM((rows, wide), jnp.bfloat16),
                pltpu.VMEM((2, 4, half, block), jnp.bfloat16),
                pltpu.VMEM((rows, hidden_units), jnp.bfloat16),
                pltpu.SemaphoreType.DMA((2, sum(piece_counts))),
                pltpu.SemaphoreType.DMA((2, 4)),
                pltpu.SemaphoreType.DMA((hidden_units // block,)),
            ],
        ),
        out_shape=out_shape,
        compiler_params=pltpu.CompilerParams(
            dimension_semantics=("arbitrary",), vmem_limit_bytes=max(47 << 20, held + 24 * rows * block + (4 << 20))
        ),
        cost_estimate=pl.CostEstimate(
            flops=8 * rows * half * hidden_units,
            bytes_accessed=8 * half * hidden_units + 4 * rows * wide + 2 * rows * hidden_units,
            transcendentals=rows * hidden_units,
        ),
        name="expert_up",
    )(spot, *own_pieces, *sib_pieces, expert_in)


def down_body(line_rows, jobs, spot_ref, act_ref, down_ref, scale_ref, *outs):
    del spot_ref
    per_job = pl.num_programs(0) // len(jobs)

    def run(groups, outs):
        lines = [line for group in groups for line in group]
        at = lambda ref: jnp.concatenate(
            [ref[line * line_rows : (line + 1) * line_rows] for line in lines], axis=0
        )
        answer = jnp.dot(at(act_ref), down_ref[...], preferred_element_type=jnp.float32)
        scale = at(scale_ref)
        for column in range(0, answer.shape[1], LANES):
            value = answer[:, column : column + LANES].astype(jnp.bfloat16).astype(jnp.float32)
            value = (value * scale).astype(jnp.bfloat16)
            first = 0
            for group, out in zip(groups, outs):
                rows = len(group) * line_rows
                out[:, column : column + LANES] = value[first : first + rows]
                first += rows

    first = 0
    for index, (_, groups) in enumerate(jobs):
        mine = outs[first : first + len(groups)]
        first += len(groups)
        if len(jobs) == 1:
            run(groups, mine)
        else:
            pl.when(pl.program_id(0) // per_job == index)(functools.partial(run, groups, mine))


def expert_down(spot, act, expert_out, scale, line_rows, jobs):
    rows, hidden_units = act.shape
    half = expert_out.shape[1] // 2
    block = 896
    steps = half // block

    def weight_at(i, c):
        side = jobs[0][0]
        for index, job in enumerate(jobs[1:]):
            side = jnp.where(i // steps > index, job[0], side)
        return (0, (c[0] + side - 2 * c[0] * side) * steps + i % steps)

    def out_at(index):
        return lambda i, c: (0, jnp.minimum(jnp.maximum(i - index * steps, 0), steps - 1))

    out_specs, out_shape = [], []
    for index, (_, groups) in enumerate(jobs):
        for group in groups:
            out_specs.append(pl.BlockSpec((len(group) * line_rows, block), out_at(index)))
            out_shape.append(jax.ShapeDtypeStruct((len(group) * line_rows, half), jnp.bfloat16))
    return pl.pallas_call(
        functools.partial(down_body, line_rows, jobs),
        grid_spec=pltpu.PrefetchScalarGridSpec(
            num_scalar_prefetch=1,
            grid=(steps * len(jobs),),
            in_specs=[
                pl.BlockSpec((rows, hidden_units), lambda i, c: (0, 0)),
                pl.BlockSpec((hidden_units, block), weight_at),
                pl.BlockSpec((rows, LANES), lambda i, c: (0, 0)),
            ],
            out_specs=out_specs,
        ),
        out_shape=out_shape,
        compiler_params=pltpu.CompilerParams(
            dimension_semantics=("arbitrary",),
            vmem_limit_bytes=4 * (rows + block) * hidden_units + 24 * rows * block + (2 << 20),
        ),
        cost_estimate=pl.CostEstimate(flops=1 << 36, bytes_accessed=1 << 10, transcendentals=0),
        name="expert_down",
    )(spot, act, expert_out, scale)


def meta_body(route_ref, weight_ref, meta_ref):
    token_count, wide = meta_ref.shape
    total = jnp.zeros((token_count, wide), jnp.float32)
    lanes = lax.broadcasted_iota(jnp.int32, (META_PICKS, wide), 1)
    picks = lax.broadcasted_iota(jnp.int32, (META_PICKS, wide), 0)
    for step in range(STEPS):
        weight = weight_ref[step]
        top = weight.astype(jnp.bfloat16)
        rest = weight - top.astype(jnp.float32)
        middle = rest.astype(jnp.bfloat16)
        last = (rest - middle.astype(jnp.float32)).astype(jnp.bfloat16)
        ids = route_ref[step].astype(jnp.float32).astype(jnp.bfloat16)
        for part, value in enumerate((ids, top, middle, last)):
            place = (step * 4 + part) * META_PICKS
            spots = (lanes == picks + place).astype(jnp.bfloat16)
            total += lax.dot_general(
                value, spots, (((0,), (0,)), ((), ())), preferred_element_type=jnp.float32
            )
    meta_ref[...] = total.astype(jnp.bfloat16)


def meta_columns(routes, weights):
    return pl.pallas_call(
        meta_body,
        out_shape=jax.ShapeDtypeStruct((routes.shape[2], LANES), jnp.bfloat16),
        name="meta_columns",
    )(routes, weights)


def pick_body(swapped_ref, cache_ref, first_ref, second_ref, info_ref, sems):
    row_count = swapped_ref.shape[0]
    for index in range(MOVE):
        info_ref[index] = 0

    def find(slot, count):
        @pl.when((swapped_ref[slot] == 1) & (count < MOVE))
        def _():
            info_ref[count] = slot

        return count + swapped_ref[slot]

    count = jnp.minimum(lax.fori_loop(0, row_count, find, jnp.int32(0)), MOVE)
    last = jnp.maximum(count - 1, 0)
    last_slot = info_ref[last]
    copies = []
    for index in range(MOVE):
        slot = jnp.where(index < count, info_ref[index], last_slot)
        info_ref[index] = slot
        info_ref[MOVE + index] = jnp.where(count > 0, jnp.minimum(index, last), -1)
        out_ref = first_ref if index < MOVE // 2 else second_ref
        copies.append(
            pltpu.make_async_copy(
                cache_ref.at[slot], out_ref.at[index % (MOVE // 2)], sems.at[index]
            )
        )
        copies[-1].start()
    for copy in copies:
        copy.wait()


def pick_caches(swapped, cache):
    part = jax.ShapeDtypeStruct((MOVE // 2,) + cache.shape[1:], cache.dtype)
    return pl.pallas_call(
        pick_body,
        grid_spec=pltpu.PrefetchScalarGridSpec(
            num_scalar_prefetch=1,
            grid=(1,),
            in_specs=[pl.BlockSpec(memory_space=pl.ANY)],
            out_specs=[
                pl.BlockSpec(part.shape, lambda i, _: (0, 0, 0)),
                pl.BlockSpec(part.shape, lambda i, _: (0, 0, 0)),
                pl.BlockSpec(memory_space=pltpu.SMEM),
            ],
            scratch_shapes=[pltpu.SemaphoreType.DMA((MOVE,))],
        ),
        out_shape=[part, part, jax.ShapeDtypeStruct((2 * MOVE,), jnp.int32)],
        name="pick_caches",
    )(swapped, cache)


def attend_one(query, cache, fresh, length):
    fresh = fresh.astype(jnp.float32)
    scores = jnp.dot(query, cache, preferred_element_type=jnp.float32) * SOFTMAX_SCALE
    own = jnp.sum(query.astype(jnp.float32) * fresh, axis=1, keepdims=True) * SOFTMAX_SCALE
    positions = lax.broadcasted_iota(jnp.int32, scores.shape, 1)
    scores = jnp.where(positions < length, scores, -jnp.inf)
    top = jnp.maximum(jnp.max(scores, axis=1, keepdims=True), own)
    weights = jnp.exp(scores - top)
    own_weight = jnp.exp(own - top)
    summed = jnp.sum(weights, axis=1, keepdims=True) + own_weight
    blended = lax.dot_general(
        weights.astype(jnp.bfloat16),
        cache[:LATENT],
        (((1,), (1,)), ((), ())),
        preferred_element_type=jnp.float32,
    )
    own_rounded = own_weight.astype(jnp.bfloat16).astype(jnp.float32)
    blended = blended + own_rounded * fresh[:, :LATENT]
    return (blended / summed).astype(jnp.bfloat16)


def attend_body(group, spot_ref, length_ref, query_ref, cache_ref, fresh_ref, out_ref):
    count = group * pl.num_programs(0)
    first = spot_ref[1] * count + pl.program_id(0) * group
    for slot in range(group):
        out_ref[slot] = attend_one(
            query_ref[slot], cache_ref[slot], fresh_ref[slot], length_ref[first + slot]
        )


def attend(spot, lengths, queries, cache, fresh):
    count, heads, full = queries.shape
    positions = cache.shape[2]
    group = 4
    return pl.pallas_call(
        functools.partial(attend_body, group),
        grid_spec=pltpu.PrefetchScalarGridSpec(
            num_scalar_prefetch=2,
            grid=(count // group,),
            in_specs=[
                pl.BlockSpec((group, heads, full), lambda i, *_: (i, 0, 0)),
                pl.BlockSpec((group, full, positions), lambda i, *_: (i, 0, 0)),
                pl.BlockSpec((group, 1, full), lambda i, *_: (i, 0, 0)),
            ],
            out_specs=pl.BlockSpec((group, heads, LATENT), lambda i, *_: (i, 0, 0)),
        ),
        out_shape=jax.ShapeDtypeStruct((count, heads, LATENT), jnp.bfloat16),
        compiler_params=pltpu.CompilerParams(
            dimension_semantics=("arbitrary",), vmem_limit_bytes=12 << 20
        ),
        cost_estimate=pl.CostEstimate(
            flops=4 * count * heads * full * positions,
            bytes_accessed=2 * count * (heads * (full + LATENT) + full * positions),
            transcendentals=count * heads * positions,
        ),
        name="attend",
    )(spot, lengths, queries, cache, fresh)


def attend_moved_body(
    row_count, spot_ref, length_ref, info_ref, query_ref, cache_ref, came_a_ref, came_b_ref, fresh_ref, old_ref, out_ref
):
    del old_ref
    index = pl.program_id(0)
    place = info_ref[MOVE + index]
    total = length_ref.shape[0]
    row = spot_ref[1] * row_count + info_ref[index]
    row = jnp.where(place >= 0, lax.rem(row + total // 2, total), row)
    came = jnp.where(place < MOVE // 2, came_a_ref[...], came_b_ref[...])[0]
    cache = jnp.where(place >= 0, came, cache_ref[0])
    out_ref[0] = attend_one(query_ref[0], cache, fresh_ref[0], length_ref[row])


def attend_moved(spot, lengths, info, queries, cache, came_a, came_b, fresh, context):
    row_count, heads, full = queries.shape
    positions = cache.shape[2]
    part = MOVE // 2
    at_slot = lambda i, spot, lengths, info: (info[i], 0, 0)
    clip = lambda value: jnp.minimum(jnp.maximum(value, 0), part - 1)
    one = (1, full, positions)
    return pl.pallas_call(
        functools.partial(attend_moved_body, row_count),
        grid_spec=pltpu.PrefetchScalarGridSpec(
            num_scalar_prefetch=3,
            grid=(MOVE,),
            in_specs=[
                pl.BlockSpec((1, heads, full), at_slot),
                pl.BlockSpec(one, at_slot),
                pl.BlockSpec(one, lambda i, spot, lengths, info: (clip(info[MOVE + i]), 0, 0)),
                pl.BlockSpec(
                    one, lambda i, spot, lengths, info: (clip(info[MOVE + i] - part), 0, 0)
                ),
                pl.BlockSpec((1, 1, full), at_slot),
                pl.BlockSpec(memory_space=pl.ANY),
            ],
            out_specs=pl.BlockSpec((1, heads, LATENT), at_slot),
        ),
        out_shape=jax.ShapeDtypeStruct(context.shape, context.dtype),
        input_output_aliases={8: 0},
        compiler_params=pltpu.CompilerParams(
            dimension_semantics=("arbitrary",), vmem_limit_bytes=48 << 20
        ),
        cost_estimate=pl.CostEstimate(flops=1 << 36, bytes_accessed=1 << 10, transcendentals=0),
        name="attend_moved",
    )(spot, lengths, info, queries, cache, came_a, came_b, fresh, context)


def per_device(
    hidden,
    routes,
    route_weights,
    expert_in,
    expert_out,
    queries,
    fresh_key,
    latent_cache,
    lengths,
    swapped,
):
    dp_count, ep_count = lax.axis_size("dp"), lax.axis_size("ep")
    device_count = dp_count * ep_count
    token_count, width = hidden.shape[1], hidden.shape[2]
    half = width // 2
    me = lax.axis_index(AXES)
    core = me % 2
    dp_bits, ep_bits = dp_count.bit_length() - 1, ep_count.bit_length() - 1
    x_masks = [ep_count << bit for bit in range(dp_bits - Z_BITS)]
    z_unit = ep_count << (dp_bits - Z_BITS)
    y_masks = [1 << bit for bit in range(1, ep_bits)]
    z_masks = [z_unit * step for step in range(1 << Z_BITS)]
    orders = (x_masks + y_masks, y_masks + x_masks)
    level_masks = list(zip(*orders))
    line_count = 1 << len(level_masks)
    sibling = (1, 1)
    spot = jnp.stack([core, me]).astype(jnp.int32)

    meta = meta_columns(jnp.swapaxes(routes, 1, 2), jnp.swapaxes(route_weights, 1, 2))

    own_half = lax.dynamic_slice_in_dim(hidden, core * half, half, axis=2)
    other_half = lax.dynamic_slice_in_dim(hidden, (1 - core) * half, half, axis=2)
    came_half = exchange(other_half, sibling)
    by_core = lambda mine, theirs, axis: jnp.where(
        core == 0,
        jnp.concatenate([mine, theirs], axis=axis),
        jnp.concatenate([theirs, mine], axis=axis),
    )
    pair = by_core(own_half, came_half, 1)
    pair_meta = by_core(meta, jnp.zeros_like(meta), 0)
    line_rows = len(z_masks) * 2 * token_count

    window = lambda *values: lax.optimization_barrier(values)
    far = device_count // 2
    bottom, top_masks = level_masks[:-1], level_masks[-1]

    def send_line(block):
        return [exchange(block, (mask, mask)) for mask in z_masks[1:]]

    def spread(line):
        for masks in bottom:
            line = jnp.concatenate([line, exchange(line, masks)], axis=0)
        return line

    add = lambda terms: functools.reduce(
        lambda total, term: total + term, [term.astype(jnp.float32) for term in terms]
    )
    rounded_sum = lambda terms: add(terms).astype(jnp.bfloat16)
    up = lambda own, sib, with_meta: expert_up(
        spot, own, sib, expert_in[0], line_rows, with_meta
    )
    down = lambda act, scale, *jobs: expert_down(
        spot, act, expert_out[0], scale, line_rows, jobs
    )
    half_bits = len(level_masks) // 2
    my_lines = list(range(line_count))
    their_lines = [swap_halves(line, half_bits) for line in my_lines]
    split = line_count // 2
    halves_of = lambda terms: (
        [term[: term.shape[0] // 2] for term in terms],
        [term[term.shape[0] // 2 :] for term in terms],
    )

    def fold(terms):
        for masks in reversed(bottom):
            terms, high = halves_of(terms)
            terms = terms + [exchange(rounded_sum(high), masks)]
        return terms

    def finish_sends(terms):
        block = 2 * token_count
        at = lambda place: [term[place * block : (place + 1) * block] for term in terms]
        return at(0), [rounded_sum(at(place)) for place in range(1, len(z_masks))]

    def finish_line(sends):
        return [exchange(value, (mask, mask)) for value, mask in zip(sends, z_masks[1:])]

    def finish(terms):
        total = rounded_sum(terms).reshape(2, token_count, half)
        kept = lax.dynamic_index_in_dim(total, core, 0, keepdims=False)
        sent = lax.dynamic_index_in_dim(total, 1 - core, 0, keepdims=False)
        return by_core(kept, exchange(sent, sibling), 1)

    block0 = jnp.concatenate([pair[0], pair_meta], axis=1)
    block0, swapped = window(block0, swapped)

    fresh = fresh_key[:, None, :]
    stored = jnp.swapaxes(latent_cache, 1, 2)

    came0 = send_line(block0)
    *leaving, info = pick_caches(swapped, stored)
    *came0, leave_a, leave_b, info = window(*came0, *leaving, info)

    low0 = spread(jnp.concatenate([block0] + came0, axis=0))
    low0, block1, early_queries = window(low0, pair[1], queries)

    high0 = exchange(low0, top_masks)
    sib_low0 = exchange(low0, sibling)
    came1 = send_line(block1)
    context = attend(spot, lengths, early_queries, stored, fresh)
    high0, sib_low0, context, *came1 = window(high0, sib_low0, context, *came1)

    line1 = jnp.concatenate([block1] + came1, axis=0)
    sib_high0 = exchange(high0, sibling)
    low0, high0, sib_low0, sib_high0, line1, leave_a = window(
        low0, high0, sib_low0, sib_high0, line1, leave_a
    )

    low1 = spread(line1)
    cache_a = exchange(leave_a, (far, far))
    act0, scale0, scale1 = up([low0, high0], [sib_low0, sib_high0], True)
    low1, cache_a, act0, scale0, scale1 = window(low1, cache_a, act0, scale0, scale1)

    part = low1.shape[0] // 2
    high1 = exchange(low1, top_masks)
    they_low0, they_high0 = down(act0, scale0, (1, (their_lines[:split], their_lines[split:])))
    sib_low1 = exchange(low1, sibling)
    they_low0, they_high0 = exchange(they_low0, sibling), exchange(they_high0, sibling)
    my_low0, my_high0 = down(act0, scale0, (0, (my_lines[:split], my_lines[split:])))
    high1, sib_low1, they_low0, they_high0, my_low0, my_high0 = window(
        high1, sib_low1, they_low0, they_high0, my_low0, my_high0
    )

    send0 = rounded_sum([my_high0, they_high0])
    sib_high1 = exchange(high1, sibling)
    send0, sib_high1, leave_b = window(send0, sib_high1, leave_b)

    came = exchange(send0, top_masks)
    cache_b = exchange(leave_b, (far, far))
    (act1,) = up([low1, high1], [sib_low1, sib_high1], False)
    came, act1, cache_b = window(came, act1, cache_b)

    terms0 = [my_low0, they_low0, came]
    for masks in reversed(bottom):
        terms0, high = halves_of(terms0)
        high, act1 = window(rounded_sum(high), act1)
        terms0 = terms0 + [exchange(high, masks)]

    they_high1, my_high1 = down(
        act1, scale1, (1, (their_lines[split:],)), (0, (my_lines[split:],))
    )
    they_high1 = exchange(they_high1, sibling)
    send1 = rounded_sum([my_high1, they_high1])
    send1, act1 = window(send1, act1)
    came = exchange(send1, top_masks)
    they_low1, my_low1 = down(
        act1, scale1, (1, (their_lines[:split],)), (0, (my_lines[:split],))
    )
    they_low1 = exchange(they_low1, sibling)
    kept0, sends0 = finish_sends(terms0)
    last0 = finish_line(sends0)
    came, they_low1, my_low1 = window(came, they_low1, my_low1)

    terms1 = [my_low1, they_low1, came]
    for masks in reversed(bottom):
        terms1, high = halves_of(terms1)
        high, queries = window(rounded_sum(high), queries)
        terms1 = terms1 + [exchange(high, masks)]
    context = attend_moved(
        spot, lengths, info, queries, stored, cache_a, cache_b, fresh, context
    )
    terms1[-1], context, *last0 = window(terms1[-1], context, *last0)
    kept1, sends1 = finish_sends(terms1)
    last1 = finish_line(sends1)
    mixed0 = finish(kept0 + last0)
    mixed1 = finish(kept1 + last1)
    return (jnp.stack([mixed0, mixed1]), context)


def solution(mesh):
    in_specs = (
        P(None, ("dp", "ep"), None),
        P(None, ("dp", "ep"), None),
        P(None, ("dp", "ep"), None),
        P(("dp", "ep"), None, None),
        P(("dp", "ep"), None, None),
        P(("dp", "ep"), None, None),
        P(("dp", "ep"), None),
        P(("dp", "ep"), None, None),
        P(),
        P(("dp", "ep")),
    )
    out_specs = (P(None, ("dp", "ep"), None), P(("dp", "ep"), None, None))
    return jax.shard_map(
        per_device, mesh=mesh, in_specs=in_specs, out_specs=out_specs, check_vma=False
    )
```

```python
import functools

import jax
import jax.numpy as jnp
from jax import lax
from jax.experimental import pallas as pl
from jax.experimental.pallas import tpu as pltpu
from jax.sharding import PartitionSpec as P

AXES = ("dp", "ep")
LATENT = 512
STEPS = 2
MOVE = 4
LANES = 128
META_PICKS = 8
Z_BITS = 2

SOFTMAX_SCALE = 192.0 ** (-0.5)


def exchange(value, masks):
    count = lax.axis_size(AXES)
    pairs = [(source, source ^ masks[source % 2]) for source in range(count)]
    return lax.ppermute(value, AXES, pairs)


def swap_halves(index, bits):
    low = index & ((1 << bits) - 1)
    return (low << bits) | (index >> bits)


def up_body(line_rows, piece_counts, with_meta, block, spot_ref, *refs):
    refs = list(refs)
    own = [refs.pop(0) for _ in piece_counts]
    sib = [refs.pop(0) for _ in piece_counts]
    weight_ref, act_ref = refs.pop(0), refs.pop(0)
    scale_refs = [refs.pop(0) for _ in range(STEPS if with_meta else 0)]
    own_rows, sib_rows, weights, act, row_sems, weight_sems, act_sems = refs
    line_count = sum(piece_counts)
    half_bits = (line_count.bit_length() - 1) // 2
    half = weight_ref.shape[0] // 2
    hidden_units = weight_ref.shape[1] // 2
    steps = hidden_units // block
    core = spot_ref[0]

    def row_copies(side):
        made = []
        line = 0
        for piece, count in zip(sib if side else own, piece_counts):
            for index in range(count):
                place = swap_halves(line, half_bits) if side else line
                made.append(
                    pltpu.make_async_copy(
                        piece.at[pl.ds(index * line_rows, line_rows)],
                        (sib_rows if side else own_rows).at[pl.ds(place * line_rows, line_rows)],
                        row_sems.at[side, line],
                    )
                )
                line += 1
        return made

    def weight_copies(step, side):
        first = pl.multiple_of((1 - core if side else core) * half, half)
        return [
            pltpu.make_async_copy(
                weight_ref.at[
                    pl.ds(first, half),
                    pl.ds(pl.multiple_of(part * hidden_units + step * block, block), block),
                ],
                weights.at[step % 2, 2 * side + part],
                weight_sems.at[step % 2, 2 * side + part],
            )
            for part in range(2)
        ]

    def act_copy(step):
        columns = pl.ds(pl.multiple_of(step * block, block), block)
        return pltpu.make_async_copy(act.at[:, columns], act_ref.at[:, columns], act_sems.at[step])

    def start(copies):
        for copy in copies:
            copy.start()

    def wait(copies):
        for copy in copies:
            copy.wait()

    for side in range(2):
        start(row_copies(side) + weight_copies(0, side))

    @pl.loop(0, steps)
    def _(step):
        slot = step % 2

        @pl.when(step == 0)
        def _():
            wait(row_copies(0))

        wait(weight_copies(step, 0))

        @pl.when(step + 1 < steps)
        def _():
            start(weight_copies(step + 1, 0) + weight_copies(step + 1, 1))

        own_value = own_rows[:, :half]
        gate = jnp.dot(own_value, weights[slot, 0], preferred_element_type=jnp.float32)
        up = jnp.dot(own_value, weights[slot, 1], preferred_element_type=jnp.float32)

        @pl.when(step == 0)
        def _():
            wait(row_copies(1))

        wait(weight_copies(step, 1))
        sib_value = sib_rows[:, :half]
        gate += jnp.dot(sib_value, weights[slot, 2], preferred_element_type=jnp.float32)
        up += jnp.dot(sib_value, weights[slot, 3], preferred_element_type=jnp.float32)
        value = (gate / (1.0 + jnp.exp(-gate)) * up).astype(jnp.bfloat16)
        act[:, pl.ds(pl.multiple_of(step * block, block), block)] = value
        act_copy(step).start()

    if with_meta:
        meta = own_rows[:, half:].astype(jnp.float32) + sib_rows[:, half:].astype(jnp.float32)
        me = spot_ref[1].astype(jnp.float32)
        lanes = lax.broadcasted_iota(jnp.int32, meta.shape, 1)
        for step, scale_ref in enumerate(scale_refs):
            base = step * 4 * META_PICKS
            value = jnp.zeros_like(meta)
            for part in range(1, 4):
                low = base + part * META_PICKS
                named = pltpu.roll(meta, part * META_PICKS, 1) == me
                inside = (lanes >= low) & (lanes < low + META_PICKS)
                value = value + jnp.where(named & inside, meta, 0.0)
            total = jnp.sum(value, axis=1, keepdims=True)
            scale_ref[...] = jnp.broadcast_to(total, scale_ref.shape)
    for step in range(steps):
        act_copy(step).wait()


def expert_up(spot, own_pieces, sib_pieces, expert_in, line_rows, with_meta):
    piece_counts = [piece.shape[0] // line_rows for piece in own_pieces]
    wide = own_pieces[0].shape[1]
    half = expert_in.shape[0] // 2
    hidden_units = expert_in.shape[1] // 2
    rows = sum(piece_counts) * line_rows
    block = 256
    out_specs = [pl.BlockSpec(memory_space=pl.ANY)]
    out_shape = [jax.ShapeDtypeStruct((rows, hidden_units), jnp.bfloat16)]
    if with_meta:
        out_specs += [pl.BlockSpec((rows, LANES), lambda i, c: (0, 0))] * STEPS
        out_shape += [jax.ShapeDtypeStruct((rows, LANES), jnp.float32)] * STEPS
    held = 2 * rows * (2 * wide + hidden_units) + 16 * half * block
    return pl.pallas_call(
        functools.partial(up_body, line_rows, piece_counts, with_meta, block),
        grid_spec=pltpu.PrefetchScalarGridSpec(
            num_scalar_prefetch=1,
            grid=(1,),
            in_specs=[pl.BlockSpec(memory_space=pl.ANY)] * (2 * len(own_pieces) + 1),
            out_specs=out_specs,
            scratch_shapes=[
                pltpu.VMEM((rows, wide), jnp.bfloat16),
                pltpu.VMEM((rows, wide), jnp.bfloat16),
                pltpu.VMEM((2, 4, half, block), jnp.bfloat16),
                pltpu.VMEM((rows, hidden_units), jnp.bfloat16),
                pltpu.SemaphoreType.DMA((2, sum(piece_counts))),
                pltpu.SemaphoreType.DMA((2, 4)),
                pltpu.SemaphoreType.DMA((hidden_units // block,)),
            ],
        ),
        out_shape=out_shape,
        compiler_params=pltpu.CompilerParams(
            dimension_semantics=("arbitrary",), vmem_limit_bytes=max(47 << 20, held + 24 * rows * block + (4 << 20))
        ),
        cost_estimate=pl.CostEstimate(
            flops=8 * rows * half * hidden_units,
            bytes_accessed=8 * half * hidden_units + 4 * rows * wide + 2 * rows * hidden_units,
            transcendentals=rows * hidden_units,
        ),
        name="expert_up",
    )(spot, *own_pieces, *sib_pieces, expert_in)


def down_body(line_rows, jobs, spot_ref, act_ref, down_ref, scale_ref, *outs):
    del spot_ref
    per_job = pl.num_programs(0) // len(jobs)

    def run(groups, outs):
        lines = [line for group in groups for line in group]
        at = lambda ref: jnp.concatenate(
            [ref[line * line_rows : (line + 1) * line_rows] for line in lines], axis=0
        )
        answer = jnp.dot(at(act_ref), down_ref[...], preferred_element_type=jnp.float32)
        scale = at(scale_ref)
        for column in range(0, answer.shape[1], LANES):
            value = answer[:, column : column + LANES].astype(jnp.bfloat16).astype(jnp.float32)
            value = (value * scale).astype(jnp.bfloat16)
            first = 0
            for group, out in zip(groups, outs):
                rows = len(group) * line_rows
                out[:, column : column + LANES] = value[first : first + rows]
                first += rows

    first = 0
    for index, (_, groups) in enumerate(jobs):
        mine = outs[first : first + len(groups)]
        first += len(groups)
        if len(jobs) == 1:
            run(groups, mine)
        else:
            pl.when(pl.program_id(0) // per_job == index)(functools.partial(run, groups, mine))


def expert_down(spot, act, expert_out, scale, line_rows, jobs):
    rows, hidden_units = act.shape
    half = expert_out.shape[1] // 2
    block = 896
    steps = half // block

    def weight_at(i, c):
        side = jobs[0][0]
        for index, job in enumerate(jobs[1:]):
            side = jnp.where(i // steps > index, job[0], side)
        return (0, (c[0] + side - 2 * c[0] * side) * steps + i % steps)

    def out_at(index):
        return lambda i, c: (0, jnp.minimum(jnp.maximum(i - index * steps, 0), steps - 1))

    out_specs, out_shape = [], []
    for index, (_, groups) in enumerate(jobs):
        for group in groups:
            out_specs.append(pl.BlockSpec((len(group) * line_rows, block), out_at(index)))
            out_shape.append(jax.ShapeDtypeStruct((len(group) * line_rows, half), jnp.bfloat16))
    return pl.pallas_call(
        functools.partial(down_body, line_rows, jobs),
        grid_spec=pltpu.PrefetchScalarGridSpec(
            num_scalar_prefetch=1,
            grid=(steps * len(jobs),),
            in_specs=[
                pl.BlockSpec((rows, hidden_units), lambda i, c: (0, 0)),
                pl.BlockSpec((hidden_units, block), weight_at),
                pl.BlockSpec((rows, LANES), lambda i, c: (0, 0)),
            ],
            out_specs=out_specs,
        ),
        out_shape=out_shape,
        compiler_params=pltpu.CompilerParams(
            dimension_semantics=("arbitrary",),
            vmem_limit_bytes=4 * (rows + block) * hidden_units + 24 * rows * block + (2 << 20),
        ),
        cost_estimate=pl.CostEstimate(flops=1 << 36, bytes_accessed=1 << 10, transcendentals=0),
        name="expert_down",
    )(spot, act, expert_out, scale)


def meta_body(route_ref, weight_ref, meta_ref):
    parts = []
    for step in range(STEPS):
        weight = weight_ref[step]
        top = weight.astype(jnp.bfloat16).astype(jnp.float32)
        middle = (weight - top).astype(jnp.bfloat16).astype(jnp.float32)
        parts += [route_ref[step].astype(jnp.float32), top, middle, weight - top - middle]
    value = jnp.concatenate(parts, axis=0).astype(jnp.bfloat16)
    shape = (value.shape[0], meta_ref.shape[1])
    rows = lax.broadcasted_iota(jnp.int32, shape, 0)
    lanes = lax.broadcasted_iota(jnp.int32, shape, 1)
    spots = (rows == lanes).astype(jnp.bfloat16)
    turned = lax.dot_general(
        value, spots, (((0,), (0,)), ((), ())), preferred_element_type=jnp.float32
    )
    meta_ref[...] = turned.astype(jnp.bfloat16)


def meta_columns(routes, weights):
    return pl.pallas_call(
        meta_body,
        out_shape=jax.ShapeDtypeStruct((routes.shape[2], LANES), jnp.bfloat16),
        name="meta_columns",
    )(routes, weights)


def pick_body(swapped_ref, cache_ref, first_ref, second_ref, info_ref, sems):
    row_count = swapped_ref.shape[0]
    for index in range(MOVE):
        info_ref[index] = 0

    def find(slot, count):
        @pl.when((swapped_ref[slot] == 1) & (count < MOVE))
        def _():
            info_ref[count] = slot

        return count + swapped_ref[slot]

    count = jnp.minimum(lax.fori_loop(0, row_count, find, jnp.int32(0)), MOVE)
    last = jnp.maximum(count - 1, 0)
    last_slot = info_ref[last]
    copies = []
    for index in range(MOVE):
        slot = jnp.where(index < count, info_ref[index], last_slot)
        info_ref[index] = slot
        info_ref[MOVE + index] = jnp.where(count > 0, jnp.minimum(index, last), -1)
        out_ref = first_ref if index < MOVE // 2 else second_ref
        copies.append(
            pltpu.make_async_copy(
                cache_ref.at[slot], out_ref.at[index % (MOVE // 2)], sems.at[index]
            )
        )
        copies[-1].start()
    for copy in copies:
        copy.wait()


def pick_caches(swapped, cache):
    part = jax.ShapeDtypeStruct((MOVE // 2,) + cache.shape[1:], cache.dtype)
    return pl.pallas_call(
        pick_body,
        grid_spec=pltpu.PrefetchScalarGridSpec(
            num_scalar_prefetch=1,
            grid=(1,),
            in_specs=[pl.BlockSpec(memory_space=pl.ANY)],
            out_specs=[
                pl.BlockSpec(part.shape, lambda i, _: (0, 0, 0)),
                pl.BlockSpec(part.shape, lambda i, _: (0, 0, 0)),
                pl.BlockSpec(memory_space=pltpu.SMEM),
            ],
            scratch_shapes=[pltpu.SemaphoreType.DMA((MOVE,))],
        ),
        out_shape=[part, part, jax.ShapeDtypeStruct((2 * MOVE,), jnp.int32)],
        name="pick_caches",
    )(swapped, cache)


def attend_one(query, cache, fresh, length):
    fresh = fresh.astype(jnp.float32)
    scores = jnp.dot(query, cache, preferred_element_type=jnp.float32) * SOFTMAX_SCALE
    own = jnp.sum(query.astype(jnp.float32) * fresh, axis=1, keepdims=True) * SOFTMAX_SCALE
    positions = lax.broadcasted_iota(jnp.int32, scores.shape, 1)
    scores = jnp.where(positions < length, scores, -jnp.inf)
    top = jnp.maximum(jnp.max(scores, axis=1, keepdims=True), own)
    weights = jnp.exp(scores - top)
    own_weight = jnp.exp(own - top)
    summed = jnp.sum(weights, axis=1, keepdims=True) + own_weight
    blended = lax.dot_general(
        weights.astype(jnp.bfloat16),
        cache[:LATENT],
        (((1,), (1,)), ((), ())),
        preferred_element_type=jnp.float32,
    )
    own_rounded = own_weight.astype(jnp.bfloat16).astype(jnp.float32)
    blended = blended + own_rounded * fresh[:, :LATENT]
    return (blended / summed).astype(jnp.bfloat16)


def attend_body(group, spot_ref, length_ref, query_ref, cache_ref, fresh_ref, out_ref):
    count = group * pl.num_programs(0)
    first = spot_ref[1] * count + pl.program_id(0) * group
    for slot in range(group):
        out_ref[slot] = attend_one(
            query_ref[slot], cache_ref[slot], fresh_ref[slot], length_ref[first + slot]
        )


def attend(spot, lengths, queries, cache, fresh):
    count, heads, full = queries.shape
    positions = cache.shape[2]
    group = 4
    return pl.pallas_call(
        functools.partial(attend_body, group),
        grid_spec=pltpu.PrefetchScalarGridSpec(
            num_scalar_prefetch=2,
            grid=(count // group,),
            in_specs=[
                pl.BlockSpec((group, heads, full), lambda i, *_: (i, 0, 0)),
                pl.BlockSpec((group, full, positions), lambda i, *_: (i, 0, 0)),
                pl.BlockSpec((group, 1, full), lambda i, *_: (i, 0, 0)),
            ],
            out_specs=pl.BlockSpec((group, heads, LATENT), lambda i, *_: (i, 0, 0)),
        ),
        out_shape=jax.ShapeDtypeStruct((count, heads, LATENT), jnp.bfloat16),
        compiler_params=pltpu.CompilerParams(
            dimension_semantics=("arbitrary",), vmem_limit_bytes=12 << 20
        ),
        cost_estimate=pl.CostEstimate(
            flops=4 * count * heads * full * positions,
            bytes_accessed=2 * count * (heads * (full + LATENT) + full * positions),
            transcendentals=count * heads * positions,
        ),
        name="attend",
    )(spot, lengths, queries, cache, fresh)


def attend_moved_body(
    row_count, spot_ref, length_ref, info_ref, query_ref, cache_ref, came_a_ref, came_b_ref, fresh_ref, old_ref, out_ref
):
    del old_ref
    index = pl.program_id(0)
    place = info_ref[MOVE + index]
    total = length_ref.shape[0]
    row = spot_ref[1] * row_count + info_ref[index]
    row = jnp.where(place >= 0, lax.rem(row + total // 2, total), row)
    came = jnp.where(place < MOVE // 2, came_a_ref[...], came_b_ref[...])[0]
    cache = jnp.where(place >= 0, came, cache_ref[0])
    out_ref[0] = attend_one(query_ref[0], cache, fresh_ref[0], length_ref[row])


def attend_moved(spot, lengths, info, queries, cache, came_a, came_b, fresh, context):
    row_count, heads, full = queries.shape
    positions = cache.shape[2]
    part = MOVE // 2
    at_slot = lambda i, spot, lengths, info: (info[i], 0, 0)
    clip = lambda value: jnp.minimum(jnp.maximum(value, 0), part - 1)
    one = (1, full, positions)
    return pl.pallas_call(
        functools.partial(attend_moved_body, row_count),
        grid_spec=pltpu.PrefetchScalarGridSpec(
            num_scalar_prefetch=3,
            grid=(MOVE,),
            in_specs=[
                pl.BlockSpec((1, heads, full), at_slot),
                pl.BlockSpec(one, at_slot),
                pl.BlockSpec(one, lambda i, spot, lengths, info: (clip(info[MOVE + i]), 0, 0)),
                pl.BlockSpec(
                    one, lambda i, spot, lengths, info: (clip(info[MOVE + i] - part), 0, 0)
                ),
                pl.BlockSpec((1, 1, full), at_slot),
                pl.BlockSpec(memory_space=pl.ANY),
            ],
            out_specs=pl.BlockSpec((1, heads, LATENT), at_slot),
        ),
        out_shape=jax.ShapeDtypeStruct(context.shape, context.dtype),
        input_output_aliases={8: 0},
        compiler_params=pltpu.CompilerParams(
            dimension_semantics=("arbitrary",), vmem_limit_bytes=48 << 20
        ),
        cost_estimate=pl.CostEstimate(flops=1 << 36, bytes_accessed=1 << 10, transcendentals=0),
        name="attend_moved",
    )(spot, lengths, info, queries, cache, came_a, came_b, fresh, context)


def per_device(
    hidden,
    routes,
    route_weights,
    expert_in,
    expert_out,
    queries,
    fresh_key,
    latent_cache,
    lengths,
    swapped,
):
    dp_count, ep_count = lax.axis_size("dp"), lax.axis_size("ep")
    device_count = dp_count * ep_count
    token_count, width = hidden.shape[1], hidden.shape[2]
    half = width // 2
    me = lax.axis_index(AXES)
    core = me % 2
    dp_bits, ep_bits = dp_count.bit_length() - 1, ep_count.bit_length() - 1
    x_masks = [ep_count << bit for bit in range(dp_bits - Z_BITS)]
    z_unit = ep_count << (dp_bits - Z_BITS)
    y_masks = [1 << bit for bit in range(1, ep_bits)]
    z_masks = [z_unit * step for step in range(1 << Z_BITS)]
    orders = (x_masks + y_masks, y_masks + x_masks)
    level_masks = list(zip(*orders))
    line_count = 1 << len(level_masks)
    sibling = (1, 1)
    spot = jnp.stack([core, me]).astype(jnp.int32)

    meta = meta_columns(jnp.swapaxes(routes, 1, 2), jnp.swapaxes(route_weights, 1, 2))

    own_half = lax.dynamic_slice_in_dim(hidden, core * half, half, axis=2)
    other_half = lax.dynamic_slice_in_dim(hidden, (1 - core) * half, half, axis=2)
    came_half = exchange(other_half, sibling)
    by_core = lambda mine, theirs, axis: jnp.where(
        core == 0,
        jnp.concatenate([mine, theirs], axis=axis),
        jnp.concatenate([theirs, mine], axis=axis),
    )
    pair = by_core(own_half, came_half, 1)
    pair_meta = by_core(meta, jnp.zeros_like(meta), 0)
    line_rows = len(z_masks) * 2 * token_count

    window = lambda *values: lax.optimization_barrier(values)
    far = device_count // 2
    bottom, top_masks = level_masks[:-1], level_masks[-1]

    swap = lambda value: exchange(value, sibling)

    def send_line(block):
        return [exchange(block, (mask, mask)) for mask in z_masks[1:]]

    def spread(line):
        for masks in bottom:
            line = jnp.concatenate([line, exchange(line, masks)], axis=0)
        return line

    add = lambda terms: functools.reduce(
        lambda total, term: total + term, [term.astype(jnp.float32) for term in terms]
    )
    rounded_sum = lambda terms: add(terms).astype(jnp.bfloat16)
    up = lambda own, sib, with_meta: expert_up(
        spot, own, sib, expert_in[0], line_rows, with_meta
    )
    down = lambda act, scale, *jobs: expert_down(
        spot, act, expert_out[0], scale, line_rows, jobs
    )
    half_bits = len(level_masks) // 2
    my_lines = list(range(line_count))
    their_lines = [swap_halves(line, half_bits) for line in my_lines]
    split = line_count // 2
    halves_of = lambda terms: (
        [term[: term.shape[0] // 2] for term in terms],
        [term[term.shape[0] // 2 :] for term in terms],
    )

    def fold(terms):
        for masks in reversed(bottom):
            terms, high = halves_of(terms)
            terms = terms + [exchange(rounded_sum(high), masks)]
        return terms

    def finish_sends(terms):
        block = 2 * token_count
        at = lambda place: [term[place * block : (place + 1) * block] for term in terms]
        return at(0), [rounded_sum(at(place)) for place in range(1, len(z_masks))]

    def finish_line(sends):
        return [exchange(value, (mask, mask)) for value, mask in zip(sends, z_masks[1:])]

    def finish(terms):
        total = rounded_sum(terms).reshape(2, token_count, half)
        kept = lax.dynamic_index_in_dim(total, core, 0, keepdims=False)
        sent = lax.dynamic_index_in_dim(total, 1 - core, 0, keepdims=False)
        return by_core(kept, exchange(sent, sibling), 1)

    block0 = jnp.concatenate([pair[0], pair_meta], axis=1)
    block0, swapped = window(block0, swapped)

    fresh = fresh_key[:, None, :]
    stored = jnp.swapaxes(latent_cache, 1, 2)

    came0 = send_line(block0)
    *leaving, info = pick_caches(swapped, stored)
    *came0, leave_a, leave_b, info = window(*came0, *leaving, info)

    low0 = spread(jnp.concatenate([block0] + came0, axis=0))
    low0, block1, early_queries = window(low0, pair[1], queries)

    high0 = exchange(low0, top_masks)
    sib_low0 = exchange(low0, sibling)
    came1 = send_line(block1)
    context = attend(spot, lengths, early_queries, stored, fresh)
    high0, sib_low0, context, *came1 = window(high0, sib_low0, context, *came1)

    line1 = jnp.concatenate([block1] + came1, axis=0)
    sib_high0 = exchange(high0, sibling)
    low0, high0, sib_low0, sib_high0, line1, leave_a = window(
        low0, high0, sib_low0, sib_high0, line1, leave_a
    )

    low1 = [line1]
    for masks in bottom:
        low1 = low1 + [exchange(line, masks) for line in low1]
    first1 = exchange(line1, top_masks)
    cache_a = exchange(leave_a, (far, far))
    act0, scale0, scale1 = up([low0, high0], [sib_low0, sib_high0], True)
    first1, cache_a, act0, scale0, scale1, *low1 = window(
        first1, cache_a, act0, scale0, scale1, *low1
    )

    rest1 = [exchange(line, top_masks) for line in low1[1:]]
    sib_low1 = [swap(line) for line in low1]
    sib_first1 = swap(first1)
    they_low0, they_high0 = down(act0, scale0, (1, (their_lines[:split], their_lines[split:])))
    they_low0, they_high0 = swap(they_low0), swap(they_high0)
    my_low0, my_high0 = down(act0, scale0, (0, (my_lines[:split], my_lines[split:])))
    sib_first1, they_low0, they_high0, my_low0, my_high0, *flat = window(
        sib_first1, they_low0, they_high0, my_low0, my_high0, *sib_low1, *rest1
    )
    sib_low1, rest1 = flat[:split], flat[split:]

    send0 = rounded_sum([my_high0, they_high0])
    sib_rest1 = [swap(line) for line in rest1]
    send0, leave_b, *sib_rest1 = window(send0, leave_b, *sib_rest1)

    came = exchange(send0, top_masks)
    cache_b = exchange(leave_b, (far, far))
    (act1,) = up(low1 + [first1] + rest1, sib_low1 + [sib_first1] + sib_rest1, False)
    came, act1, cache_b = window(came, act1, cache_b)

    they_high1, my_high1 = down(
        act1, scale1, (1, (their_lines[split:],)), (0, (my_lines[split:],))
    )
    terms0 = [my_low0, they_low0, came]
    for masks in reversed(bottom):
        terms0, high = halves_of(terms0)
        high, my_high1 = window(rounded_sum(high), my_high1)
        terms0 = terms0 + [exchange(high, masks)]

    they_high1 = exchange(they_high1, sibling)
    send1 = rounded_sum([my_high1, they_high1])
    send1, act1 = window(send1, act1)
    came = exchange(send1, top_masks)
    they_low1, my_low1 = down(
        act1, scale1, (1, (their_lines[:split],)), (0, (my_lines[:split],))
    )
    they_low1 = exchange(they_low1, sibling)
    kept0, sends0 = finish_sends(terms0)
    last0 = finish_line(sends0)
    came, my_low1 = window(came, my_low1)

    terms1 = [my_low1, they_low1, came]
    for masks in reversed(bottom):
        terms1, high = halves_of(terms1)
        high, queries = window(rounded_sum(high), queries)
        terms1 = terms1 + [exchange(high, masks)]
    context = attend_moved(
        spot, lengths, info, queries, stored, cache_a, cache_b, fresh, context
    )
    terms1[-1], context, *last0 = window(terms1[-1], context, *last0)
    kept1, sends1 = finish_sends(terms1)
    last1 = finish_line(sends1)
    mixed0 = finish(kept0 + last0)
    mixed1 = finish(kept1 + last1)
    return (jnp.stack([mixed0, mixed1]), context)


def solution(mesh):
    in_specs = (
        P(None, ("dp", "ep"), None),
        P(None, ("dp", "ep"), None),
        P(None, ("dp", "ep"), None),
        P(("dp", "ep"), None, None),
        P(("dp", "ep"), None, None),
        P(("dp", "ep"), None, None),
        P(("dp", "ep"), None),
        P(("dp", "ep"), None, None),
        P(),
        P(("dp", "ep")),
    )
    out_specs = (P(None, ("dp", "ep"), None), P(("dp", "ep"), None, None))
    return jax.shard_map(
        per_device, mesh=mesh, in_specs=in_specs, out_specs=out_specs, check_vma=False
    )
```

```python
import functools

import jax
import jax.numpy as jnp
from jax import lax
from jax.experimental import pallas as pl
from jax.experimental.pallas import tpu as pltpu
from jax.sharding import PartitionSpec as P

AXES = ("dp", "ep")
LATENT = 512
STEPS = 2
MOVE = 4
LANES = 128
META_PICKS = 8
Z_BITS = 2

SOFTMAX_SCALE = 192.0 ** (-0.5)


def exchange(value, masks):
    count = lax.axis_size(AXES)
    pairs = [(source, source ^ masks[source % 2]) for source in range(count)]
    return lax.ppermute(value, AXES, pairs)


def swap_halves(index, bits):
    low = index & ((1 << bits) - 1)
    return (low << bits) | (index >> bits)


def up_body(line_rows, piece_counts, with_meta, block, spot_ref, *refs):
    refs = list(refs)
    own = [refs.pop(0) for _ in piece_counts]
    sib = [refs.pop(0) for _ in piece_counts]
    weight_ref, act_ref = refs.pop(0), refs.pop(0)
    scale_refs = [refs.pop(0) for _ in range(STEPS if with_meta else 0)]
    own_rows, sib_rows, weights, act, row_sems, weight_sems, act_sems = refs
    line_count = sum(piece_counts)
    half_bits = (line_count.bit_length() - 1) // 2
    half = weight_ref.shape[0] // 2
    hidden_units = weight_ref.shape[1] // 2
    steps = hidden_units // block
    core = spot_ref[0]

    def row_copies(side):
        made = []
        line = 0
        for piece, count in zip(sib if side else own, piece_counts):
            for index in range(count):
                place = swap_halves(line, half_bits) if side else line
                made.append(
                    pltpu.make_async_copy(
                        piece.at[pl.ds(index * line_rows, line_rows)],
                        (sib_rows if side else own_rows).at[pl.ds(place * line_rows, line_rows)],
                        row_sems.at[side, line],
                    )
                )
                line += 1
        return made

    def weight_copies(step, side):
        first = pl.multiple_of((1 - core if side else core) * half, half)
        return [
            pltpu.make_async_copy(
                weight_ref.at[
                    pl.ds(first, half),
                    pl.ds(pl.multiple_of(part * hidden_units + step * block, block), block),
                ],
                weights.at[step % 2, 2 * side + part],
                weight_sems.at[step % 2, 2 * side + part],
            )
            for part in range(2)
        ]

    def act_copy(step):
        columns = pl.ds(pl.multiple_of(step * block, block), block)
        return pltpu.make_async_copy(act.at[:, columns], act_ref.at[:, columns], act_sems.at[step])

    def start(copies):
        for copy in copies:
            copy.start()

    def wait(copies):
        for copy in copies:
            copy.wait()

    for side in range(2):
        start(row_copies(side) + weight_copies(0, side))

    @pl.loop(0, steps)
    def _(step):
        slot = step % 2

        @pl.when(step == 0)
        def _():
            wait(row_copies(0))

        wait(weight_copies(step, 0))

        @pl.when(step + 1 < steps)
        def _():
            start(weight_copies(step + 1, 0) + weight_copies(step + 1, 1))

        own_value = own_rows[:, :half]
        gate = jnp.dot(own_value, weights[slot, 0], preferred_element_type=jnp.float32)
        up = jnp.dot(own_value, weights[slot, 1], preferred_element_type=jnp.float32)

        @pl.when(step == 0)
        def _():
            wait(row_copies(1))

        wait(weight_copies(step, 1))
        sib_value = sib_rows[:, :half]
        gate += jnp.dot(sib_value, weights[slot, 2], preferred_element_type=jnp.float32)
        up += jnp.dot(sib_value, weights[slot, 3], preferred_element_type=jnp.float32)
        value = (gate / (1.0 + jnp.exp(-gate)) * up).astype(jnp.bfloat16)
        act[:, pl.ds(pl.multiple_of(step * block, block), block)] = value
        act_copy(step).start()

    if with_meta:
        meta = own_rows[:, half:].astype(jnp.float32) + sib_rows[:, half:].astype(jnp.float32)
        me = spot_ref[1].astype(jnp.float32)
        lanes = lax.broadcasted_iota(jnp.int32, meta.shape, 1)
        for step, scale_ref in enumerate(scale_refs):
            base = step * 4 * META_PICKS
            value = jnp.zeros_like(meta)
            for part in range(1, 4):
                low = base + part * META_PICKS
                named = pltpu.roll(meta, part * META_PICKS, 1) == me
                inside = (lanes >= low) & (lanes < low + META_PICKS)
                value = value + jnp.where(named & inside, meta, 0.0)
            total = jnp.sum(value, axis=1, keepdims=True)
            scale_ref[...] = jnp.broadcast_to(total, scale_ref.shape)
    for step in range(steps):
        act_copy(step).wait()


def expert_up(spot, own_pieces, sib_pieces, expert_in, line_rows, with_meta):
    piece_counts = [piece.shape[0] // line_rows for piece in own_pieces]
    wide = own_pieces[0].shape[1]
    half = expert_in.shape[0] // 2
    hidden_units = expert_in.shape[1] // 2
    rows = sum(piece_counts) * line_rows
    block = 256
    out_specs = [pl.BlockSpec(memory_space=pl.ANY)]
    out_shape = [jax.ShapeDtypeStruct((rows, hidden_units), jnp.bfloat16)]
    if with_meta:
        out_specs += [pl.BlockSpec((rows, LANES), lambda i, c: (0, 0))] * STEPS
        out_shape += [jax.ShapeDtypeStruct((rows, LANES), jnp.float32)] * STEPS
    held = 2 * rows * (2 * wide + hidden_units) + 16 * half * block
    return pl.pallas_call(
        functools.partial(up_body, line_rows, piece_counts, with_meta, block),
        grid_spec=pltpu.PrefetchScalarGridSpec(
            num_scalar_prefetch=1,
            grid=(1,),
            in_specs=[pl.BlockSpec(memory_space=pl.ANY)] * (2 * len(own_pieces) + 1),
            out_specs=out_specs,
            scratch_shapes=[
                pltpu.VMEM((rows, wide), jnp.bfloat16),
                pltpu.VMEM((rows, wide), jnp.bfloat16),
                pltpu.VMEM((2, 4, half, block), jnp.bfloat16),
                pltpu.VMEM((rows, hidden_units), jnp.bfloat16),
                pltpu.SemaphoreType.DMA((2, sum(piece_counts))),
                pltpu.SemaphoreType.DMA((2, 4)),
                pltpu.SemaphoreType.DMA((hidden_units // block,)),
            ],
        ),
        out_shape=out_shape,
        compiler_params=pltpu.CompilerParams(
            dimension_semantics=("arbitrary",), vmem_limit_bytes=max(47 << 20, held + 24 * rows * block + (4 << 20))
        ),
        cost_estimate=pl.CostEstimate(
            flops=8 * rows * half * hidden_units,
            bytes_accessed=8 * half * hidden_units + 4 * rows * wide + 2 * rows * hidden_units,
            transcendentals=rows * hidden_units,
        ),
        name="expert_up",
    )(spot, *own_pieces, *sib_pieces, expert_in)


def down_body(line_rows, jobs, spot_ref, act_ref, down_ref, scale_ref, *outs):
    del spot_ref
    per_job = pl.num_programs(0) // len(jobs)

    def run(groups, outs):
        lines = [line for group in groups for line in group]
        at = lambda ref: jnp.concatenate(
            [ref[line * line_rows : (line + 1) * line_rows] for line in lines], axis=0
        )
        answer = jnp.dot(at(act_ref), down_ref[...], preferred_element_type=jnp.float32)
        scale = at(scale_ref)
        for column in range(0, answer.shape[1], LANES):
            value = answer[:, column : column + LANES].astype(jnp.bfloat16).astype(jnp.float32)
            value = (value * scale).astype(jnp.bfloat16)
            first = 0
            for group, out in zip(groups, outs):
                rows = len(group) * line_rows
                out[:, column : column + LANES] = value[first : first + rows]
                first += rows

    first = 0
    for index, (_, groups) in enumerate(jobs):
        mine = outs[first : first + len(groups)]
        first += len(groups)
        if len(jobs) == 1:
            run(groups, mine)
        else:
            pl.when(pl.program_id(0) // per_job == index)(functools.partial(run, groups, mine))


def expert_down(spot, act, expert_out, scale, line_rows, jobs):
    rows, hidden_units = act.shape
    half = expert_out.shape[1] // 2
    block = 896
    steps = half // block

    def weight_at(i, c):
        side = jobs[0][0]
        for index, job in enumerate(jobs[1:]):
            side = jnp.where(i // steps > index, job[0], side)
        return (0, (c[0] + side - 2 * c[0] * side) * steps + i % steps)

    def out_at(index):
        return lambda i, c: (0, jnp.minimum(jnp.maximum(i - index * steps, 0), steps - 1))

    out_specs, out_shape = [], []
    for index, (_, groups) in enumerate(jobs):
        for group in groups:
            out_specs.append(pl.BlockSpec((len(group) * line_rows, block), out_at(index)))
            out_shape.append(jax.ShapeDtypeStruct((len(group) * line_rows, half), jnp.bfloat16))
    return pl.pallas_call(
        functools.partial(down_body, line_rows, jobs),
        grid_spec=pltpu.PrefetchScalarGridSpec(
            num_scalar_prefetch=1,
            grid=(steps * len(jobs),),
            in_specs=[
                pl.BlockSpec((rows, hidden_units), lambda i, c: (0, 0)),
                pl.BlockSpec((hidden_units, block), weight_at),
                pl.BlockSpec((rows, LANES), lambda i, c: (0, 0)),
            ],
            out_specs=out_specs,
        ),
        out_shape=out_shape,
        compiler_params=pltpu.CompilerParams(
            dimension_semantics=("arbitrary",),
            vmem_limit_bytes=4 * (rows + block) * hidden_units + 24 * rows * block + (2 << 20),
        ),
        cost_estimate=pl.CostEstimate(flops=1 << 36, bytes_accessed=1 << 10, transcendentals=0),
        name="expert_down",
    )(spot, act, expert_out, scale)


def meta_body(route_ref, weight_ref, meta_ref):
    parts = []
    for step in range(STEPS):
        weight = weight_ref[step]
        top = weight.astype(jnp.bfloat16).astype(jnp.float32)
        middle = (weight - top).astype(jnp.bfloat16).astype(jnp.float32)
        parts += [route_ref[step].astype(jnp.float32), top, middle, weight - top - middle]
    value = jnp.concatenate(parts, axis=0).astype(jnp.bfloat16)
    shape = (value.shape[0], meta_ref.shape[1])
    rows = lax.broadcasted_iota(jnp.int32, shape, 0)
    lanes = lax.broadcasted_iota(jnp.int32, shape, 1)
    spots = (rows == lanes).astype(jnp.bfloat16)
    turned = lax.dot_general(
        value, spots, (((0,), (0,)), ((), ())), preferred_element_type=jnp.float32
    )
    meta_ref[...] = turned.astype(jnp.bfloat16)


def meta_columns(routes, weights):
    return pl.pallas_call(
        meta_body,
        out_shape=jax.ShapeDtypeStruct((routes.shape[2], LANES), jnp.bfloat16),
        name="meta_columns",
    )(routes, weights)


def pick_body(swapped_ref, cache_ref, first_ref, second_ref, info_ref, sems):
    row_count = swapped_ref.shape[0]
    for index in range(MOVE):
        info_ref[index] = 0

    def find(slot, count):
        @pl.when((swapped_ref[slot] == 1) & (count < MOVE))
        def _():
            info_ref[count] = slot

        return count + swapped_ref[slot]

    count = jnp.minimum(lax.fori_loop(0, row_count, find, jnp.int32(0)), MOVE)
    last = jnp.maximum(count - 1, 0)
    last_slot = info_ref[last]
    copies = []
    for index in range(MOVE):
        slot = jnp.where(index < count, info_ref[index], last_slot)
        info_ref[index] = slot
        info_ref[MOVE + index] = jnp.where(count > 0, jnp.minimum(index, last), -1)
        out_ref = first_ref if index < MOVE // 2 else second_ref
        copies.append(
            pltpu.make_async_copy(
                cache_ref.at[slot], out_ref.at[index % (MOVE // 2)], sems.at[index]
            )
        )
        copies[-1].start()
    for copy in copies:
        copy.wait()


def pick_caches(swapped, cache):
    part = jax.ShapeDtypeStruct((MOVE // 2,) + cache.shape[1:], cache.dtype)
    return pl.pallas_call(
        pick_body,
        grid_spec=pltpu.PrefetchScalarGridSpec(
            num_scalar_prefetch=1,
            grid=(1,),
            in_specs=[pl.BlockSpec(memory_space=pl.ANY)],
            out_specs=[
                pl.BlockSpec(part.shape, lambda i, _: (0, 0, 0)),
                pl.BlockSpec(part.shape, lambda i, _: (0, 0, 0)),
                pl.BlockSpec(memory_space=pltpu.SMEM),
            ],
            scratch_shapes=[pltpu.SemaphoreType.DMA((MOVE,))],
        ),
        out_shape=[part, part, jax.ShapeDtypeStruct((2 * MOVE,), jnp.int32)],
        name="pick_caches",
    )(swapped, cache)


def attend_one(query, cache, fresh, length):
    fresh = fresh.astype(jnp.float32)
    scores = jnp.dot(query, cache, preferred_element_type=jnp.float32) * SOFTMAX_SCALE
    own = jnp.sum(query.astype(jnp.float32) * fresh, axis=1, keepdims=True) * SOFTMAX_SCALE
    positions = lax.broadcasted_iota(jnp.int32, scores.shape, 1)
    scores = jnp.where(positions < length, scores, -jnp.inf)
    top = jnp.maximum(jnp.max(scores, axis=1, keepdims=True), own)
    weights = jnp.exp(scores - top)
    own_weight = jnp.exp(own - top)
    summed = jnp.sum(weights, axis=1, keepdims=True) + own_weight
    blended = lax.dot_general(
        weights.astype(jnp.bfloat16),
        cache[:LATENT],
        (((1,), (1,)), ((), ())),
        preferred_element_type=jnp.float32,
    )
    own_rounded = own_weight.astype(jnp.bfloat16).astype(jnp.float32)
    blended = blended + own_rounded * fresh[:, :LATENT]
    return (blended / summed).astype(jnp.bfloat16)


def attend_body(group, spot_ref, length_ref, query_ref, cache_ref, fresh_ref, out_ref):
    count = group * pl.num_programs(0)
    first = spot_ref[1] * count + pl.program_id(0) * group
    for slot in range(group):
        out_ref[slot] = attend_one(
            query_ref[slot], cache_ref[slot], fresh_ref[slot], length_ref[first + slot]
        )


def attend(spot, lengths, queries, cache, fresh):
    count, heads, full = queries.shape
    positions = cache.shape[2]
    group = 4
    return pl.pallas_call(
        functools.partial(attend_body, group),
        grid_spec=pltpu.PrefetchScalarGridSpec(
            num_scalar_prefetch=2,
            grid=(count // group,),
            in_specs=[
                pl.BlockSpec((group, heads, full), lambda i, *_: (i, 0, 0)),
                pl.BlockSpec((group, full, positions), lambda i, *_: (i, 0, 0)),
                pl.BlockSpec((group, 1, full), lambda i, *_: (i, 0, 0)),
            ],
            out_specs=pl.BlockSpec((group, heads, LATENT), lambda i, *_: (i, 0, 0)),
        ),
        out_shape=jax.ShapeDtypeStruct((count, heads, LATENT), jnp.bfloat16),
        compiler_params=pltpu.CompilerParams(
            dimension_semantics=("arbitrary",), vmem_limit_bytes=12 << 20
        ),
        cost_estimate=pl.CostEstimate(
            flops=4 * count * heads * full * positions,
            bytes_accessed=2 * count * (heads * (full + LATENT) + full * positions),
            transcendentals=count * heads * positions,
        ),
        name="attend",
    )(spot, lengths, queries, cache, fresh)


def attend_moved_body(
    row_count, spot_ref, length_ref, info_ref, query_ref, cache_ref, came_a_ref, came_b_ref, fresh_ref, old_ref, out_ref
):
    del old_ref
    index = pl.program_id(0)
    place = info_ref[MOVE + index]
    total = length_ref.shape[0]
    row = spot_ref[1] * row_count + info_ref[index]
    row = jnp.where(place >= 0, lax.rem(row + total // 2, total), row)
    came = jnp.where(place < MOVE // 2, came_a_ref[...], came_b_ref[...])[0]
    cache = jnp.where(place >= 0, came, cache_ref[0])
    out_ref[0] = attend_one(query_ref[0], cache, fresh_ref[0], length_ref[row])


def attend_moved(spot, lengths, info, queries, cache, came_a, came_b, fresh, context):
    row_count, heads, full = queries.shape
    positions = cache.shape[2]
    part = MOVE // 2
    at_slot = lambda i, spot, lengths, info: (info[i], 0, 0)
    clip = lambda value: jnp.minimum(jnp.maximum(value, 0), part - 1)
    one = (1, full, positions)
    return pl.pallas_call(
        functools.partial(attend_moved_body, row_count),
        grid_spec=pltpu.PrefetchScalarGridSpec(
            num_scalar_prefetch=3,
            grid=(MOVE,),
            in_specs=[
                pl.BlockSpec((1, heads, full), at_slot),
                pl.BlockSpec(one, at_slot),
                pl.BlockSpec(one, lambda i, spot, lengths, info: (clip(info[MOVE + i]), 0, 0)),
                pl.BlockSpec(
                    one, lambda i, spot, lengths, info: (clip(info[MOVE + i] - part), 0, 0)
                ),
                pl.BlockSpec((1, 1, full), at_slot),
                pl.BlockSpec(memory_space=pl.ANY),
            ],
            out_specs=pl.BlockSpec((1, heads, LATENT), at_slot),
        ),
        out_shape=jax.ShapeDtypeStruct(context.shape, context.dtype),
        input_output_aliases={8: 0},
        compiler_params=pltpu.CompilerParams(
            dimension_semantics=("arbitrary",), vmem_limit_bytes=48 << 20
        ),
        cost_estimate=pl.CostEstimate(flops=1 << 36, bytes_accessed=1 << 10, transcendentals=0),
        name="attend_moved",
    )(spot, lengths, info, queries, cache, came_a, came_b, fresh, context)


def per_device(
    hidden,
    routes,
    route_weights,
    expert_in,
    expert_out,
    queries,
    fresh_key,
    latent_cache,
    lengths,
    swapped,
):
    dp_count, ep_count = lax.axis_size("dp"), lax.axis_size("ep")
    device_count = dp_count * ep_count
    token_count, width = hidden.shape[1], hidden.shape[2]
    half = width // 2
    me = lax.axis_index(AXES)
    core = me % 2
    dp_bits, ep_bits = dp_count.bit_length() - 1, ep_count.bit_length() - 1
    x_masks = [ep_count << bit for bit in range(dp_bits - Z_BITS)]
    z_unit = ep_count << (dp_bits - Z_BITS)
    y_masks = [1 << bit for bit in range(1, ep_bits)]
    z_steps = sorted(range(1, 1 << Z_BITS), key=lambda step: step < 1 << (Z_BITS - 1))
    z_masks = [z_unit * step for step in [0] + z_steps]
    orders = (x_masks + y_masks, y_masks + x_masks)
    level_masks = list(zip(*orders))
    line_count = 1 << len(level_masks)
    sibling = (1, 1)
    spot = jnp.stack([core, me]).astype(jnp.int32)

    meta = meta_columns(jnp.swapaxes(routes, 1, 2), jnp.swapaxes(route_weights, 1, 2))

    own_half = lax.dynamic_slice_in_dim(hidden, core * half, half, axis=2)
    other_half = lax.dynamic_slice_in_dim(hidden, (1 - core) * half, half, axis=2)
    came_half = exchange(other_half, sibling)
    by_core = lambda mine, theirs, axis: jnp.where(
        core == 0,
        jnp.concatenate([mine, theirs], axis=axis),
        jnp.concatenate([theirs, mine], axis=axis),
    )
    pair = by_core(own_half, came_half, 1)
    pair_meta = by_core(meta, jnp.zeros_like(meta), 0)
    line_rows = len(z_masks) * 2 * token_count

    window = lambda *values: lax.optimization_barrier(values)
    far = device_count // 2
    bottom, top_masks = level_masks[:-1], level_masks[-1]

    swap = lambda value: exchange(value, sibling)

    def send_line(block):
        return [exchange(block, (mask, mask)) for mask in z_masks[1:]]

    def spread(line):
        for masks in bottom:
            line = jnp.concatenate([line, exchange(line, masks)], axis=0)
        return line

    add = lambda terms: functools.reduce(
        lambda total, term: total + term, [term.astype(jnp.float32) for term in terms]
    )
    rounded_sum = lambda terms: add(terms).astype(jnp.bfloat16)
    up = lambda own, sib, with_meta: expert_up(
        spot, own, sib, expert_in[0], line_rows, with_meta
    )
    down = lambda act, scale, *jobs: expert_down(
        spot, act, expert_out[0], scale, line_rows, jobs
    )
    half_bits = len(level_masks) // 2
    my_lines = list(range(line_count))
    their_lines = [swap_halves(line, half_bits) for line in my_lines]
    split = line_count // 2
    halves_of = lambda terms: (
        [term[: term.shape[0] // 2] for term in terms],
        [term[term.shape[0] // 2 :] for term in terms],
    )

    def fold(terms):
        for masks in reversed(bottom):
            terms, high = halves_of(terms)
            terms = terms + [exchange(rounded_sum(high), masks)]
        return terms

    def finish_sends(terms):
        block = 2 * token_count
        at = lambda place: [term[place * block : (place + 1) * block] for term in terms]
        return at(0), [rounded_sum(at(place)) for place in range(1, len(z_masks))]

    def finish_line(sends):
        return [exchange(value, (mask, mask)) for value, mask in zip(sends, z_masks[1:])]

    def finish(terms):
        total = rounded_sum(terms).reshape(2, token_count, half)
        kept = lax.dynamic_index_in_dim(total, core, 0, keepdims=False)
        sent = lax.dynamic_index_in_dim(total, 1 - core, 0, keepdims=False)
        return by_core(kept, exchange(sent, sibling), 1)

    block0 = jnp.concatenate([pair[0], pair_meta], axis=1)
    block0, swapped = window(block0, swapped)

    fresh = fresh_key[:, None, :]
    stored = jnp.swapaxes(latent_cache, 1, 2)

    came0 = send_line(block0)
    *leaving, info = pick_caches(swapped, stored)
    *came0, leave_a, leave_b, info = window(*came0, *leaving, info)

    low0 = spread(jnp.concatenate([block0] + came0, axis=0))
    low0, block1, early_queries = window(low0, pair[1], queries)

    high0 = exchange(low0, top_masks)
    sib_low0 = exchange(low0, sibling)
    came1 = send_line(block1)
    context = attend(spot, lengths, early_queries, stored, fresh)
    high0, sib_low0, context, *came1 = window(high0, sib_low0, context, *came1)

    line1 = jnp.concatenate([block1] + came1, axis=0)
    sib_high0 = exchange(high0, sibling)
    low0, high0, sib_low0, sib_high0, line1, leave_a = window(
        low0, high0, sib_low0, sib_high0, line1, leave_a
    )

    low1 = [line1]
    for masks in bottom:
        low1 = low1 + [exchange(line, masks) for line in low1]
    first1 = exchange(line1, top_masks)
    cache_a = exchange(leave_a, (far, far))
    act0, scale0, scale1 = up([low0, high0], [sib_low0, sib_high0], True)
    first1, cache_a, act0, scale0, scale1, *low1 = window(
        first1, cache_a, act0, scale0, scale1, *low1
    )

    rest1 = [exchange(line, top_masks) for line in low1[1:]]
    sib_low1 = [swap(line) for line in low1]
    sib_first1 = swap(first1)
    they_low0, they_high0 = down(act0, scale0, (1, (their_lines[:split], their_lines[split:])))
    they_low0, they_high0 = swap(they_low0), swap(they_high0)
    my_low0, my_high0 = down(act0, scale0, (0, (my_lines[:split], my_lines[split:])))
    sib_first1, they_low0, they_high0, my_low0, my_high0, *flat = window(
        sib_first1, they_low0, they_high0, my_low0, my_high0, *sib_low1, *rest1
    )
    sib_low1, rest1 = flat[:split], flat[split:]

    send0 = rounded_sum([my_high0, they_high0])
    sib_rest1 = [swap(line) for line in rest1]
    send0, leave_b, *sib_rest1 = window(send0, leave_b, *sib_rest1)

    came = exchange(send0, top_masks)
    cache_b = exchange(leave_b, (far, far))
    (act1,) = up(low1 + [first1] + rest1, sib_low1 + [sib_first1] + sib_rest1, False)
    came, act1, cache_b = window(came, act1, cache_b)

    they_high1, my_high1 = down(
        act1, scale1, (1, (their_lines[split:],)), (0, (my_lines[split:],))
    )
    terms0 = [my_low0, they_low0, came]
    for masks in reversed(bottom):
        terms0, high = halves_of(terms0)
        high, my_high1 = window(rounded_sum(high), my_high1)
        terms0 = terms0 + [exchange(high, masks)]

    they_high1 = exchange(they_high1, sibling)
    send1 = rounded_sum([my_high1, they_high1])
    send1, act1 = window(send1, act1)
    came = exchange(send1, top_masks)
    they_low1, my_low1 = down(
        act1, scale1, (1, (their_lines[:split],)), (0, (my_lines[:split],))
    )
    they_low1 = exchange(they_low1, sibling)
    kept0, sends0 = finish_sends(terms0)
    last0 = finish_line(sends0)
    came, my_low1 = window(came, my_low1)

    terms1 = [my_low1, they_low1, came]
    for masks in reversed(bottom):
        terms1, high = halves_of(terms1)
        high, queries = window(rounded_sum(high), queries)
        terms1 = terms1 + [exchange(high, masks)]
    context = attend_moved(
        spot, lengths, info, queries, stored, cache_a, cache_b, fresh, context
    )
    terms1[-1], context, *last0 = window(terms1[-1], context, *last0)
    kept1, sends1 = finish_sends(terms1)
    last1 = finish_line(sends1)
    mixed0 = finish(kept0 + last0)
    mixed1 = finish(kept1 + last1)
    return (jnp.stack([mixed0, mixed1]), context)


def solution(mesh):
    in_specs = (
        P(None, ("dp", "ep"), None),
        P(None, ("dp", "ep"), None),
        P(None, ("dp", "ep"), None),
        P(("dp", "ep"), None, None),
        P(("dp", "ep"), None, None),
        P(("dp", "ep"), None, None),
        P(("dp", "ep"), None),
        P(("dp", "ep"), None, None),
        P(),
        P(("dp", "ep")),
    )
    out_specs = (P(None, ("dp", "ep"), None), P(("dp", "ep"), None, None))
    return jax.shard_map(
        per_device, mesh=mesh, in_specs=in_specs, out_specs=out_specs, check_vma=False
    )
```

```python
import functools

import jax
import jax.numpy as jnp
from jax import lax
from jax.experimental import pallas as pl
from jax.experimental.pallas import tpu as pltpu
from jax.sharding import PartitionSpec as P

AXES = ("dp", "ep")
LATENT = 512
STEPS = 2
MOVE = 4
LANES = 128
META_PICKS = 8
Z_BITS = 2

SOFTMAX_SCALE = 192.0 ** (-0.5)


def exchange(value, masks):
    count = lax.axis_size(AXES)
    pairs = [(source, source ^ masks[source % 2]) for source in range(count)]
    return lax.ppermute(value, AXES, pairs)


def swap_halves(index, bits):
    low = index & ((1 << bits) - 1)
    return (low << bits) | (index >> bits)


def up_body(line_rows, piece_counts, with_meta, block, spot_ref, *refs):
    refs = list(refs)
    own = [refs.pop(0) for _ in piece_counts]
    sib = [refs.pop(0) for _ in piece_counts]
    weight_ref, act_ref = refs.pop(0), refs.pop(0)
    scale_refs = [refs.pop(0) for _ in range(STEPS if with_meta else 0)]
    own_rows, sib_rows, weights, act, row_sems, weight_sems, act_sems = refs
    line_count = sum(piece_counts)
    half_bits = (line_count.bit_length() - 1) // 2
    half = weight_ref.shape[0] // 2
    hidden_units = weight_ref.shape[1] // 2
    steps = hidden_units // block
    core = spot_ref[0]

    def row_copies(side):
        made = []
        line = 0
        for piece, count in zip(sib if side else own, piece_counts):
            for index in range(count):
                place = swap_halves(line, half_bits) if side else line
                made.append(
                    pltpu.make_async_copy(
                        piece.at[pl.ds(index * line_rows, line_rows)],
                        (sib_rows if side else own_rows).at[pl.ds(place * line_rows, line_rows)],
                        row_sems.at[side, line],
                    )
                )
                line += 1
        return made

    def weight_copies(step, side):
        first = pl.multiple_of((1 - core if side else core) * half, half)
        return [
            pltpu.make_async_copy(
                weight_ref.at[
                    pl.ds(first, half),
                    pl.ds(pl.multiple_of(part * hidden_units + step * block, block), block),
                ],
                weights.at[step % 2, 2 * side + part],
                weight_sems.at[step % 2, 2 * side + part],
            )
            for part in range(2)
        ]

    def act_copy(step):
        columns = pl.ds(pl.multiple_of(step * block, block), block)
        return pltpu.make_async_copy(act.at[:, columns], act_ref.at[:, columns], act_sems.at[step])

    def start(copies):
        for copy in copies:
            copy.start()

    def wait(copies):
        for copy in copies:
            copy.wait()

    for side in range(2):
        start(row_copies(side) + weight_copies(0, side))

    @pl.loop(0, steps)
    def _(step):
        slot = step % 2

        @pl.when(step == 0)
        def _():
            wait(row_copies(0))

        wait(weight_copies(step, 0))

        @pl.when(step + 1 < steps)
        def _():
            start(weight_copies(step + 1, 0) + weight_copies(step + 1, 1))

        own_value = own_rows[:, :half]
        gate = jnp.dot(own_value, weights[slot, 0], preferred_element_type=jnp.float32)
        up = jnp.dot(own_value, weights[slot, 1], preferred_element_type=jnp.float32)

        @pl.when(step == 0)
        def _():
            wait(row_copies(1))

        wait(weight_copies(step, 1))
        sib_value = sib_rows[:, :half]
        gate += jnp.dot(sib_value, weights[slot, 2], preferred_element_type=jnp.float32)
        up += jnp.dot(sib_value, weights[slot, 3], preferred_element_type=jnp.float32)
        value = (gate / (1.0 + jnp.exp(-gate)) * up).astype(jnp.bfloat16)
        act[:, pl.ds(pl.multiple_of(step * block, block), block)] = value
        act_copy(step).start()

    if with_meta:
        meta = own_rows[:, half:].astype(jnp.float32) + sib_rows[:, half:].astype(jnp.float32)
        me = spot_ref[1].astype(jnp.float32)
        lanes = lax.broadcasted_iota(jnp.int32, meta.shape, 1)
        for step, scale_ref in enumerate(scale_refs):
            base = step * 4 * META_PICKS
            value = jnp.zeros_like(meta)
            for part in range(1, 4):
                low = base + part * META_PICKS
                named = pltpu.roll(meta, part * META_PICKS, 1) == me
                inside = (lanes >= low) & (lanes < low + META_PICKS)
                value = value + jnp.where(named & inside, meta, 0.0)
            total = jnp.sum(value, axis=1, keepdims=True)
            scale_ref[...] = jnp.broadcast_to(total, scale_ref.shape)
    for step in range(steps):
        act_copy(step).wait()


def expert_up(spot, own_pieces, sib_pieces, expert_in, line_rows, with_meta):
    piece_counts = [piece.shape[0] // line_rows for piece in own_pieces]
    wide = own_pieces[0].shape[1]
    half = expert_in.shape[0] // 2
    hidden_units = expert_in.shape[1] // 2
    rows = sum(piece_counts) * line_rows
    block = 256
    out_specs = [pl.BlockSpec(memory_space=pl.ANY)]
    out_shape = [jax.ShapeDtypeStruct((rows, hidden_units), jnp.bfloat16)]
    if with_meta:
        out_specs += [pl.BlockSpec((rows, LANES), lambda i, c: (0, 0))] * STEPS
        out_shape += [jax.ShapeDtypeStruct((rows, LANES), jnp.float32)] * STEPS
    held = 2 * rows * (2 * wide + hidden_units) + 16 * half * block
    return pl.pallas_call(
        functools.partial(up_body, line_rows, piece_counts, with_meta, block),
        grid_spec=pltpu.PrefetchScalarGridSpec(
            num_scalar_prefetch=1,
            grid=(1,),
            in_specs=[pl.BlockSpec(memory_space=pl.ANY)] * (2 * len(own_pieces) + 1),
            out_specs=out_specs,
            scratch_shapes=[
                pltpu.VMEM((rows, wide), jnp.bfloat16),
                pltpu.VMEM((rows, wide), jnp.bfloat16),
                pltpu.VMEM((2, 4, half, block), jnp.bfloat16),
                pltpu.VMEM((rows, hidden_units), jnp.bfloat16),
                pltpu.SemaphoreType.DMA((2, sum(piece_counts))),
                pltpu.SemaphoreType.DMA((2, 4)),
                pltpu.SemaphoreType.DMA((hidden_units // block,)),
            ],
        ),
        out_shape=out_shape,
        compiler_params=pltpu.CompilerParams(
            dimension_semantics=("arbitrary",), vmem_limit_bytes=max(47 << 20, held + 24 * rows * block + (4 << 20))
        ),
        cost_estimate=pl.CostEstimate(
            flops=8 * rows * half * hidden_units,
            bytes_accessed=8 * half * hidden_units + 4 * rows * wide + 2 * rows * hidden_units,
            transcendentals=rows * hidden_units,
        ),
        name="expert_up",
    )(spot, *own_pieces, *sib_pieces, expert_in)


def down_body(line_rows, jobs, spot_ref, act_ref, down_ref, scale_ref, *outs):
    del spot_ref
    per_job = pl.num_programs(0) // len(jobs)

    def run(groups, outs):
        lines = [line for group in groups for line in group]
        at = lambda ref: jnp.concatenate(
            [ref[line * line_rows : (line + 1) * line_rows] for line in lines], axis=0
        )
        answer = jnp.dot(at(act_ref), down_ref[...], preferred_element_type=jnp.float32)
        scale = at(scale_ref)
        for column in range(0, answer.shape[1], LANES):
            value = answer[:, column : column + LANES].astype(jnp.bfloat16).astype(jnp.float32)
            value = (value * scale).astype(jnp.bfloat16)
            first = 0
            for group, out in zip(groups, outs):
                rows = len(group) * line_rows
                out[:, column : column + LANES] = value[first : first + rows]
                first += rows

    first = 0
    for index, (_, groups) in enumerate(jobs):
        mine = outs[first : first + len(groups)]
        first += len(groups)
        if len(jobs) == 1:
            run(groups, mine)
        else:
            pl.when(pl.program_id(0) // per_job == index)(functools.partial(run, groups, mine))


def expert_down(spot, act, expert_out, scale, line_rows, jobs):
    rows, hidden_units = act.shape
    half = expert_out.shape[1] // 2
    block = 896
    steps = half // block

    def weight_at(i, c):
        side = jobs[0][0]
        for index, job in enumerate(jobs[1:]):
            side = jnp.where(i // steps > index, job[0], side)
        return (0, (c[0] + side - 2 * c[0] * side) * steps + i % steps)

    def out_at(index):
        return lambda i, c: (0, jnp.minimum(jnp.maximum(i - index * steps, 0), steps - 1))

    out_specs, out_shape = [], []
    for index, (_, groups) in enumerate(jobs):
        for group in groups:
            out_specs.append(pl.BlockSpec((len(group) * line_rows, block), out_at(index)))
            out_shape.append(jax.ShapeDtypeStruct((len(group) * line_rows, half), jnp.bfloat16))
    return pl.pallas_call(
        functools.partial(down_body, line_rows, jobs),
        grid_spec=pltpu.PrefetchScalarGridSpec(
            num_scalar_prefetch=1,
            grid=(steps * len(jobs),),
            in_specs=[
                pl.BlockSpec((rows, hidden_units), lambda i, c: (0, 0)),
                pl.BlockSpec((hidden_units, block), weight_at),
                pl.BlockSpec((rows, LANES), lambda i, c: (0, 0)),
            ],
            out_specs=out_specs,
        ),
        out_shape=out_shape,
        compiler_params=pltpu.CompilerParams(
            dimension_semantics=("arbitrary",),
            vmem_limit_bytes=4 * (rows + block) * hidden_units + 24 * rows * block + (2 << 20),
        ),
        cost_estimate=pl.CostEstimate(flops=1 << 36, bytes_accessed=1 << 10, transcendentals=0),
        name="expert_down",
    )(spot, act, expert_out, scale)


def meta_body(route_ref, weight_ref, meta_ref):
    parts = []
    for step in range(STEPS):
        weight = weight_ref[step]
        top = weight.astype(jnp.bfloat16).astype(jnp.float32)
        middle = (weight - top).astype(jnp.bfloat16).astype(jnp.float32)
        parts += [route_ref[step].astype(jnp.float32), top, middle, weight - top - middle]
    value = jnp.concatenate(parts, axis=0).astype(jnp.bfloat16)
    shape = (value.shape[0], meta_ref.shape[1])
    rows = lax.broadcasted_iota(jnp.int32, shape, 0)
    lanes = lax.broadcasted_iota(jnp.int32, shape, 1)
    spots = (rows == lanes).astype(jnp.bfloat16)
    turned = lax.dot_general(
        value, spots, (((0,), (0,)), ((), ())), preferred_element_type=jnp.float32
    )
    meta_ref[...] = turned.astype(jnp.bfloat16)


def meta_columns(routes, weights):
    return pl.pallas_call(
        meta_body,
        out_shape=jax.ShapeDtypeStruct((routes.shape[2], LANES), jnp.bfloat16),
        name="meta_columns",
    )(routes, weights)


def pick_body(swapped_ref, cache_ref, first_ref, second_ref, info_ref, sems):
    row_count = swapped_ref.shape[0]
    for index in range(MOVE):
        info_ref[index] = 0

    def find(slot, count):
        @pl.when((swapped_ref[slot] == 1) & (count < MOVE))
        def _():
            info_ref[count] = slot

        return count + swapped_ref[slot]

    count = jnp.minimum(lax.fori_loop(0, row_count, find, jnp.int32(0)), MOVE)
    last = jnp.maximum(count - 1, 0)
    last_slot = info_ref[last]
    copies = []
    for index in range(MOVE):
        slot = jnp.where(index < count, info_ref[index], last_slot)
        info_ref[index] = slot
        info_ref[MOVE + index] = jnp.where(count > 0, jnp.minimum(index, last), -1)
        out_ref = first_ref if index < MOVE // 2 else second_ref
        copies.append(
            pltpu.make_async_copy(
                cache_ref.at[slot], out_ref.at[index % (MOVE // 2)], sems.at[index]
            )
        )
        copies[-1].start()
    for copy in copies:
        copy.wait()


def pick_caches(swapped, cache):
    part = jax.ShapeDtypeStruct((MOVE // 2,) + cache.shape[1:], cache.dtype)
    return pl.pallas_call(
        pick_body,
        grid_spec=pltpu.PrefetchScalarGridSpec(
            num_scalar_prefetch=1,
            grid=(1,),
            in_specs=[pl.BlockSpec(memory_space=pl.ANY)],
            out_specs=[
                pl.BlockSpec(part.shape, lambda i, _: (0, 0, 0)),
                pl.BlockSpec(part.shape, lambda i, _: (0, 0, 0)),
                pl.BlockSpec(memory_space=pltpu.SMEM),
            ],
            scratch_shapes=[pltpu.SemaphoreType.DMA((MOVE,))],
        ),
        out_shape=[part, part, jax.ShapeDtypeStruct((2 * MOVE,), jnp.int32)],
        name="pick_caches",
    )(swapped, cache)


def attend_one(query, cache, fresh, length):
    fresh = fresh.astype(jnp.float32)
    scores = jnp.dot(query, cache, preferred_element_type=jnp.float32) * SOFTMAX_SCALE
    own = jnp.sum(query.astype(jnp.float32) * fresh, axis=1, keepdims=True) * SOFTMAX_SCALE
    positions = lax.broadcasted_iota(jnp.int32, scores.shape, 1)
    scores = jnp.where(positions < length, scores, -jnp.inf)
    top = jnp.maximum(jnp.max(scores, axis=1, keepdims=True), own)
    weights = jnp.exp(scores - top)
    own_weight = jnp.exp(own - top)
    summed = jnp.sum(weights, axis=1, keepdims=True) + own_weight
    blended = lax.dot_general(
        weights.astype(jnp.bfloat16),
        cache[:LATENT],
        (((1,), (1,)), ((), ())),
        preferred_element_type=jnp.float32,
    )
    own_rounded = own_weight.astype(jnp.bfloat16).astype(jnp.float32)
    blended = blended + own_rounded * fresh[:, :LATENT]
    return (blended / summed).astype(jnp.bfloat16)


def attend_body(group, spot_ref, length_ref, query_ref, cache_ref, fresh_ref, out_ref):
    count = group * pl.num_programs(0)
    first = spot_ref[1] * count + pl.program_id(0) * group
    for slot in range(group):
        out_ref[slot] = attend_one(
            query_ref[slot], cache_ref[slot], fresh_ref[slot], length_ref[first + slot]
        )


def attend(spot, lengths, queries, cache, fresh):
    count, heads, full = queries.shape
    positions = cache.shape[2]
    group = 4
    return pl.pallas_call(
        functools.partial(attend_body, group),
        grid_spec=pltpu.PrefetchScalarGridSpec(
            num_scalar_prefetch=2,
            grid=(count // group,),
            in_specs=[
                pl.BlockSpec((group, heads, full), lambda i, *_: (i, 0, 0)),
                pl.BlockSpec((group, full, positions), lambda i, *_: (i, 0, 0)),
                pl.BlockSpec((group, 1, full), lambda i, *_: (i, 0, 0)),
            ],
            out_specs=pl.BlockSpec((group, heads, LATENT), lambda i, *_: (i, 0, 0)),
        ),
        out_shape=jax.ShapeDtypeStruct((count, heads, LATENT), jnp.bfloat16),
        compiler_params=pltpu.CompilerParams(
            dimension_semantics=("arbitrary",), vmem_limit_bytes=12 << 20
        ),
        cost_estimate=pl.CostEstimate(
            flops=4 * count * heads * full * positions,
            bytes_accessed=2 * count * (heads * (full + LATENT) + full * positions),
            transcendentals=count * heads * positions,
        ),
        name="attend",
    )(spot, lengths, queries, cache, fresh)


def attend_moved_body(
    row_count, spot_ref, length_ref, info_ref, query_ref, cache_ref, came_a_ref, came_b_ref, fresh_ref, old_ref, out_ref
):
    del old_ref
    index = pl.program_id(0)
    place = info_ref[MOVE + index]
    total = length_ref.shape[0]
    row = spot_ref[1] * row_count + info_ref[index]
    row = jnp.where(place >= 0, lax.rem(row + total // 2, total), row)
    came = jnp.where(place < MOVE // 2, came_a_ref[...], came_b_ref[...])[0]
    cache = jnp.where(place >= 0, came, cache_ref[0])
    out_ref[0] = attend_one(query_ref[0], cache, fresh_ref[0], length_ref[row])


def attend_moved(spot, lengths, info, queries, cache, came_a, came_b, fresh, context):
    row_count, heads, full = queries.shape
    positions = cache.shape[2]
    part = MOVE // 2
    at_slot = lambda i, spot, lengths, info: (info[i], 0, 0)
    clip = lambda value: jnp.minimum(jnp.maximum(value, 0), part - 1)
    one = (1, full, positions)
    return pl.pallas_call(
        functools.partial(attend_moved_body, row_count),
        grid_spec=pltpu.PrefetchScalarGridSpec(
            num_scalar_prefetch=3,
            grid=(MOVE,),
            in_specs=[
                pl.BlockSpec((1, heads, full), at_slot),
                pl.BlockSpec(one, at_slot),
                pl.BlockSpec(one, lambda i, spot, lengths, info: (clip(info[MOVE + i]), 0, 0)),
                pl.BlockSpec(
                    one, lambda i, spot, lengths, info: (clip(info[MOVE + i] - part), 0, 0)
                ),
                pl.BlockSpec((1, 1, full), at_slot),
                pl.BlockSpec(memory_space=pl.ANY),
            ],
            out_specs=pl.BlockSpec((1, heads, LATENT), at_slot),
        ),
        out_shape=jax.ShapeDtypeStruct(context.shape, context.dtype),
        input_output_aliases={8: 0},
        compiler_params=pltpu.CompilerParams(
            dimension_semantics=("arbitrary",), vmem_limit_bytes=48 << 20
        ),
        cost_estimate=pl.CostEstimate(flops=1 << 36, bytes_accessed=1 << 10, transcendentals=0),
        name="attend_moved",
    )(spot, lengths, info, queries, cache, came_a, came_b, fresh, context)


def per_device(
    hidden,
    routes,
    route_weights,
    expert_in,
    expert_out,
    queries,
    fresh_key,
    latent_cache,
    lengths,
    swapped,
):
    dp_count, ep_count = lax.axis_size("dp"), lax.axis_size("ep")
    device_count = dp_count * ep_count
    token_count, width = hidden.shape[1], hidden.shape[2]
    half = width // 2
    me = lax.axis_index(AXES)
    core = me % 2
    dp_bits, ep_bits = dp_count.bit_length() - 1, ep_count.bit_length() - 1
    x_masks = [ep_count << bit for bit in range(dp_bits - Z_BITS)]
    z_unit = ep_count << (dp_bits - Z_BITS)
    y_masks = [1 << bit for bit in range(1, ep_bits)]
    z_steps = sorted(range(1, 1 << Z_BITS), key=lambda step: step < 1 << (Z_BITS - 1))
    z_masks = [z_unit * step for step in [0] + z_steps]
    orders = (x_masks + y_masks, y_masks + x_masks)
    level_masks = list(zip(*orders))
    line_count = 1 << len(level_masks)
    sibling = (1, 1)
    spot = jnp.stack([core, me]).astype(jnp.int32)

    meta = meta_columns(jnp.swapaxes(routes, 1, 2), jnp.swapaxes(route_weights, 1, 2))

    own_half = lax.dynamic_slice_in_dim(hidden, core * half, half, axis=2)
    other_half = lax.dynamic_slice_in_dim(hidden, (1 - core) * half, half, axis=2)
    came_half = exchange(other_half, sibling)
    by_core = lambda mine, theirs, axis: jnp.where(
        core == 0,
        jnp.concatenate([mine, theirs], axis=axis),
        jnp.concatenate([theirs, mine], axis=axis),
    )
    pair = by_core(own_half, came_half, 1)
    pair_meta = by_core(meta, jnp.zeros_like(meta), 0)
    line_rows = len(z_masks) * 2 * token_count

    window = lambda *values: lax.optimization_barrier(values)
    far = device_count // 2
    bottom, top_masks = level_masks[:-1], level_masks[-1]

    swap = lambda value: exchange(value, sibling)

    def send_line(block):
        return [exchange(block, (mask, mask)) for mask in z_masks[1:]]

    def spread(line):
        for masks in bottom:
            line = jnp.concatenate([line, exchange(line, masks)], axis=0)
        return line

    add = lambda terms: functools.reduce(
        lambda total, term: total + term, [term.astype(jnp.float32) for term in terms]
    )
    rounded_sum = lambda terms: add(terms).astype(jnp.bfloat16)
    up = lambda own, sib, with_meta: expert_up(
        spot, own, sib, expert_in[0], line_rows, with_meta
    )
    down = lambda act, scale, *jobs: expert_down(
        spot, act, expert_out[0], scale, line_rows, jobs
    )
    half_bits = len(level_masks) // 2
    my_lines = list(range(line_count))
    their_lines = [swap_halves(line, half_bits) for line in my_lines]
    split = line_count // 2
    halves_of = lambda terms: (
        [term[: term.shape[0] // 2] for term in terms],
        [term[term.shape[0] // 2 :] for term in terms],
    )

    def fold(terms):
        for masks in reversed(bottom):
            terms, high = halves_of(terms)
            terms = terms + [exchange(rounded_sum(high), masks)]
        return terms

    def finish_sends(terms):
        block = 2 * token_count
        at = lambda place: [term[place * block : (place + 1) * block] for term in terms]
        return at(0), [rounded_sum(at(place)) for place in range(1, len(z_masks))]

    def finish_line(sends):
        return [exchange(value, (mask, mask)) for value, mask in zip(sends, z_masks[1:])]

    def finish(terms):
        total = rounded_sum(terms).reshape(2, token_count, half)
        kept = lax.dynamic_index_in_dim(total, core, 0, keepdims=False)
        sent = lax.dynamic_index_in_dim(total, 1 - core, 0, keepdims=False)
        return by_core(kept, exchange(sent, sibling), 1)

    block0 = jnp.concatenate([pair[0], pair_meta], axis=1)
    block0, swapped = window(block0, swapped)

    fresh = fresh_key[:, None, :]
    stored = jnp.swapaxes(latent_cache, 1, 2)

    came0 = send_line(block0)
    *leaving, info = pick_caches(swapped, stored)
    *came0, leave_a, leave_b, info = window(*came0, *leaving, info)

    low0 = spread(jnp.concatenate([block0] + came0, axis=0))
    low0, block1, early_queries = window(low0, pair[1], queries)

    high0 = exchange(low0, top_masks)
    sib_low0 = exchange(low0, sibling)
    came1 = send_line(block1)
    context = attend(spot, lengths, early_queries, stored, fresh)
    high0, sib_low0, context, *came1 = window(high0, sib_low0, context, *came1)

    line1 = jnp.concatenate([block1] + came1, axis=0)
    low0, high0, sib_low0, line1, leave_a = window(low0, high0, sib_low0, line1, leave_a)
    sib_high0 = exchange(high0, sibling)

    low1 = [line1]
    for masks in bottom:
        low1 = low1 + [exchange(line, masks) for line in low1]
    first1 = exchange(line1, top_masks)
    cache_a = exchange(leave_a, (far, far))
    act0, scale0, scale1 = up([low0, high0], [sib_low0, sib_high0], True)
    first1, cache_a, act0, scale0, scale1, *low1 = window(
        first1, cache_a, act0, scale0, scale1, *low1
    )

    rest1 = [exchange(line, top_masks) for line in low1[1:]]
    sib_low1 = [swap(line) for line in low1]
    sib_first1 = swap(first1)
    they_low0, they_high0 = down(act0, scale0, (1, (their_lines[:split], their_lines[split:])))
    they_low0, they_high0 = swap(they_low0), swap(they_high0)
    my_low0, my_high0 = down(act0, scale0, (0, (my_lines[:split], my_lines[split:])))
    sib_first1, they_low0, they_high0, my_low0, my_high0, *flat = window(
        sib_first1, they_low0, they_high0, my_low0, my_high0, *sib_low1, *rest1
    )
    sib_low1, rest1 = flat[:split], flat[split:]

    send0 = rounded_sum([my_high0, they_high0])
    send0, leave_b, *rest1 = window(send0, leave_b, *rest1)
    sib_rest1 = [swap(line) for line in rest1]

    came = exchange(send0, top_masks)
    cache_b = exchange(leave_b, (far, far))
    (act1,) = up(low1 + [first1] + rest1, sib_low1 + [sib_first1] + sib_rest1, False)
    came, act1, cache_b = window(came, act1, cache_b)

    they_high1, my_high1 = down(
        act1, scale1, (1, (their_lines[split:],)), (0, (my_lines[split:],))
    )
    terms0 = [my_low0, they_low0, came]
    for masks in reversed(bottom):
        terms0, high = halves_of(terms0)
        high, my_high1 = window(rounded_sum(high), my_high1)
        terms0 = terms0 + [exchange(high, masks)]

    they_high1 = exchange(they_high1, sibling)
    send1 = rounded_sum([my_high1, they_high1])
    send1, act1 = window(send1, act1)
    came = exchange(send1, top_masks)
    they_low1, my_low1 = down(
        act1, scale1, (1, (their_lines[:split],)), (0, (my_lines[:split],))
    )
    they_low1 = exchange(they_low1, sibling)
    kept0, sends0 = finish_sends(terms0)
    last0 = finish_line(sends0)
    came, my_low1 = window(came, my_low1)

    terms1 = [my_low1, they_low1, came]
    for masks in reversed(bottom):
        terms1, high = halves_of(terms1)
        high, queries = window(rounded_sum(high), queries)
        terms1 = terms1 + [exchange(high, masks)]
    context = attend_moved(
        spot, lengths, info, queries, stored, cache_a, cache_b, fresh, context
    )
    terms1[-1], context, *last0 = window(terms1[-1], context, *last0)
    kept1, sends1 = finish_sends(terms1)
    last1 = finish_line(sends1)
    mixed0 = finish(kept0 + last0)
    mixed1 = finish(kept1 + last1)
    return (jnp.stack([mixed0, mixed1]), context)


def solution(mesh):
    in_specs = (
        P(None, ("dp", "ep"), None),
        P(None, ("dp", "ep"), None),
        P(None, ("dp", "ep"), None),
        P(("dp", "ep"), None, None),
        P(("dp", "ep"), None, None),
        P(("dp", "ep"), None, None),
        P(("dp", "ep"), None),
        P(("dp", "ep"), None, None),
        P(),
        P(("dp", "ep")),
    )
    out_specs = (P(None, ("dp", "ep"), None), P(("dp", "ep"), None, None))
    return jax.shard_map(
        per_device, mesh=mesh, in_specs=in_specs, out_specs=out_specs, check_vma=False
    )
```

```python
import functools

import jax
import jax.numpy as jnp
from jax import lax
from jax.experimental import pallas as pl
from jax.experimental.pallas import tpu as pltpu
from jax.sharding import PartitionSpec as P

AXES = ("dp", "ep")
LATENT = 512
STEPS = 2
MOVE = 4
LANES = 128
META_PICKS = 8
Z_BITS = 2

SOFTMAX_SCALE = 192.0 ** (-0.5)


def exchange(value, masks):
    count = lax.axis_size(AXES)
    pairs = [(source, source ^ masks[source % 2]) for source in range(count)]
    return lax.ppermute(value, AXES, pairs)


def swap_halves(index, bits):
    low = index & ((1 << bits) - 1)
    return (low << bits) | (index >> bits)


def up_body(line_rows, piece_counts, with_meta, block, spot_ref, *refs):
    refs = list(refs)
    own = [refs.pop(0) for _ in piece_counts]
    sib = [refs.pop(0) for _ in piece_counts]
    weight_ref, act_ref = refs.pop(0), refs.pop(0)
    scale_refs = [refs.pop(0) for _ in range(STEPS if with_meta else 0)]
    own_rows, sib_rows, weights, act, row_sems, weight_sems, act_sems = refs
    line_count = sum(piece_counts)
    half_bits = (line_count.bit_length() - 1) // 2
    half = weight_ref.shape[0] // 2
    hidden_units = weight_ref.shape[1] // 2
    steps = hidden_units // block
    core = spot_ref[0]

    def row_copies(side):
        made = []
        line = 0
        for piece, count in zip(sib if side else own, piece_counts):
            for index in range(count):
                place = swap_halves(line, half_bits) if side else line
                made.append(
                    pltpu.make_async_copy(
                        piece.at[pl.ds(index * line_rows, line_rows)],
                        (sib_rows if side else own_rows).at[pl.ds(place * line_rows, line_rows)],
                        row_sems.at[side, line],
                    )
                )
                line += 1
        return made

    def weight_copies(step, side):
        first = pl.multiple_of((1 - core if side else core) * half, half)
        return [
            pltpu.make_async_copy(
                weight_ref.at[
                    pl.ds(first, half),
                    pl.ds(pl.multiple_of(part * hidden_units + step * block, block), block),
                ],
                weights.at[step % 2, 2 * side + part],
                weight_sems.at[step % 2, 2 * side + part],
            )
            for part in range(2)
        ]

    def act_copy(step):
        columns = pl.ds(pl.multiple_of(step * block, block), block)
        return pltpu.make_async_copy(act.at[:, columns], act_ref.at[:, columns], act_sems.at[step])

    def start(copies):
        for copy in copies:
            copy.start()

    def wait(copies):
        for copy in copies:
            copy.wait()

    for side in range(2):
        start(row_copies(side) + weight_copies(0, side))

    @pl.loop(0, steps)
    def _(step):
        slot = step % 2

        @pl.when(step == 0)
        def _():
            wait(row_copies(0))

        wait(weight_copies(step, 0))

        @pl.when(step + 1 < steps)
        def _():
            start(weight_copies(step + 1, 0) + weight_copies(step + 1, 1))

        own_value = own_rows[:, :half]
        gate = jnp.dot(own_value, weights[slot, 0], preferred_element_type=jnp.float32)
        up = jnp.dot(own_value, weights[slot, 1], preferred_element_type=jnp.float32)

        @pl.when(step == 0)
        def _():
            wait(row_copies(1))

        wait(weight_copies(step, 1))
        sib_value = sib_rows[:, :half]
        gate += jnp.dot(sib_value, weights[slot, 2], preferred_element_type=jnp.float32)
        up += jnp.dot(sib_value, weights[slot, 3], preferred_element_type=jnp.float32)
        value = (gate / (1.0 + jnp.exp(-gate)) * up).astype(jnp.bfloat16)
        act[:, pl.ds(pl.multiple_of(step * block, block), block)] = value
        act_copy(step).start()

    if with_meta:
        meta = own_rows[:, half:].astype(jnp.float32) + sib_rows[:, half:].astype(jnp.float32)
        me = spot_ref[1].astype(jnp.float32)
        lanes = lax.broadcasted_iota(jnp.int32, meta.shape, 1)
        for step, scale_ref in enumerate(scale_refs):
            base = step * 4 * META_PICKS
            value = jnp.zeros_like(meta)
            for part in range(1, 4):
                low = base + part * META_PICKS
                named = pltpu.roll(meta, part * META_PICKS, 1) == me
                inside = (lanes >= low) & (lanes < low + META_PICKS)
                value = value + jnp.where(named & inside, meta, 0.0)
            total = jnp.sum(value, axis=1, keepdims=True)
            scale_ref[...] = jnp.broadcast_to(total, scale_ref.shape)
    for step in range(steps):
        act_copy(step).wait()


def expert_up(spot, own_pieces, sib_pieces, expert_in, line_rows, with_meta):
    piece_counts = [piece.shape[0] // line_rows for piece in own_pieces]
    wide = own_pieces[0].shape[1]
    half = expert_in.shape[0] // 2
    hidden_units = expert_in.shape[1] // 2
    rows = sum(piece_counts) * line_rows
    block = 256
    out_specs = [pl.BlockSpec(memory_space=pl.ANY)]
    out_shape = [jax.ShapeDtypeStruct((rows, hidden_units), jnp.bfloat16)]
    if with_meta:
        out_specs += [pl.BlockSpec((rows, LANES), lambda i, c: (0, 0))] * STEPS
        out_shape += [jax.ShapeDtypeStruct((rows, LANES), jnp.float32)] * STEPS
    held = 2 * rows * (2 * wide + hidden_units) + 16 * half * block
    return pl.pallas_call(
        functools.partial(up_body, line_rows, piece_counts, with_meta, block),
        grid_spec=pltpu.PrefetchScalarGridSpec(
            num_scalar_prefetch=1,
            grid=(1,),
            in_specs=[pl.BlockSpec(memory_space=pl.ANY)] * (2 * len(own_pieces) + 1),
            out_specs=out_specs,
            scratch_shapes=[
                pltpu.VMEM((rows, wide), jnp.bfloat16),
                pltpu.VMEM((rows, wide), jnp.bfloat16),
                pltpu.VMEM((2, 4, half, block), jnp.bfloat16),
                pltpu.VMEM((rows, hidden_units), jnp.bfloat16),
                pltpu.SemaphoreType.DMA((2, sum(piece_counts))),
                pltpu.SemaphoreType.DMA((2, 4)),
                pltpu.SemaphoreType.DMA((hidden_units // block,)),
            ],
        ),
        out_shape=out_shape,
        compiler_params=pltpu.CompilerParams(
            dimension_semantics=("arbitrary",), vmem_limit_bytes=max(47 << 20, held + 24 * rows * block + (4 << 20))
        ),
        cost_estimate=pl.CostEstimate(
            flops=8 * rows * half * hidden_units,
            bytes_accessed=8 * half * hidden_units + 4 * rows * wide + 2 * rows * hidden_units,
            transcendentals=rows * hidden_units,
        ),
        name="expert_up",
    )(spot, *own_pieces, *sib_pieces, expert_in)


def down_body(line_rows, jobs, spot_ref, act_ref, down_ref, scale_ref, *outs):
    del spot_ref
    per_job = pl.num_programs(0) // len(jobs)

    def run(groups, outs):
        lines = [line for group in groups for line in group]
        at = lambda ref: jnp.concatenate(
            [ref[line * line_rows : (line + 1) * line_rows] for line in lines], axis=0
        )
        answer = jnp.dot(at(act_ref), down_ref[...], preferred_element_type=jnp.float32)
        scale = at(scale_ref)
        for column in range(0, answer.shape[1], LANES):
            value = answer[:, column : column + LANES].astype(jnp.bfloat16).astype(jnp.float32)
            value = (value * scale).astype(jnp.bfloat16)
            first = 0
            for group, out in zip(groups, outs):
                rows = len(group) * line_rows
                out[:, column : column + LANES] = value[first : first + rows]
                first += rows

    first = 0
    for index, (_, groups) in enumerate(jobs):
        mine = outs[first : first + len(groups)]
        first += len(groups)
        if len(jobs) == 1:
            run(groups, mine)
        else:
            pl.when(pl.program_id(0) // per_job == index)(functools.partial(run, groups, mine))


def expert_down(spot, act, expert_out, scale, line_rows, jobs):
    rows, hidden_units = act.shape
    half = expert_out.shape[1] // 2
    block = 896
    steps = half // block

    def weight_at(i, c):
        side = jobs[0][0]
        for index, job in enumerate(jobs[1:]):
            side = jnp.where(i // steps > index, job[0], side)
        return (0, (c[0] + side - 2 * c[0] * side) * steps + i % steps)

    def out_at(index):
        return lambda i, c: (0, jnp.minimum(jnp.maximum(i - index * steps, 0), steps - 1))

    out_specs, out_shape = [], []
    for index, (_, groups) in enumerate(jobs):
        for group in groups:
            out_specs.append(pl.BlockSpec((len(group) * line_rows, block), out_at(index)))
            out_shape.append(jax.ShapeDtypeStruct((len(group) * line_rows, half), jnp.bfloat16))
    return pl.pallas_call(
        functools.partial(down_body, line_rows, jobs),
        grid_spec=pltpu.PrefetchScalarGridSpec(
            num_scalar_prefetch=1,
            grid=(steps * len(jobs),),
            in_specs=[
                pl.BlockSpec((rows, hidden_units), lambda i, c: (0, 0)),
                pl.BlockSpec((hidden_units, block), weight_at),
                pl.BlockSpec((rows, LANES), lambda i, c: (0, 0)),
            ],
            out_specs=out_specs,
        ),
        out_shape=out_shape,
        compiler_params=pltpu.CompilerParams(
            dimension_semantics=("arbitrary",),
            vmem_limit_bytes=4 * (rows + block) * hidden_units + 24 * rows * block + (10 << 20),
        ),
        cost_estimate=pl.CostEstimate(flops=1 << 36, bytes_accessed=1 << 10, transcendentals=0),
        name="expert_down",
    )(spot, act, expert_out, scale)


def meta_body(route_ref, weight_ref, meta_ref):
    parts = []
    for step in range(STEPS):
        weight = weight_ref[step]
        top = weight.astype(jnp.bfloat16).astype(jnp.float32)
        middle = (weight - top).astype(jnp.bfloat16).astype(jnp.float32)
        parts += [route_ref[step].astype(jnp.float32), top, middle, weight - top - middle]
    value = jnp.concatenate(parts, axis=0).astype(jnp.bfloat16)
    shape = (value.shape[0], meta_ref.shape[1])
    rows = lax.broadcasted_iota(jnp.int32, shape, 0)
    lanes = lax.broadcasted_iota(jnp.int32, shape, 1)
    spots = (rows == lanes).astype(jnp.bfloat16)
    turned = lax.dot_general(
        value, spots, (((0,), (0,)), ((), ())), preferred_element_type=jnp.float32
    )
    meta_ref[...] = turned.astype(jnp.bfloat16)


def meta_columns(routes, weights):
    return pl.pallas_call(
        meta_body,
        out_shape=jax.ShapeDtypeStruct((routes.shape[2], LANES), jnp.bfloat16),
        name="meta_columns",
    )(routes, weights)


def pick_body(swapped_ref, cache_ref, first_ref, second_ref, info_ref, sems):
    row_count = swapped_ref.shape[0]
    for index in range(MOVE):
        info_ref[index] = 0

    def find(slot, count):
        @pl.when((swapped_ref[slot] == 1) & (count < MOVE))
        def _():
            info_ref[count] = slot

        return count + swapped_ref[slot]

    count = jnp.minimum(lax.fori_loop(0, row_count, find, jnp.int32(0)), MOVE)
    last = jnp.maximum(count - 1, 0)
    last_slot = info_ref[last]
    copies = []
    for index in range(MOVE):
        slot = jnp.where(index < count, info_ref[index], last_slot)
        info_ref[index] = slot
        info_ref[MOVE + index] = jnp.where(count > 0, jnp.minimum(index, last), -1)
        out_ref = first_ref if index < MOVE // 2 else second_ref
        copies.append(
            pltpu.make_async_copy(
                cache_ref.at[slot], out_ref.at[index % (MOVE // 2)], sems.at[index]
            )
        )
        copies[-1].start()
    for copy in copies:
        copy.wait()


def pick_caches(swapped, cache):
    part = jax.ShapeDtypeStruct((MOVE // 2,) + cache.shape[1:], cache.dtype)
    return pl.pallas_call(
        pick_body,
        grid_spec=pltpu.PrefetchScalarGridSpec(
            num_scalar_prefetch=1,
            grid=(1,),
            in_specs=[pl.BlockSpec(memory_space=pl.ANY)],
            out_specs=[
                pl.BlockSpec(part.shape, lambda i, _: (0, 0, 0)),
                pl.BlockSpec(part.shape, lambda i, _: (0, 0, 0)),
                pl.BlockSpec(memory_space=pltpu.SMEM),
            ],
            scratch_shapes=[pltpu.SemaphoreType.DMA((MOVE,))],
        ),
        out_shape=[part, part, jax.ShapeDtypeStruct((2 * MOVE,), jnp.int32)],
        name="pick_caches",
    )(swapped, cache)


def attend_one(query, cache, fresh, length):
    fresh = fresh.astype(jnp.float32)
    scores = jnp.dot(query, cache, preferred_element_type=jnp.float32) * SOFTMAX_SCALE
    own = jnp.sum(query.astype(jnp.float32) * fresh, axis=1, keepdims=True) * SOFTMAX_SCALE
    positions = lax.broadcasted_iota(jnp.int32, scores.shape, 1)
    scores = jnp.where(positions < length, scores, -jnp.inf)
    top = jnp.maximum(jnp.max(scores, axis=1, keepdims=True), own)
    weights = jnp.exp(scores - top)
    own_weight = jnp.exp(own - top)
    summed = jnp.sum(weights, axis=1, keepdims=True) + own_weight
    blended = lax.dot_general(
        weights.astype(jnp.bfloat16),
        cache[:LATENT],
        (((1,), (1,)), ((), ())),
        preferred_element_type=jnp.float32,
    )
    own_rounded = own_weight.astype(jnp.bfloat16).astype(jnp.float32)
    blended = blended + own_rounded * fresh[:, :LATENT]
    return (blended / summed).astype(jnp.bfloat16)


def attend_body(group, spot_ref, length_ref, query_ref, cache_ref, fresh_ref, out_ref):
    count = group * pl.num_programs(0)
    first = spot_ref[1] * count + pl.program_id(0) * group
    for slot in range(group):
        out_ref[slot] = attend_one(
            query_ref[slot], cache_ref[slot], fresh_ref[slot], length_ref[first + slot]
        )


def attend(spot, lengths, queries, cache, fresh):
    count, heads, full = queries.shape
    positions = cache.shape[2]
    group = 4
    return pl.pallas_call(
        functools.partial(attend_body, group),
        grid_spec=pltpu.PrefetchScalarGridSpec(
            num_scalar_prefetch=2,
            grid=(count // group,),
            in_specs=[
                pl.BlockSpec((group, heads, full), lambda i, *_: (i, 0, 0)),
                pl.BlockSpec((group, full, positions), lambda i, *_: (i, 0, 0)),
                pl.BlockSpec((group, 1, full), lambda i, *_: (i, 0, 0)),
            ],
            out_specs=pl.BlockSpec((group, heads, LATENT), lambda i, *_: (i, 0, 0)),
        ),
        out_shape=jax.ShapeDtypeStruct((count, heads, LATENT), jnp.bfloat16),
        compiler_params=pltpu.CompilerParams(
            dimension_semantics=("arbitrary",), vmem_limit_bytes=12 << 20
        ),
        cost_estimate=pl.CostEstimate(
            flops=4 * count * heads * full * positions,
            bytes_accessed=2 * count * (heads * (full + LATENT) + full * positions),
            transcendentals=count * heads * positions,
        ),
        name="attend",
    )(spot, lengths, queries, cache, fresh)


def attend_moved_body(
    row_count, spot_ref, length_ref, info_ref, query_ref, cache_ref, came_a_ref, came_b_ref, fresh_ref, old_ref, out_ref
):
    del old_ref
    index = pl.program_id(0)
    place = info_ref[MOVE + index]
    total = length_ref.shape[0]
    row = spot_ref[1] * row_count + info_ref[index]
    row = jnp.where(place >= 0, lax.rem(row + total // 2, total), row)
    came = jnp.where(place < MOVE // 2, came_a_ref[...], came_b_ref[...])[0]
    cache = jnp.where(place >= 0, came, cache_ref[0])
    out_ref[0] = attend_one(query_ref[0], cache, fresh_ref[0], length_ref[row])


def attend_moved(spot, lengths, info, queries, cache, came_a, came_b, fresh, context):
    row_count, heads, full = queries.shape
    positions = cache.shape[2]
    part = MOVE // 2
    at_slot = lambda i, spot, lengths, info: (info[i], 0, 0)
    clip = lambda value: jnp.minimum(jnp.maximum(value, 0), part - 1)
    one = (1, full, positions)
    return pl.pallas_call(
        functools.partial(attend_moved_body, row_count),
        grid_spec=pltpu.PrefetchScalarGridSpec(
            num_scalar_prefetch=3,
            grid=(MOVE,),
            in_specs=[
                pl.BlockSpec((1, heads, full), at_slot),
                pl.BlockSpec(one, at_slot),
                pl.BlockSpec(one, lambda i, spot, lengths, info: (clip(info[MOVE + i]), 0, 0)),
                pl.BlockSpec(
                    one, lambda i, spot, lengths, info: (clip(info[MOVE + i] - part), 0, 0)
                ),
                pl.BlockSpec((1, 1, full), at_slot),
                pl.BlockSpec(memory_space=pl.ANY),
            ],
            out_specs=pl.BlockSpec((1, heads, LATENT), at_slot),
        ),
        out_shape=jax.ShapeDtypeStruct(context.shape, context.dtype),
        input_output_aliases={8: 0},
        compiler_params=pltpu.CompilerParams(
            dimension_semantics=("arbitrary",), vmem_limit_bytes=48 << 20
        ),
        cost_estimate=pl.CostEstimate(flops=1 << 36, bytes_accessed=1 << 10, transcendentals=0),
        name="attend_moved",
    )(spot, lengths, info, queries, cache, came_a, came_b, fresh, context)


def per_device(
    hidden,
    routes,
    route_weights,
    expert_in,
    expert_out,
    queries,
    fresh_key,
    latent_cache,
    lengths,
    swapped,
):
    dp_count, ep_count = lax.axis_size("dp"), lax.axis_size("ep")
    device_count = dp_count * ep_count
    token_count, width = hidden.shape[1], hidden.shape[2]
    half = width // 2
    me = lax.axis_index(AXES)
    core = me % 2
    dp_bits, ep_bits = dp_count.bit_length() - 1, ep_count.bit_length() - 1
    x_masks = [ep_count << bit for bit in range(dp_bits - Z_BITS)]
    z_unit = ep_count << (dp_bits - Z_BITS)
    y_masks = [1 << bit for bit in range(1, ep_bits)]
    z_steps = sorted(range(1, 1 << Z_BITS), key=lambda step: step < 1 << (Z_BITS - 1))
    z_masks = [z_unit * step for step in [0] + z_steps]
    orders = (x_masks + y_masks, y_masks + x_masks)
    level_masks = list(zip(*orders))
    line_count = 1 << len(level_masks)
    sibling = (1, 1)
    spot = jnp.stack([core, me]).astype(jnp.int32)

    meta = meta_columns(jnp.swapaxes(routes, 1, 2), jnp.swapaxes(route_weights, 1, 2))

    own_half = lax.dynamic_slice_in_dim(hidden, core * half, half, axis=2)
    came_half = lax.dynamic_slice_in_dim(exchange(hidden, sibling), core * half, half, axis=2)
    by_core = lambda mine, theirs, axis: jnp.where(
        core == 0,
        jnp.concatenate([mine, theirs], axis=axis),
        jnp.concatenate([theirs, mine], axis=axis),
    )
    pair = by_core(own_half, came_half, 1)
    pair_meta = by_core(meta, jnp.zeros_like(meta), 0)
    line_rows = len(z_masks) * 2 * token_count

    window = lambda *values: lax.optimization_barrier(values)
    far = device_count // 2
    bottom, top_masks = level_masks[:-1], level_masks[-1]

    swap = lambda value: exchange(value, sibling)

    def send_line(block):
        return [exchange(block, (mask, mask)) for mask in z_masks[1:]]

    def spread(line):
        for masks in bottom:
            line = jnp.concatenate([line, exchange(line, masks)], axis=0)
        return line

    add = lambda terms: functools.reduce(
        lambda total, term: total + term, [term.astype(jnp.float32) for term in terms]
    )
    rounded_sum = lambda terms: add(terms).astype(jnp.bfloat16)
    up = lambda own, sib, with_meta: expert_up(
        spot, own, sib, expert_in[0], line_rows, with_meta
    )
    down = lambda act, scale, *jobs: expert_down(
        spot, act, expert_out[0], scale, line_rows, jobs
    )
    half_bits = len(level_masks) // 2
    my_lines = list(range(line_count))
    their_lines = [swap_halves(line, half_bits) for line in my_lines]
    split = line_count // 2
    halves_of = lambda terms: (
        [term[: term.shape[0] // 2] for term in terms],
        [term[term.shape[0] // 2 :] for term in terms],
    )

    def fold(terms):
        for masks in reversed(bottom):
            terms, high = halves_of(terms)
            terms = terms + [exchange(rounded_sum(high), masks)]
        return terms

    def finish_sends(terms):
        block = 2 * token_count
        at = lambda place: [term[place * block : (place + 1) * block] for term in terms]
        return at(0), [rounded_sum(at(place)) for place in range(1, len(z_masks))]

    def finish_line(sends):
        return [exchange(value, (mask, mask)) for value, mask in zip(sends, z_masks[1:])]

    def finish(terms):
        total = rounded_sum(terms).reshape(2, token_count, half)
        kept = lax.dynamic_index_in_dim(total, core, 0, keepdims=False)
        sent = lax.dynamic_index_in_dim(total, 1 - core, 0, keepdims=False)
        return by_core(kept, exchange(sent, sibling), 1)

    block0 = jnp.concatenate([pair[0], pair_meta], axis=1)
    block0, swapped = window(block0, swapped)

    fresh = fresh_key[:, None, :]
    stored = jnp.swapaxes(latent_cache, 1, 2)

    came0 = send_line(block0)
    *leaving, info = pick_caches(swapped, stored)
    *came0, leave_a, leave_b, info = window(*came0, *leaving, info)

    low0 = spread(jnp.concatenate([block0] + came0, axis=0))
    low0, block1, early_queries = window(low0, pair[1], queries)

    high0 = exchange(low0, top_masks)
    sib_low0 = exchange(low0, sibling)
    came1 = send_line(block1)
    context = attend(spot, lengths, early_queries, stored, fresh)
    high0, sib_low0, context, *came1 = window(high0, sib_low0, context, *came1)

    line1 = jnp.concatenate([block1] + came1, axis=0)
    low0, high0, sib_low0, line1, leave_a = window(low0, high0, sib_low0, line1, leave_a)
    sib_high0 = exchange(high0, sibling)

    low1 = [line1]
    for masks in bottom:
        low1 = low1 + [exchange(line, masks) for line in low1]
    first1 = exchange(line1, top_masks)
    cache_a = exchange(leave_a, (far, far))
    act0, scale0, scale1 = up([low0, high0], [sib_low0, sib_high0], True)
    first1, cache_a, act0, scale0, scale1, *low1 = window(
        first1, cache_a, act0, scale0, scale1, *low1
    )

    rest1 = [exchange(line, top_masks) for line in low1[1:]]
    sib_low1 = [swap(line) for line in low1]
    sib_first1 = swap(first1)
    they_low0, they_high0 = down(act0, scale0, (1, (their_lines[:split], their_lines[split:])))
    they_low0, they_high0 = swap(they_low0), swap(they_high0)
    my_low0, my_high0 = down(act0, scale0, (0, (my_lines[:split], my_lines[split:])))
    sib_first1, they_low0, they_high0, my_low0, my_high0, *flat = window(
        sib_first1, they_low0, they_high0, my_low0, my_high0, *sib_low1, *rest1
    )
    sib_low1, rest1 = flat[:split], flat[split:]

    send0 = rounded_sum([my_high0, they_high0])
    send0, leave_b, *rest1 = window(send0, leave_b, *rest1)
    sib_rest1 = [swap(line) for line in rest1]

    came = exchange(send0, top_masks)
    cache_b = exchange(leave_b, (far, far))
    (act1,) = up(low1 + [first1] + rest1, sib_low1 + [sib_first1] + sib_rest1, False)
    came, act1, cache_b = window(came, act1, cache_b)

    they_high1, my_high1 = down(
        act1, scale1, (1, (their_lines[split:],)), (0, (my_lines[split:],))
    )
    terms0 = [my_low0, they_low0, came]
    for masks in reversed(bottom):
        terms0, high = halves_of(terms0)
        high, my_high1 = window(rounded_sum(high), my_high1)
        terms0 = terms0 + [exchange(high, masks)]

    they_high1 = exchange(they_high1, sibling)
    send1 = rounded_sum([my_high1, they_high1])
    send1, act1 = window(send1, act1)
    came = exchange(send1, top_masks)
    they_low1, my_low1 = down(
        act1, scale1, (1, (their_lines[:split],)), (0, (my_lines[:split],))
    )
    they_low1 = exchange(they_low1, sibling)
    kept0, sends0 = finish_sends(terms0)
    last0 = finish_line(sends0)
    came, my_low1 = window(came, my_low1)

    terms1 = [my_low1, they_low1, came]
    for masks in reversed(bottom):
        terms1, high = halves_of(terms1)
        high, queries = window(rounded_sum(high), queries)
        terms1 = terms1 + [exchange(high, masks)]
    context = attend_moved(
        spot, lengths, info, queries, stored, cache_a, cache_b, fresh, context
    )
    terms1[-1], context, *last0 = window(terms1[-1], context, *last0)
    kept1, sends1 = finish_sends(terms1)
    last1 = finish_line(sends1)
    mixed0 = finish(kept0 + last0)
    mixed1 = finish(kept1 + last1)
    return (jnp.stack([mixed0, mixed1]), context)


def solution(mesh):
    in_specs = (
        P(None, ("dp", "ep"), None),
        P(None, ("dp", "ep"), None),
        P(None, ("dp", "ep"), None),
        P(("dp", "ep"), None, None),
        P(("dp", "ep"), None, None),
        P(("dp", "ep"), None, None),
        P(("dp", "ep"), None),
        P(("dp", "ep"), None, None),
        P(),
        P(("dp", "ep")),
    )
    out_specs = (P(None, ("dp", "ep"), None), P(("dp", "ep"), None, None))
    return jax.shard_map(
        per_device, mesh=mesh, in_specs=in_specs, out_specs=out_specs, check_vma=False
    )
```
